256 devices in a mesh: band: 8 (over y, core), sector: 32 (over x, z).
Axes of the slice: x: 4, y: 4, z: 8, core: 2. Of those that a mesh axis runs over, the one named last changes fastest.
Arguments:
- blocks: float32 [8, 32, 12, 24, 1024], P('band', 'sector'), may hold values from -64 to 64, as said below
- connectivity: int32 [8, 32, 8, 1024], P('band', 'sector'), may hold values from 0 to 2047, as said below
- send_lists: int32 [8, 32, 4, 256], P('band', 'sector'), may hold values from 0 to 1023, as said below
- nodal_loads: float32 [8, 32, 3, 1024], P('band', 'sector'), may hold values from -48 to 48
- step_scale: float32 [1], replicated, may hold values from 0.5 to 0.9
Outputs:
- velocities: float32 [8, 32, 3, 1024], P('band', 'sector')
- multipliers: float32 [8, 32, 12, 1024], P('band', 'sector')
The draws below stay inside these ranges and needn't reach their ends.
Inputs may be any that keep to these rules, and one draw needn't show every extreme that they name: `connectivity`: indices into the device's extended list of 2048 nodes. Row 0 is a permutation of the 1024 owned nodes; rows 1 and 2 together are a permutation of the whole extended list. `send_lists`: the four lists of a device together are a permutation of its 1024 owned nodes. `blocks`: every entry has magnitude 0.2 or more.
All inputs are finite; a program needn't handle non-finite values.
Results may differ from the reference program's by a relative error of at most 0.0003.
Values sent between devices are 32-bit elements; how exact they have to be, the bound alone decides.
No kernel may reach another device: no remote copies, remote signals or barrier semaphores. Data moves between devices by JAX's collectives and lax.ppermute only.
A program may use at most 128 MiB of HBM per device.

```python
import math
import jax
import jax.numpy as jnp
from jax import lax

EL = 1024
HALO = 256
STRAINS = 12
CORNERS = 8
RUIZ_PASSES = 3
POWER_STEPS = 3
PRIMAL_DUAL_STEPS = 2
BANDS = 8
SECTORS = 32


def signed_factor(key, shape):
    sign_key, size_key = jax.random.split(key)
    signs = jnp.where(jax.random.bernoulli(sign_key, 0.5, shape), 1.0, -1.0)
    return signs * jax.random.uniform(size_key, shape, jnp.float32, 0.5, 1.5)


def draw_blocks(key, part):
    key = jax.random.fold_in(key, 5)
    sign_key = jax.random.fold_in(key, 0)
    size_key = jax.random.fold_in(key, 1)
    left_key = jax.random.fold_in(key, 3)
    right_key = jax.random.fold_in(key, 4)
    seed_key = jax.random.fold_in(key, 5)
    device_key = jax.random.fold_in(key, 6)
    shape = (BANDS, SECTORS, STRAINS, 3 * CORNERS, EL)
    signs = jnp.where(jax.random.bernoulli(sign_key, 0.5, shape), 1.0, -1.0)
    magnitude = jnp.exp(jax.random.uniform(size_key, shape, jnp.float32, math.log(0.2), math.log(5.0)))
    left = signed_factor(left_key, (BANDS, SECTORS, STRAINS, 1, EL))
    right = signed_factor(right_key, (BANDS, SECTORS, 1, 3 * CORNERS, EL))
    strength = jax.random.uniform(seed_key, (), jnp.float32, 0.2, 1.6)
    device_factor = jax.random.uniform(device_key, (BANDS, SECTORS, 1, 1, 1), jnp.float32, 0.3, 1.7)
    core = signs * (magnitude - 0.2) + strength * device_factor * left * right
    entry = jnp.where(core >= 0.0, core + 0.2, core - 0.2)
    return entry.astype(jnp.float32)


def draw_connectivity(key, part):
    key = jax.random.fold_in(key, 11)
    device_keys = jax.random.split(key, BANDS * SECTORS)

    def one_device(device_key):
        own_key, whole_key, rest_key = jax.random.split(device_key, 3)
        first_row = jax.random.permutation(own_key, EL).astype(jnp.int32)[None]
        middle_rows = jax.random.permutation(whole_key, 2 * EL).astype(jnp.int32).reshape(2, EL)
        other_rows = jax.random.randint(rest_key, (CORNERS - 3, EL), 0, 2 * EL).astype(jnp.int32)
        return jnp.concatenate([first_row, middle_rows, other_rows], axis=0)
    return jax.vmap(one_device)(device_keys).reshape(BANDS, SECTORS, CORNERS, EL)


def draw_send_lists(key, part):
    key = jax.random.fold_in(key, 17)
    device_keys = jax.random.split(key, BANDS * SECTORS)

    def one_device(device_key):
        return jax.random.permutation(device_key, EL).astype(jnp.int32).reshape(4, HALO)
    return jax.vmap(one_device)(device_keys).reshape(BANDS, SECTORS, 4, HALO)


def level_of(rng, dims, shards, least, high):
    loudness, own = 1.0, jax.random.fold_in(rng, 6)
    for axis_at, blocks in shards:
        heights = jnp.exp(jax.random.uniform(jax.random.fold_in(own, axis_at), (blocks,), jnp.float32, least / len(shards), high / len(shards)))
        loudness = loudness * jnp.repeat(heights, dims[axis_at] // blocks).reshape([-1 if axis == axis_at else 1 for axis in range(len(dims))])
    return loudness


def scatter_about(key, extent, scale, limit, shards=(), held_as=jnp.bfloat16):
    drawn = jax.random.normal(key, extent, jnp.float32) * scale
    if len(shards) > 0:
        drawn = level_of(key, extent, shards, -0.22, 0.18) * drawn
    return jnp.clip(drawn, min=-limit, max=limit).astype(held_as)


def setup_inputs(seed: int = 0) -> dict:
    key_list = jax.random.split(jax.random.key(seed), 6)
    return {
        "blocks": draw_blocks(jax.random.fold_in(key_list[5], 71), 0),
        "connectivity": draw_connectivity(jax.random.fold_in(key_list[5], 71), 0),
        "send_lists": draw_send_lists(jax.random.fold_in(key_list[5], 71), 0),
        "nodal_loads": scatter_about(key_list[3], (BANDS, SECTORS, 3, EL), 8.0, 48.0, ((0, 8), (1, 32)), jnp.float32),
        "step_scale": jnp.clip(jax.random.uniform(key_list[4], (1,), jnp.float32, 0.5, 0.9), 0.5, 0.9),
    }


epsilon = 1e-06

def per_device(function):

    def run_all(*arrays):
        return lax.map(lambda band_group: jax.vmap(function)(*band_group), arrays)
    return run_all

def trade(packets):
    zero_rows = jnp.zeros_like(packets[:1, :, :, 0])
    from_left = jnp.roll(packets[:, :, :, 1], 1, axis=1)
    from_right = jnp.roll(packets[:, :, :, 0], -1, axis=1)
    from_below = jnp.concatenate([zero_rows, packets[:-1, :, :, 3]], axis=0)
    from_above = jnp.concatenate([packets[1:, :, :, 2], zero_rows], axis=0)
    return jnp.stack([from_left, from_right, from_below, from_above], axis=3)

def pick_rows(own_values, send_rows):
    return jnp.take(own_values, send_rows, axis=1)

def spread(own_values, send_lists):
    arrived = trade(per_device(pick_rows)(own_values, send_lists))
    return jnp.concatenate([own_values, arrived.reshape(own_values.shape[:3] + (-1,))], axis=3)

def merge_sum(own_values, send_rows, arrived):
    return own_values.at[:, send_rows].add(arrived)

def merge_max(own_values, send_rows, arrived):
    return own_values.at[:, send_rows].max(arrived)

def collect(extended, send_lists, merge_rule):
    own_width = extended.shape[3] - 4 * send_lists.shape[3]
    own_values = extended[..., :own_width]
    slot_rows = extended[..., own_width:].reshape(extended.shape[:3] + (4, -1))
    return per_device(merge_rule)(own_values, send_lists, trade(slot_rows))

def dof_values(extended, corner_ids):
    return jnp.take(extended, corner_ids, axis=1).reshape(-1, corner_ids.shape[1])

def local_maxima(blocks, row_scale, ext_scale, corner_ids):
    magnitudes = jnp.abs(blocks) * row_scale[:, None, :] * dof_values(ext_scale, corner_ids)[None]
    column_max = lax.optimization_barrier(jnp.max(magnitudes, axis=0)).reshape(3, corner_ids.shape[0], corner_ids.shape[1])
    placed = jnp.zeros((3, ext_scale.shape[1]), jnp.float32).at[:, corner_ids].max(column_max)
    return (lax.optimization_barrier(jnp.max(magnitudes, axis=1)), placed)

def scale_blocks(blocks, row_scale, ext_scale, corner_ids):
    return blocks * row_scale[:, None, :] * dof_values(ext_scale, corner_ids)[None]

def apply_blocks(scaled, extended, corner_ids):
    return lax.optimization_barrier(jnp.sum(scaled * dof_values(extended, corner_ids)[None], axis=1))

def apply_transpose(scaled, dual_vars, corner_ids):
    dof_terms = lax.optimization_barrier(jnp.sum(scaled * dual_vars[:, None, :], axis=0)).reshape(3, corner_ids.shape[0], corner_ids.shape[1])
    return jnp.zeros((3, EL + 4 * HALO), jnp.float32).at[:, corner_ids].add(dof_terms)

def project_cones(values):
    cones = values.reshape(values.shape[:-2] + (4, 3, values.shape[-1]))
    cone_top = cones[..., 0, :]
    cone_side = cones[..., 1:, :]
    side_norm = jnp.sqrt(lax.optimization_barrier(jnp.sum(cone_side * cone_side, axis=-2)))
    inside = side_norm <= cone_top
    middle = side_norm > jnp.abs(cone_top)
    safe_norm = jnp.where(middle, side_norm, 1.0)
    factor = 0.5 * (1.0 + cone_top / safe_norm)
    new_top = jnp.where(inside, cone_top, jnp.where(middle, factor * side_norm, 0.0))
    new_side = jnp.where(inside[..., None, :], cone_side, jnp.where(middle[..., None, :], factor[..., None, :] * cone_side, 0.0))
    return jnp.concatenate([new_top[..., None, :], new_side], axis=-2).reshape(values.shape)

def reference(blocks, connectivity, send_lists, nodal_loads, step_scale):
    row_scale = jnp.ones(blocks.shape[:3] + (blocks.shape[4],), jnp.float32)
    col_scale = jnp.ones_like(nodal_loads)
    ext_scale = spread(jnp.ones_like(nodal_loads), send_lists)
    for sweep in range(RUIZ_PASSES):
        row_max, column_max = per_device(local_maxima)(blocks, row_scale, ext_scale, connectivity)
        own_max = collect(column_max, send_lists, merge_max)
        row_scale = row_scale / jnp.sqrt(row_max)
        col_scale = col_scale / jnp.sqrt(own_max)
        ext_scale = spread(col_scale, send_lists)
    scaled = per_device(scale_blocks)(blocks, row_scale, ext_scale, connectivity)

    def forward(own_values):
        return per_device(apply_blocks)(scaled, spread(own_values, send_lists), connectivity)

    def backward(dual_vars):
        return collect(per_device(apply_transpose)(scaled, dual_vars, connectivity), send_lists, merge_sum)
    target = col_scale * nodal_loads
    iterate = target
    previous = target
    for sweep in range(POWER_STEPS):
        previous = iterate
        iterate = backward(forward(iterate))
    largest = jnp.sqrt(jnp.sum(iterate * iterate) + epsilon) / jnp.sqrt(jnp.sum(previous * previous) + epsilon)
    step_size = step_scale[0] / jnp.sqrt(largest)
    primal = jnp.zeros_like(target)
    dual_vars = jnp.zeros_like(row_scale)
    for sweep in range(PRIMAL_DUAL_STEPS):
        primal_new = primal - step_size * (target - backward(dual_vars))
        dual_vars = project_cones(dual_vars - step_size * forward(2.0 * primal_new - primal))
        primal = primal_new
    return (col_scale * primal, row_scale * dual_vars)
```

```python
import functools

import jax
import jax.numpy as jnp
from jax import lax
from jax.experimental import pallas as pl
from jax.experimental.pallas import tpu as pltpu
from jax.sharding import PartitionSpec as P

LANES = 128
CHUNKS = 8
STRAINS = 12
NODE_ROWS = 16
ITEM_ROWS = 64
SIDES = 4
AXES = ("band", "sector")
epsilon = 1e-06
F32 = jnp.float32
I32 = jnp.int32


def tile_iota(axis):
    return lax.broadcasted_iota(I32, (8, LANES), axis)


def pick(rows, index, axis):
    dims = lax.GatherDimensionNumbers(
        offset_dims=(),
        collapsed_slice_dims=(axis,),
        start_index_map=(axis,),
        operand_batching_dims=(1 - axis,),
        start_indices_batching_dims=(1 - axis,),
    )
    return lax.gather(
        rows,
        index[..., None],
        dims,
        slice_sizes=(1, 1),
        mode=lax.GatherScatterMode.PROMISE_IN_BOUNDS,
    )


def table_picks(row_getters, count, flat):
    lanes = flat & (LANES - 1)
    levels = count.bit_length() - 1
    bits = [(flat & (LANES << level)) != 0 for level in range(levels)]

    def descend(row_at, level, base):
        if level < 0:
            return pick(jnp.broadcast_to(row_at(base), (8, LANES)), lanes, 1)
        low = descend(row_at, level - 1, base)
        high = descend(row_at, level - 1, base + (1 << level))
        return jnp.where(bits[level], high, low)

    return [descend(row_at, levels - 1, 0) for row_at in row_getters]


def rows_of(ref, offset):
    return lambda row: ref[offset + row : offset + row + 1, :]


def chunk_at(chunk):
    return pl.ds(pl.multiple_of(chunk * LANES, LANES), LANES)


def eight_at(chunk, offset=0):
    return pl.ds(pl.multiple_of(offset + chunk * 8, 8), 8)


def group_shift(values, distance):
    if distance >= 8:
        return pltpu.roll(values, distance // 8, 1)
    turned = pltpu.roll(values, distance, 0)
    return jnp.where(tile_iota(0) < distance, pltpu.roll(turned, 1, 1), turned)


SCAN_STEPS = tuple(1 << step for step in range(10))


def sort_items(keys):
    sub, lane = tile_iota(0), tile_iota(1)
    size = 2
    while size <= 8192:
        half = size // 2
        while half >= 1:
            new = list(keys)

            def rising(register):
                if size < 8:
                    return (register & size) == 0
                if size < 64:
                    return (sub & (size // 8)) == 0
                if size < 8192:
                    return (lane & (size // 64)) == 0
                return True

            for register in range(8):
                up = rising(register)
                if half < 8:
                    other = register ^ half
                    if other < register:
                        continue
                    low = jnp.minimum(keys[register], keys[other])
                    high = jnp.maximum(keys[register], keys[other])
                    if isinstance(up, bool):
                        new[register], new[other] = (low, high) if up else (high, low)
                    else:
                        new[register] = jnp.where(up, low, high)
                        new[other] = jnp.where(up, high, low)
                    continue
                if half < 64:
                    step = half // 8
                    partner = pick(keys[register], sub ^ step, 0)
                    first = (sub & step) == 0
                else:
                    step = half // 64
                    partner = pick(keys[register], lane ^ step, 1)
                    first = (lane & step) == 0
                low = jnp.minimum(keys[register], partner)
                high = jnp.maximum(keys[register], partner)
                if isinstance(up, bool):
                    keep_low = first if up else jnp.logical_not(first)
                else:
                    keep_low = first == up
                new[register] = jnp.where(keep_low, low, high)
            keys = new
            half //= 2
        size *= 2
    return keys


def make_plan(conn_ref, send_ref, conn_out, key_out, scan_out, end_out, inverse_out, send_scratch):
    for half in range(8):
        start = (half % 2) * LANES
        send_scratch[half : half + 1, :] = send_ref[0, 0, half // 2 : half // 2 + 1, start : start + LANES]
    send_line = jnp.concatenate([send_scratch[row : row + 1, :] for row in range(8)], axis=1)
    place = lax.broadcasted_iota(I32, (8, 8 * LANES), 1)
    in_row = (send_line >> 7) == lax.broadcasted_iota(I32, (8, 8 * LANES), 0)
    left = jnp.concatenate(
        [
            jnp.where(in_row, (place >> 5).astype(F32), 0.0),
            jnp.where(in_row, (place & 31).astype(F32), 0.0),
        ],
        axis=0,
    ).astype(jnp.bfloat16)
    in_lane = (send_line & (LANES - 1)) == lax.broadcasted_iota(I32, (LANES, 8 * LANES), 0)
    right = jnp.where(in_lane, 1.0, 0.0).astype(jnp.bfloat16)
    found = lax.dot_general(left, right, (((1,), (1,)), ((), ())), preferred_element_type=F32)
    inverse_out[...] = (found[0:8] * 32.0 + found[8:16]).astype(I32)
    sub, lane = tile_iota(0), tile_iota(1)
    keys = []
    for chunk in range(CHUNKS):
        ids = conn_ref[0, 0, :, chunk * LANES : (chunk + 1) * LANES]
        (label,) = table_picks([rows_of(inverse_out, 0)], 8, ids & 1023)
        ids = jnp.where(ids < 1024, label, ids)
        conn_out[8 * chunk : 8 * chunk + 8, :] = ids
        keys.append(ids * 8192 + (chunk * 1024 + sub * LANES + lane))
    keys = sort_items(keys)
    for register in range(8):
        key_out[8 * register : 8 * register + 8, :] = keys[register]
    first, last = keys[0] >> 13, keys[7] >> 13
    group = lane * 8 + sub
    scan = jnp.zeros((8, LANES), I32)
    for step, distance in enumerate(SCAN_STEPS):
        same = (group >= distance) & (group_shift(last, distance) == last)
        scan = jnp.where(same, scan | (1 << step), scan)
    same = (group >= 1) & (group_shift(last, 1) == first)
    scan_out[...] = jnp.where(same, scan | (1 << len(SCAN_STEPS)), scan)
    lane_last = jnp.broadcast_to(key_out[63:64, :] >> 13, (8, LANES))
    for half in range(2):
        node = (half * 8 + sub) * LANES + lane
        column = jnp.zeros((8, LANES), I32)
        for step in (64, 32, 16, 8, 4, 2, 1):
            seen = pick(lane_last, column + (step - 1), 1)
            column = jnp.where(seen <= node, column + step, column)
        count = column * 64
        for row in range(ITEM_ROWS):
            seen = pick(jnp.broadcast_to(key_out[row : row + 1, :], (8, LANES)), column, 1)
            count = count + jnp.where((seen >> 13) <= node, 1, 0)
        place = count - 1
        row = (place & 7) * 8 + ((place >> 3) & 7)
        end_out[8 * half : 8 * half + 8, :] = row * LANES + (place >> 6)


def scatter_items(term_ref, channels, plan, sorted_ref, out_ref, merge):
    key_ref, scan_ref, end_ref = plan

    def bring(register, _):
        item = key_ref[eight_at(register), :] & 8191
        tables = [rows_of(term_ref, ITEM_ROWS * channel) for channel in range(channels)]
        for channel, values in enumerate(table_picks(tables, ITEM_ROWS, item)):
            sorted_ref[eight_at(register, ITEM_ROWS * channel), :] = values
        return 0

    lax.fori_loop(0, 8, bring, 0)
    nodes = [key_ref[8 * register : 8 * register + 8, :] >> 13 for register in range(8)]
    scan = scan_ref[...]
    follows = [(scan & (1 << step)) != 0 for step in range(len(SCAN_STEPS) + 1)]
    for channel in range(channels):
        base = ITEM_ROWS * channel
        runs = [sorted_ref[base : base + 8, :]]
        for register in range(1, 8):
            same = nodes[register] == nodes[register - 1]
            here = sorted_ref[base + 8 * register : base + 8 * register + 8, :]
            runs.append(merge(here, jnp.where(same, runs[-1], 0.0)))
        total = runs[7]
        for step, distance in enumerate(SCAN_STEPS):
            total = merge(total, jnp.where(follows[step], group_shift(total, distance), 0.0))
        carry = jnp.where(follows[-1], group_shift(total, 1), 0.0)
        for register in range(8):
            open_run = nodes[register] == nodes[0]
            sorted_ref[base + 8 * register : base + 8 * register + 8, :] = merge(
                runs[register], jnp.where(open_run, carry, 0.0)
            )

    def deliver(half, _):
        index = end_ref[eight_at(half), :]
        tables = [rows_of(sorted_ref, ITEM_ROWS * channel) for channel in range(channels)]
        for channel, values in enumerate(table_picks(tables, ITEM_ROWS, index)):
            out_ref[eight_at(half, NODE_ROWS * channel), :] = values
        return 0

    lax.fori_loop(0, 2, deliver, 0)


def node_picks(table_ref, channels, conn_ref, chunk):
    tables = [rows_of(table_ref, NODE_ROWS * channel) for channel in range(channels)]
    return table_picks(tables, NODE_ROWS, conn_ref[eight_at(chunk), :])


def measure_blocks(blocks_ref, row_ref, scale_ref, conn_ref, term_ref, max_ref):
    def one(chunk, _):
        scales = node_picks(scale_ref, 3, conn_ref, chunk)
        best = [jnp.zeros((8, LANES), F32)] * 3
        at = chunk_at(chunk)
        for r in range(STRAINS):
            sized = [
                jnp.abs(blocks_ref[0, 0, r, 8 * c : 8 * c + 8, at]) * scales[c] for c in range(3)
            ]
            whole = jnp.maximum(jnp.maximum(sized[0], sized[1]), sized[2])
            max_ref[r : r + 1, at] = jnp.max(whole, axis=0, keepdims=True)
            row = row_ref[r : r + 1, at]
            best = [jnp.maximum(best[c], sized[c] * row) for c in range(3)]
        for c in range(3):
            term_ref[eight_at(chunk, ITEM_ROWS * c), :] = best[c]
        return 0

    lax.fori_loop(0, CHUNKS, one, 0)


def apply_blocks(blocks_ref, table_ref, sets, conn_ref, strain_ref):
    def one(chunk, _):
        values = node_picks(table_ref, 3 * sets, conn_ref, chunk)
        at = chunk_at(chunk)
        for r in range(STRAINS):
            parts = [blocks_ref[0, 0, r, 8 * c : 8 * c + 8, at] for c in range(3)]
            for k in range(sets):
                mine = values[3 * k : 3 * k + 3]
                total = parts[0] * mine[0] + parts[1] * mine[1] + parts[2] * mine[2]
                strain_ref[STRAINS * k + r : STRAINS * k + r + 1, at] = jnp.sum(
                    total, axis=0, keepdims=True
                )
        return 0

    lax.fori_loop(0, CHUNKS, one, 0)


def apply_transpose(blocks_ref, strain_ref, sets, term_ref):
    def one(chunk, _):
        at = chunk_at(chunk)
        totals = [jnp.zeros((8, LANES), F32)] * (3 * sets)
        for r in range(STRAINS):
            parts = [blocks_ref[0, 0, r, 8 * c : 8 * c + 8, at] for c in range(3)]
            for k in range(sets):
                strain = strain_ref[STRAINS * k + r : STRAINS * k + r + 1, at]
                for c in range(3):
                    totals[3 * k + c] = totals[3 * k + c] + parts[c] * strain
        for channel in range(3 * sets):
            term_ref[eight_at(chunk, ITEM_ROWS * channel), :] = totals[channel]
        return 0

    lax.fori_loop(0, CHUNKS, one, 0)


def pack(part_ref, channels, packet_refs):
    for side in range(SIDES):
        for channel in range(channels):
            base = NODE_ROWS * channel + 2 * side
            packet_refs[side][4 * channel : 4 * channel + 2, :] = part_ref[base : base + 2, :]
            packet_refs[side][4 * channel + 2 : 4 * channel + 4, :] = part_ref[base + 8 : base + 10, :]


def live_sides():
    band = lax.axis_index("band")
    return [None, None, band > 0, band < lax.axis_size("band") - 1]


def unpack(part_ref, channels, arrived_refs, merge, out_ref, groups=True):
    live = live_sides()
    for side in range(SIDES):
        for channel in range(channels):
            base = NODE_ROWS * channel + 2 * side
            theirs = arrived_refs[side][4 * channel + 2 : 4 * channel + 4, :]
            if live[side] is not None:
                theirs = jnp.where(live[side], theirs, 0.0)
            out_ref[base : base + 2, :] = merge(part_ref[base : base + 2, :], theirs)
            if groups:
                theirs = arrived_refs[side][4 * channel : 4 * channel + 2, :]
                if live[side] is not None:
                    theirs = jnp.where(live[side], theirs, 0.0)
                out_ref[base + 8 : base + 10, :] = merge(part_ref[base + 8 : base + 10, :], theirs)


def rescale(scale, peak):
    seen = peak > 0.0
    return jnp.where(seen, scale / jnp.sqrt(jnp.where(seen, peak, 1.0)), 0.0)


def project_rows(ref):
    def every_third(start):
        return jnp.concatenate([ref[r : r + 1, :] for r in range(start, STRAINS, 3)], axis=0)

    top, first, second = [every_third(start) for start in range(3)]
    norm = jnp.sqrt(first * first + second * second)
    inside = norm <= top
    middle = norm > jnp.abs(top)
    factor = 0.5 * (1.0 + top / jnp.where(middle, norm, 1.0))
    gain = jnp.where(inside, 1.0, jnp.where(middle, factor, 0.0))
    top = jnp.where(inside, top, jnp.where(middle, factor * norm, 0.0))
    for start, values in enumerate((top, gain * first, gain * second)):
        for cone in range(4):
            ref[3 * cone + start : 3 * cone + start + 1, :] = values[cone : cone + 1, :]


def start_kernel(
    blocks_ref,
    conn_ref,
    send_ref,
    loads_ref,
    conn_out,
    key_out,
    scan_out,
    end_out,
    inverse_out,
    row_out,
    scale_out,
    part_out,
    own_loads_out,
    *rest,
):
    packets, (send_ids, term, items, peaks, ones) = rest[:4], rest[4:]
    make_plan(conn_ref, send_ref, conn_out, key_out, scan_out, end_out, inverse_out, send_ids)
    row = lax.broadcasted_iota(I32, (NODE_ROWS, LANES), 0)
    below, above = live_sides()[2:]
    first = jnp.where(row < 12, 1.0, jnp.where(row < 14, below.astype(F32), above.astype(F32)))
    for c in range(3):
        scale_out[NODE_ROWS * c : NODE_ROWS * (c + 1), :] = first
    ones[...] = jnp.ones_like(ones)
    measure_blocks(blocks_ref, ones, scale_out, conn_out, term, peaks)
    row_out[...] = 1.0 / jnp.sqrt(peaks[...])
    scatter_items(term, 3, (key_out, scan_out, end_out), items, part_out, jnp.maximum)
    pack(part_out, 3, packets)
    tables = [
        lambda r, c=c: loads_ref[0, 0, c : c + 1, r * LANES : (r + 1) * LANES] for c in range(3)
    ]
    for c, values in enumerate(table_picks(tables, 8, send_ids[...])):
        own_loads_out[8 * c : 8 * c + 8, :] = values
        for side in range(SIDES):
            packets[side][12 + 2 * c : 14 + 2 * c, :] = own_loads_out[
                8 * c + 2 * side : 8 * c + 2 * side + 2, :
            ]


def sweep_kernel(
    with_loads,
    blocks_ref,
    conn_ref,
    key_ref,
    scan_ref,
    end_ref,
    row_ref,
    scale_ref,
    part_ref,
    *rest,
):
    arrived, rest = rest[:4], rest[4:]
    if with_loads:
        own_loads, rest = rest[0], rest[1:]
    row_out, scale_out, part_out, rest = rest[0], rest[1], rest[2], rest[3:]
    if with_loads:
        loads_out, rest = rest[0], rest[1:]
    packets, (term, items, peaks, merged) = rest[:4], rest[4:]
    unpack(part_ref, 3, arrived, jnp.maximum, merged)
    scale_out[...] = rescale(scale_ref[...], merged[...])
    if with_loads:
        for c in range(3):
            loads_out[NODE_ROWS * c : NODE_ROWS * c + 8, :] = own_loads[8 * c : 8 * c + 8, :]
            for side in range(SIDES):
                base = NODE_ROWS * c + 8 + 2 * side
                loads_out[base : base + 2, :] = arrived[side][12 + 2 * c : 14 + 2 * c, :]
    measure_blocks(blocks_ref, row_ref, scale_out, conn_ref, term, peaks)
    row_out[...] = row_ref[...] / jnp.sqrt(row_ref[...] * peaks[...])
    scatter_items(term, 3, (key_ref, scan_ref, end_ref), items, part_out, jnp.maximum)
    pack(part_out, 3, packets)


def target_kernel(
    blocks_ref,
    conn_ref,
    key_ref,
    scan_ref,
    end_ref,
    row_ref,
    scale_ref,
    part_ref,
    loads_ref,
    *rest,
):
    arrived, rest = rest[:4], rest[4:]
    scale_out, strain_out, part_out, rest = rest[0], rest[1], rest[2], rest[3:]
    packets, (term, items, table, strain, cones) = rest[:4], rest[4:]
    unpack(part_ref, 3, arrived, jnp.maximum, table)
    scale = rescale(scale_ref[...], table[...])
    scale_out[...] = scale
    table[...] = scale * (scale * loads_ref[...])
    apply_blocks(blocks_ref, table, 1, conn_ref, strain)
    row = row_ref[...]
    image = row * strain[0:STRAINS, :]
    cones[...] = image
    project_rows(cones)
    strain[0:STRAINS, :] = row * image
    strain[STRAINS : 2 * STRAINS, :] = row * cones[...]
    strain_out[...] = 3.0 * image + 2.0 * cones[...]
    apply_transpose(blocks_ref, strain, 2, term)
    scatter_items(term, 6, (key_ref, scan_ref, end_ref), items, part_out, jnp.add)
    part_out[0:48, :] = part_out[0:48, :] * scale
    part_out[48:96, :] = part_out[48:96, :] * scale
    pack(part_out, 6, packets)


def second_kernel(
    blocks_ref, conn_ref, key_ref, scan_ref, end_ref, row_ref, scale_ref, part_ref, *rest
):
    arrived, rest = rest[:4], rest[4:]
    joint_out, strain_out, part_out, rest = rest[0], rest[1], rest[2], rest[3:]
    packets, (term, items, table, strain) = rest[:4], rest[4:]
    unpack(part_ref, 6, arrived, jnp.add, table)
    joint_out[...] = table[48:96, :]
    scale = scale_ref[...]
    table[0:48, :] = scale * table[0:48, :]
    table[48:96, :] = scale * table[48:96, :]
    apply_blocks(blocks_ref, table, 2, conn_ref, strain)
    row = row_ref[...]
    strain_out[...] = row * strain[STRAINS : 2 * STRAINS, :]
    strain[0:STRAINS, :] = row * (row * strain[0:STRAINS, :])
    apply_transpose(blocks_ref, strain, 1, term)
    scatter_items(term, 3, (key_ref, scan_ref, end_ref), items, part_out, jnp.add)
    part_out[...] = part_out[...] * scale
    pack(part_out, 3, packets)


def own_square(ref):
    total = jnp.zeros((8, LANES), F32)
    for c in range(3):
        mine = ref[NODE_ROWS * c : NODE_ROWS * c + 8, :]
        total = total + mine * mine
    return jnp.sum(total, axis=0, keepdims=True)


def third_kernel(
    blocks_ref, conn_ref, key_ref, scan_ref, end_ref, row_ref, scale_ref, part_ref, *rest
):
    arrived, rest = rest[:4], rest[4:]
    norm_out, part_out, rest = rest[0], rest[1], rest[2:]
    packets, (term, items, table, strain) = rest[:4], rest[4:]
    unpack(part_ref, 3, arrived, jnp.add, table)
    norm_out[...] = own_square(table)
    scale = scale_ref[...]
    table[...] = scale * table[...]
    apply_blocks(blocks_ref, table, 1, conn_ref, strain)
    row = row_ref[...]
    strain[...] = row * (row * strain[...])
    apply_transpose(blocks_ref, strain, 1, term)
    scatter_items(term, 3, (key_ref, scan_ref, end_ref), items, part_out, jnp.add)
    part_out[...] = part_out[...] * scale
    pack(part_out, 3, packets)


def norm_kernel(
    part_ref, norm_ref, scale_ref, loads_ref, joint_ref, inverse_ref, *rest
):
    arrived, (sums_out, velocity_out, table, lines) = rest[:4], rest[4:]
    unpack(part_ref, 3, arrived, jnp.add, table, groups=False)
    first = jnp.sum(norm_ref[...], axis=1, keepdims=True)
    last = jnp.sum(own_square(table), axis=1, keepdims=True)
    lane = lax.broadcasted_iota(I32, (1, LANES), 1)
    line = jnp.where(lane == 0, first, jnp.where(lane == 1, last, 0.0))
    sums_out[...] = jnp.broadcast_to(line, sums_out.shape)
    for c in range(3):
        base = NODE_ROWS * c
        scale = scale_ref[base : base + 8, :]
        lines[8 * c : 8 * c + 8, :] = scale * (scale * loads_ref[base : base + 8, :])
        lines[24 + 8 * c : 32 + 8 * c, :] = scale * joint_ref[base : base + 8, :]
    tables = [rows_of(lines, 8 * channel) for channel in range(6)]
    for channel, values in enumerate(table_picks(tables, 8, inverse_ref[...])):
        for r in range(8):
            velocity_out[channel : channel + 1, r * LANES : (r + 1) * LANES] = values[r : r + 1, :]


def final_kernel(
    sums_ref, step_ref, velocity_ref, base_ref, joint_ref, row_ref, velocity_out, multiplier_out, cones
):
    sums = jnp.sum(sums_ref[...], axis=0, keepdims=True)
    lane = lax.broadcasted_iota(I32, (1, LANES), 1)
    before = jnp.sum(jnp.where(lane == 0, sums, 0.0), axis=1, keepdims=True)
    after = jnp.sum(jnp.where(lane == 1, sums, 0.0), axis=1, keepdims=True)
    largest = jnp.sqrt(after + epsilon) / jnp.sqrt(before + epsilon)
    step = step_ref[0] / jnp.sqrt(largest)
    square = step * step
    target = velocity_ref[0:3, :]
    joint = velocity_ref[3:6, :]
    velocity_out[0, 0] = (2.0 * step) * (square * joint - target)
    cones[...] = square * (base_ref[...] - (4.0 * square) * joint_ref[...])
    project_rows(cones)
    multiplier_out[0, 0] = row_ref[...] * cones[...]


def call(body, out_shapes, scratch, *arrays, smem=()):
    specs = [
        pl.BlockSpec(memory_space=pltpu.SMEM if i in smem else pltpu.VMEM) for i in range(len(arrays))
    ]
    return pl.pallas_call(
        body,
        out_shape=[jax.ShapeDtypeStruct(shape, kind) for shape, kind in out_shapes],
        in_specs=specs,
        out_specs=[pl.BlockSpec(memory_space=pltpu.VMEM) for _ in out_shapes],
        scratch_shapes=[pltpu.VMEM(shape, kind) for shape, kind in scratch],
        compiler_params=pltpu.CompilerParams(vmem_limit_bytes=24 * 1024 * 1024),
    )(*arrays)


def exchange(packets):
    arrived = []
    for side, packet in enumerate(packets):
        axis = "sector" if side < 2 else "band"
        count = lax.axis_size(axis)
        toward = 1 if side % 2 == 0 else -1
        arrived.append(lax.ppermute(packets[side ^ 1], axis, [(i, (i + toward) % count) for i in range(count)]))
    return arrived


def per_device(blocks, connectivity, send_lists, nodal_loads, step_scale):
    packet = [((12, LANES), F32)] * 4
    nodes = ((48, LANES), F32)
    rows = ((STRAINS, 1024), F32)
    items = ((3 * ITEM_ROWS, LANES), F32)
    (conn, key, scan, end, inverse, row, scale, part, own_loads, *packets) = call(
        start_kernel,
        [
            ((64, LANES), I32),
            ((64, LANES), I32),
            ((8, LANES), I32),
            ((16, LANES), I32),
            ((8, LANES), I32),
            rows,
            nodes,
            nodes,
            ((24, LANES), F32),
        ]
        + [((18, LANES), F32)] * 4,
        [((8, LANES), I32), items, items, rows, rows],
        blocks,
        connectivity,
        send_lists,
        nodal_loads,
    )
    plan = (blocks, conn, key, scan, end)
    row, scale, part, loads, *packets = call(
        functools.partial(sweep_kernel, True),
        [rows, nodes, nodes, nodes] + packet,
        [items, items, rows, nodes],
        *plan,
        row,
        scale,
        part,
        *exchange(packets),
        own_loads,
    )
    row, scale, part, *packets = call(
        functools.partial(sweep_kernel, False),
        [rows, nodes, nodes] + packet,
        [items, items, rows, nodes],
        *plan,
        row,
        scale,
        part,
        *exchange(packets),
    )
    twice = ((6 * ITEM_ROWS, LANES), F32)
    scale, base, part, *packets = call(
        target_kernel,
        [nodes, rows, ((96, LANES), F32)] + [((24, LANES), F32)] * 4,
        [twice, twice, nodes, ((2 * STRAINS, 1024), F32), rows],
        *plan,
        row,
        scale,
        part,
        loads,
        *exchange(packets),
    )
    joint, image, part, *packets = call(
        second_kernel,
        [nodes, rows, nodes] + packet,
        [items, items, ((96, LANES), F32), ((2 * STRAINS, 1024), F32)],
        *plan,
        row,
        scale,
        part,
        *exchange(packets),
    )
    norm, part, *packets = call(
        third_kernel,
        [((1, LANES), F32), nodes] + packet,
        [items, items, nodes, rows],
        *plan,
        row,
        scale,
        part,
        *exchange(packets),
    )
    count = lax.axis_size("band") * lax.axis_size("sector")
    sums, lines = call(
        norm_kernel,
        [((count, LANES), F32), ((6, 1024), F32)],
        [nodes, nodes],
        part,
        norm,
        scale,
        loads,
        joint,
        inverse,
        *exchange(packets),
    )
    sums = lax.all_to_all(sums, AXES, 0, 0, tiled=True)
    return tuple(
        call(
            final_kernel,
            [((1, 1, 3, 1024), F32), ((1, 1, STRAINS, 1024), F32)],
            [rows],
            sums,
            step_scale,
            lines,
            base,
            image,
            row,
            smem=(1,),
        )
    )


def solution(mesh):
    in_specs = (
        P("band", "sector", None, None, None),
        P("band", "sector", None, None),
        P("band", "sector", None, None),
        P("band", "sector", None, None),
        P(),
    )
    out_specs = (P("band", "sector", None, None), P("band", "sector", None, None))
    return jax.shard_map(
        per_device, mesh=mesh, in_specs=in_specs, out_specs=out_specs, check_vma=False
    )
```

```python
import functools

import jax
import jax.numpy as jnp
from jax import lax
from jax.experimental import pallas as pl
from jax.experimental.pallas import tpu as pltpu
from jax.sharding import PartitionSpec as P

LANES = 128
CHUNKS = 8
STRAINS = 12
NODE_ROWS = 16
ITEM_ROWS = 64
SIDES = 4
PARTS = 3
AXES = ("band", "sector")
epsilon = 1e-06
F32 = jnp.float32
I32 = jnp.int32


def tile_iota(axis):
    return lax.broadcasted_iota(I32, (8, LANES), axis)


def pick(rows, index, axis):
    dims = lax.GatherDimensionNumbers(
        offset_dims=(),
        collapsed_slice_dims=(axis,),
        start_index_map=(axis,),
        operand_batching_dims=(1 - axis,),
        start_indices_batching_dims=(1 - axis,),
    )
    return lax.gather(
        rows,
        index[..., None],
        dims,
        slice_sizes=(1, 1),
        mode=lax.GatherScatterMode.PROMISE_IN_BOUNDS,
    )


def table_picks(row_getters, count, flat):
    lanes = flat & (LANES - 1)
    levels = count.bit_length() - 1
    bits = [(flat & (LANES << level)) != 0 for level in range(levels)]

    def descend(row_at, level, base):
        if level < 0:
            return pick(jnp.broadcast_to(row_at(base), (8, LANES)), lanes, 1)
        low = descend(row_at, level - 1, base)
        high = descend(row_at, level - 1, base + (1 << level))
        return jnp.where(bits[level], high, low)

    return [descend(row_at, levels - 1, 0) for row_at in row_getters]


def rows_of(ref, offset):
    return lambda row: ref[offset + row : offset + row + 1, :]


def chunk_at(chunk):
    return pl.ds(pl.multiple_of(chunk * LANES, LANES), LANES)


def eight_at(chunk, offset=0):
    return pl.ds(pl.multiple_of(offset + chunk * 8, 8), 8)


def group_shift(values, distance):
    if distance >= 8:
        return pltpu.roll(values, distance // 8, 1)
    turned = pltpu.roll(values, distance, 0)
    return jnp.where(tile_iota(0) < distance, pltpu.roll(turned, 1, 1), turned)


SCAN_STEPS = tuple(1 << step for step in range(10))


def sort_items(keys):
    sub, lane = tile_iota(0), tile_iota(1)
    size = 2
    while size <= 8192:
        half = size // 2
        while half >= 1:
            new = list(keys)

            def rising(register):
                if size < 8:
                    return (register & size) == 0
                if size < 64:
                    return (sub & (size // 8)) == 0
                if size < 8192:
                    return (lane & (size // 64)) == 0
                return True

            for register in range(8):
                up = rising(register)
                if half < 8:
                    other = register ^ half
                    if other < register:
                        continue
                    low = jnp.minimum(keys[register], keys[other])
                    high = jnp.maximum(keys[register], keys[other])
                    if isinstance(up, bool):
                        new[register], new[other] = (low, high) if up else (high, low)
                    else:
                        new[register] = jnp.where(up, low, high)
                        new[other] = jnp.where(up, high, low)
                    continue
                if half < 64:
                    step = half // 8
                    partner = pick(keys[register], sub ^ step, 0)
                    first = (sub & step) == 0
                else:
                    step = half // 64
                    partner = pick(keys[register], lane ^ step, 1)
                    first = (lane & step) == 0
                low = jnp.minimum(keys[register], partner)
                high = jnp.maximum(keys[register], partner)
                if isinstance(up, bool):
                    keep_low = first if up else jnp.logical_not(first)
                else:
                    keep_low = first == up
                new[register] = jnp.where(keep_low, low, high)
            keys = new
            half //= 2
        size *= 2
    return keys


def plan_kernel(conn_ref, send_ref, conn_out, key_out, scan_out, end_out, inverse_out, send_scratch):
    for half in range(8):
        start = (half % 2) * LANES
        send_scratch[half : half + 1, :] = send_ref[0, 0, half // 2 : half // 2 + 1, start : start + LANES]
    send_line = jnp.concatenate([send_scratch[row : row + 1, :] for row in range(8)], axis=1)
    place = lax.broadcasted_iota(I32, (8, 8 * LANES), 1)
    in_row = (send_line >> 7) == lax.broadcasted_iota(I32, (8, 8 * LANES), 0)
    left = jnp.concatenate(
        [
            jnp.where(in_row, (place >> 5).astype(F32), 0.0),
            jnp.where(in_row, (place & 31).astype(F32), 0.0),
        ],
        axis=0,
    ).astype(jnp.bfloat16)
    in_lane = (send_line & (LANES - 1)) == lax.broadcasted_iota(I32, (LANES, 8 * LANES), 0)
    right = jnp.where(in_lane, 1.0, 0.0).astype(jnp.bfloat16)
    found = lax.dot_general(left, right, (((1,), (1,)), ((), ())), preferred_element_type=F32)
    inverse_out[...] = (found[0:8] * 32.0 + found[8:16]).astype(I32)
    sub, lane = tile_iota(0), tile_iota(1)
    keys = []
    for chunk in range(CHUNKS):
        ids = conn_ref[0, 0, :, chunk * LANES : (chunk + 1) * LANES]
        (label,) = table_picks([rows_of(inverse_out, 0)], 8, ids & 1023)
        ids = jnp.where(ids < 1024, label, ids)
        conn_out[8 * chunk : 8 * chunk + 8, :] = ids
        keys.append(ids * 8192 + (chunk * 1024 + sub * LANES + lane))
    keys = sort_items(keys)
    for register in range(8):
        key_out[8 * register : 8 * register + 8, :] = keys[register]
    first, last = keys[0] >> 13, keys[7] >> 13
    group = lane * 8 + sub
    scan = jnp.zeros((8, LANES), I32)
    for step, distance in enumerate(SCAN_STEPS):
        same = (group >= distance) & (group_shift(last, distance) == last)
        scan = jnp.where(same, scan | (1 << step), scan)
    same = (group >= 1) & (group_shift(last, 1) == first)
    scan_out[...] = jnp.where(same, scan | (1 << len(SCAN_STEPS)), scan)
    lane_last = jnp.broadcast_to(key_out[63:64, :] >> 13, (8, LANES))
    for half in range(2):
        node = (half * 8 + sub) * LANES + lane
        column = jnp.zeros((8, LANES), I32)
        for step in (64, 32, 16, 8, 4, 2, 1):
            seen = pick(lane_last, column + (step - 1), 1)
            column = jnp.where(seen <= node, column + step, column)
        count = column * 64
        for row in range(ITEM_ROWS):
            seen = pick(jnp.broadcast_to(key_out[row : row + 1, :], (8, LANES)), column, 1)
            count = count + jnp.where((seen >> 13) <= node, 1, 0)
        place = count - 1
        row = (place & 7) * 8 + ((place >> 3) & 7)
        end_out[8 * half : 8 * half + 8, :] = row * LANES + (place >> 6)


def scatter_items(term_ref, channels, plan, sorted_ref, out_ref, merge):
    key_ref, scan_ref, end_ref = plan

    def bring(register, _):
        item = key_ref[eight_at(register), :] & 8191
        tables = [rows_of(term_ref, ITEM_ROWS * channel) for channel in range(channels)]
        for channel, values in enumerate(table_picks(tables, ITEM_ROWS, item)):
            sorted_ref[eight_at(register, ITEM_ROWS * channel), :] = values
        return 0

    lax.fori_loop(0, 8, bring, 0, unroll=True)
    nodes = [key_ref[8 * register : 8 * register + 8, :] >> 13 for register in range(8)]
    scan = scan_ref[...]
    follows = [(scan & (1 << step)) != 0 for step in range(len(SCAN_STEPS) + 1)]
    for channel in range(channels):
        base = ITEM_ROWS * channel
        runs = [sorted_ref[base : base + 8, :]]
        for register in range(1, 8):
            same = nodes[register] == nodes[register - 1]
            here = sorted_ref[base + 8 * register : base + 8 * register + 8, :]
            runs.append(merge(here, jnp.where(same, runs[-1], 0.0)))
        total = runs[7]
        for step, distance in enumerate(SCAN_STEPS):
            total = merge(total, jnp.where(follows[step], group_shift(total, distance), 0.0))
        carry = jnp.where(follows[-1], group_shift(total, 1), 0.0)
        for register in range(8):
            open_run = nodes[register] == nodes[0]
            sorted_ref[base + 8 * register : base + 8 * register + 8, :] = merge(
                runs[register], jnp.where(open_run, carry, 0.0)
            )

    def deliver(half, _):
        index = end_ref[eight_at(half), :]
        tables = [rows_of(sorted_ref, ITEM_ROWS * channel) for channel in range(channels)]
        for channel, values in enumerate(table_picks(tables, ITEM_ROWS, index)):
            out_ref[eight_at(half, NODE_ROWS * channel), :] = values
        return 0

    lax.fori_loop(0, 2, deliver, 0, unroll=True)


def bf16_parts(values, count):
    parts = []
    for _ in range(count):
        part = values.astype(jnp.bfloat16).astype(F32)
        parts.append(part)
        values = values - part
    return parts


def one_line(rows):
    return jnp.concatenate([rows[k : k + 1] for k in range(8)], axis=1)


def scatter_sums(term_ref, channels, conn_ref, out_ref):
    width = 8 * LANES
    row_ids = lax.broadcasted_iota(I32, (NODE_ROWS, width), 0).astype(F32)
    lane_ids = lax.broadcasted_iota(I32, (LANES, width), 0).astype(F32)
    total = jnp.zeros((channels * PARTS * NODE_ROWS, LANES), F32)
    for chunk in range(CHUNKS):
        ids = conn_ref[8 * chunk : 8 * chunk + 8, :]
        in_row = one_line((ids >> 7).astype(F32)) == row_ids
        in_lane = one_line((ids & (LANES - 1)).astype(F32)) == lane_ids
        left = []
        for channel in range(channels):
            base = ITEM_ROWS * channel + 8 * chunk
            for part in bf16_parts(one_line(term_ref[base : base + 8, :]), PARTS):
                left.append(jnp.where(in_row, part, 0.0).astype(jnp.bfloat16))
        total = total + lax.dot_general(
            jnp.concatenate(left, axis=0),
            jnp.where(in_lane, 1.0, 0.0).astype(jnp.bfloat16),
            (((1,), (1,)), ((), ())),
            preferred_element_type=F32,
        )
    for channel in range(channels):
        base = PARTS * NODE_ROWS * channel
        out = total[base : base + NODE_ROWS]
        for part in range(1, PARTS):
            out = out + total[base + part * NODE_ROWS : base + (part + 1) * NODE_ROWS]
        out_ref[NODE_ROWS * channel : NODE_ROWS * (channel + 1), :] = out


def node_picks(table_ref, channels, conn_ref, chunk):
    tables = [rows_of(table_ref, NODE_ROWS * channel) for channel in range(channels)]
    return table_picks(tables, NODE_ROWS, conn_ref[eight_at(chunk), :])


def row_maxima(blocks_ref, picked, at, max_ref):
    for r in range(STRAINS):
        sized = [jnp.abs(blocks_ref[0, 0, r, 8 * c : 8 * c + 8, at]) for c in range(3)]
        for k, scales in enumerate(picked):
            whole = sized[0] * scales[0]
            for c in range(1, 3):
                whole = jnp.maximum(whole, sized[c] * scales[c])
            max_ref[STRAINS * k + r : STRAINS * k + r + 1, at] = jnp.max(whole, axis=0, keepdims=True)


def column_maxima(blocks_ref, row_ref, term_ref, first_channel):
    for chunk in range(CHUNKS):
        at = slice(chunk * LANES, (chunk + 1) * LANES)
        best = [jnp.zeros((8, LANES), F32)] * 3
        for r in range(STRAINS):
            row = 1.0 if row_ref is None else row_ref[r : r + 1, at]
            for c in range(3):
                size = jnp.abs(blocks_ref[0, 0, r, 8 * c : 8 * c + 8, at]) * row
                best[c] = jnp.maximum(best[c], size)
        for c in range(3):
            base = ITEM_ROWS * (first_channel + c) + 8 * chunk
            term_ref[base : base + 8, :] = best[c]


def apply_blocks(blocks_ref, table_ref, sets, conn_ref, strain_ref):
    def one(chunk, _):
        values = node_picks(table_ref, 3 * sets, conn_ref, chunk)
        at = chunk_at(chunk)
        for r in range(STRAINS):
            parts = [blocks_ref[0, 0, r, 8 * c : 8 * c + 8, at] for c in range(3)]
            for k in range(sets):
                mine = values[3 * k : 3 * k + 3]
                total = parts[0] * mine[0] + parts[1] * mine[1] + parts[2] * mine[2]
                strain_ref[STRAINS * k + r : STRAINS * k + r + 1, at] = jnp.sum(
                    total, axis=0, keepdims=True
                )
        return 0

    lax.fori_loop(0, CHUNKS, one, 0, unroll=True)


def apply_transpose(blocks_ref, strain_ref, sets, term_ref):
    def one(chunk, _):
        at = chunk_at(chunk)
        totals = [jnp.zeros((8, LANES), F32)] * (3 * sets)
        for r in range(STRAINS):
            parts = [blocks_ref[0, 0, r, 8 * c : 8 * c + 8, at] for c in range(3)]
            for k in range(sets):
                strain = strain_ref[STRAINS * k + r : STRAINS * k + r + 1, at]
                for c in range(3):
                    totals[3 * k + c] = totals[3 * k + c] + parts[c] * strain
        for channel in range(3 * sets):
            term_ref[eight_at(chunk, ITEM_ROWS * channel), :] = totals[channel]
        return 0

    lax.fori_loop(0, CHUNKS, one, 0, unroll=True)


def even_places():
    return lax.axis_index("sector") % 2 == 0, lax.axis_index("band") % 2 == 0


def side_rows(part_ref, side, channel, length=2):
    base = NODE_ROWS * channel + 2 * side
    return part_ref[base : base + length, :]


def pack(part_ref, channels, packet_refs):
    even_sector, even_band = even_places()
    for slot, (even, low, high) in enumerate(
        ((even_sector, 1, 0), (even_band, 3, 2), (even_sector, 0, 1), (even_band, 2, 3))
    ):
        for channel in range(channels):
            for part in range(2):
                packet_refs[slot][4 * channel + 2 * part : 4 * channel + 2 * part + 2, :] = jnp.where(
                    even,
                    side_rows(part_ref, high + 4 * part, channel),
                    side_rows(part_ref, low + 4 * part, channel),
                )


def by_side(arrived_refs):
    even_sector, even_band = even_places()
    odd_cycle, odd_band, even_cycle, even_pair = [ref[...] for ref in arrived_refs]
    below, above = live_sides()
    return [
        jnp.where(even_sector, odd_cycle, even_cycle),
        jnp.where(even_sector, even_cycle, odd_cycle),
        jnp.where(below, jnp.where(even_band, odd_band, even_pair), 0.0),
        jnp.where(above, jnp.where(even_band, even_pair, odd_band), 0.0),
    ]


def live_sides():
    band = lax.axis_index("band")
    return [band > 0, band < lax.axis_size("band") - 1]


def unpack(part_ref, channels, arrived, merge, out_ref):
    for side in range(SIDES):
        for channel in range(channels):
            base = NODE_ROWS * channel + 2 * side
            theirs = arrived[side][4 * channel : 4 * channel + 4]
            out_ref[base : base + 2, :] = merge(part_ref[base : base + 2, :], theirs[2:4])
            out_ref[base + 8 : base + 10, :] = merge(part_ref[base + 8 : base + 10, :], theirs[0:2])


def rescale(scale, peak):
    peak = scale * peak
    seen = peak > 0.0
    return jnp.where(seen, scale / jnp.sqrt(jnp.where(seen, peak, 1.0)), 0.0)


def project_rows(ref):
    def every_third(start):
        return jnp.concatenate([ref[r : r + 1, :] for r in range(start, STRAINS, 3)], axis=0)

    top, first, second = [every_third(start) for start in range(3)]
    norm = jnp.sqrt(first * first + second * second)
    inside = norm <= top
    middle = norm > jnp.abs(top)
    factor = 0.5 * (1.0 + top / jnp.where(middle, norm, 1.0))
    gain = jnp.where(inside, 1.0, jnp.where(middle, factor, 0.0))
    top = jnp.where(inside, top, jnp.where(middle, factor * norm, 0.0))
    for start, values in enumerate((top, gain * first, gain * second)):
        for cone in range(4):
            ref[3 * cone + start : 3 * cone + start + 1, :] = values[cone : cone + 1, :]


def start_kernel(
    blocks_ref, ids_ref, loads_ref, send_ref, key_ref, scan_ref, end_ref, row_out, part_out, loads_out, *rest
):
    packets, (term, items, peaks) = rest[:4], rest[4:]
    below, above = [live.astype(F32) for live in live_sides()]
    for chunk in range(CHUNKS):
        at = slice(chunk * LANES, (chunk + 1) * LANES)
        ids = ids_ref[0, 0, :, at]
        scale = jnp.where(ids < 1536, 1.0, jnp.where(ids < 1792, below, above))
        row_maxima(blocks_ref, [[scale] * 3], at, peaks)
    row_out[...] = 1.0 / jnp.sqrt(peaks[...])
    column_maxima(blocks_ref, None, term, 0)
    column_maxima(blocks_ref, row_out, term, 3)
    scatter_items(term, 6, (key_ref, scan_ref, end_ref), items, part_out, jnp.maximum)
    pack(part_out, 6, packets)
    tables = [rows_of(loads_ref, 8 * c) for c in range(3)]
    for c, values in enumerate(table_picks(tables, 8, send_ref[...])):
        loads_out[8 * c : 8 * c + 8, :] = values
    even_sector, even_band = even_places()
    for slot, (even, low, high) in enumerate(
        ((even_sector, 1, 0), (even_band, 3, 2), (even_sector, 0, 1), (even_band, 2, 3))
    ):
        for c in range(3):
            packets[slot][24 + 2 * c : 26 + 2 * c, :] = jnp.where(
                even,
                loads_out[8 * c + 2 * high : 8 * c + 2 * high + 2, :],
                loads_out[8 * c + 2 * low : 8 * c + 2 * low + 2, :],
            )


def sweep_kernel(
    blocks_ref, conn_ref, key_ref, scan_ref, end_ref, row_ref, part_ref, own_loads, *rest
):
    arrived, rest = by_side(rest[:4]), rest[4:]
    row_out, scale_out, part_out, loads_out, rest = rest[0], rest[1], rest[2], rest[3], rest[4:]
    packets, (term, items, peaks, merged, second_row) = rest[:4], rest[4:]
    unpack(part_ref, 6, arrived, jnp.maximum, merged)
    for c in range(3):
        loads_out[NODE_ROWS * c : NODE_ROWS * c + 8, :] = own_loads[8 * c : 8 * c + 8, :]
        for side in range(SIDES):
            base = NODE_ROWS * c + 8 + 2 * side
            loads_out[base : base + 2, :] = arrived[side][24 + 2 * c : 26 + 2 * c]
    row = lax.broadcasted_iota(I32, (NODE_ROWS, LANES), 0)
    below, above = [live.astype(F32) for live in live_sides()]
    start = jnp.where(row < 12, 1.0, jnp.where(row < 14, below, above))
    for c in range(3):
        first = rescale(start, merged[NODE_ROWS * c : NODE_ROWS * (c + 1), :])
        later = NODE_ROWS * (c + 3)
        second = rescale(first, merged[later : later + NODE_ROWS, :])
        merged[NODE_ROWS * c : NODE_ROWS * (c + 1), :] = first
        merged[later : later + NODE_ROWS, :] = second
        scale_out[NODE_ROWS * c : NODE_ROWS * (c + 1), :] = second
    for chunk in range(CHUNKS):
        at = slice(chunk * LANES, (chunk + 1) * LANES)
        scales = node_picks(merged, 6, conn_ref, chunk)
        row_maxima(blocks_ref, [scales[0:3], scales[3:6]], at, peaks)
    first_row = row_ref[...]
    second_row[...] = first_row / jnp.sqrt(first_row * peaks[0:STRAINS, :])
    row_out[...] = second_row[...] / jnp.sqrt(second_row[...] * peaks[STRAINS : 2 * STRAINS, :])
    column_maxima(blocks_ref, second_row, term, 0)
    scatter_items(term, 3, (key_ref, scan_ref, end_ref), items, part_out, jnp.maximum)
    pack(part_out, 3, packets)


def target_kernel(
    blocks_ref,
    conn_ref,
    row_ref,
    scale_ref,
    part_ref,
    loads_ref,
    *rest,
):
    arrived, rest = rest[:4], rest[4:]
    scale_out, strain_out, part_out, rest = rest[0], rest[1], rest[2], rest[3:]
    packets, (term, table, strain, cones) = rest[:4], rest[4:]
    arrived = by_side(arrived)
    unpack(part_ref, 3, arrived, jnp.maximum, table)
    scale = rescale(scale_ref[...], table[...])
    scale_out[...] = scale
    table[...] = scale * (scale * loads_ref[...])
    apply_blocks(blocks_ref, table, 1, conn_ref, strain)
    row = row_ref[...]
    image = row * strain[0:STRAINS, :]
    cones[...] = image
    project_rows(cones)
    strain[0:STRAINS, :] = row * image
    strain[STRAINS : 2 * STRAINS, :] = row * cones[...]
    strain_out[...] = 3.0 * image + 2.0 * cones[...]
    apply_transpose(blocks_ref, strain, 2, term)
    scatter_sums(term, 6, conn_ref, part_out)
    part_out[0:48, :] = part_out[0:48, :] * scale
    part_out[48:96, :] = part_out[48:96, :] * scale
    pack(part_out, 6, packets)


def second_kernel(
    blocks_ref, conn_ref, row_ref, scale_ref, part_ref, *rest
):
    arrived, rest = rest[:4], rest[4:]
    joint_out, strain_out, part_out, rest = rest[0], rest[1], rest[2], rest[3:]
    packets, (term, table, strain) = rest[:4], rest[4:]
    arrived = by_side(arrived)
    unpack(part_ref, 6, arrived, jnp.add, table)
    joint_out[...] = table[48:96, :]
    scale = scale_ref[...]
    table[0:48, :] = scale * table[0:48, :]
    table[48:96, :] = scale * table[48:96, :]
    apply_blocks(blocks_ref, table, 2, conn_ref, strain)
    row = row_ref[...]
    strain_out[...] = row * strain[STRAINS : 2 * STRAINS, :]
    strain[0:STRAINS, :] = row * (row * strain[0:STRAINS, :])
    apply_transpose(blocks_ref, strain, 1, term)
    scatter_sums(term, 3, conn_ref, part_out)
    part_out[...] = part_out[...] * scale
    pack(part_out, 3, packets)


def own_square(ref):
    total = jnp.zeros((8, LANES), F32)
    for c in range(3):
        mine = ref[NODE_ROWS * c : NODE_ROWS * c + 8, :]
        total = total + mine * mine
    return jnp.sum(total, axis=0, keepdims=True)


def third_kernel(
    blocks_ref, conn_ref, row_ref, scale_ref, part_ref, *rest
):
    arrived, rest = rest[:4], rest[4:]
    norm_out, part_out, right_out, above_out, term, table, strain = rest
    unpack(part_ref, 3, by_side(arrived), jnp.add, table)
    norm_out[...] = own_square(table)
    scale = scale_ref[...]
    table[...] = scale * table[...]
    apply_blocks(blocks_ref, table, 1, conn_ref, strain)
    row = row_ref[...]
    strain[...] = row * (row * strain[...])
    apply_transpose(blocks_ref, strain, 1, term)
    scatter_sums(term, 3, conn_ref, part_out)
    part_out[...] = part_out[...] * scale
    for packet, side in ((right_out, 1), (above_out, 3)):
        for channel in range(3):
            packet[4 * channel : 4 * channel + 2, :] = side_rows(part_out, side, channel)
            packet[4 * channel + 2 : 4 * channel + 4, :] = side_rows(part_out, side + 4, channel)


def norm_kernel(
    part_ref, norm_ref, scale_ref, loads_ref, joint_ref, inverse_ref, left_ref, below_ref, *rest
):
    sums_out, velocity_out, lines = rest
    below, above = live_sides()
    squares = jnp.zeros((2, LANES), F32)
    for channel in range(3):
        for side, arrived, live in ((0, left_ref, True), (2, below_ref, below)):
            theirs = arrived[4 * channel : 4 * channel + 4, :]
            theirs = jnp.where(live, theirs, 0.0)
            own = side_rows(part_ref, side, channel) + theirs[2:4]
            copy = side_rows(part_ref, side + 4, channel) + theirs[0:2]
            squares = squares + own * own + copy * copy
        alone = jnp.where(above, 0.0, side_rows(part_ref, 3, channel))
        squares = squares + alone * alone
    first = jnp.sum(norm_ref[...], axis=1, keepdims=True)
    last = jnp.sum(jnp.sum(squares, axis=0, keepdims=True), axis=1, keepdims=True)
    lane = lax.broadcasted_iota(I32, (1, LANES), 1)
    line = jnp.where(lane == 0, first, jnp.where(lane == 1, last, 0.0))
    sums_out[...] = jnp.broadcast_to(line, sums_out.shape)
    for c in range(3):
        base = NODE_ROWS * c
        scale = scale_ref[base : base + 8, :]
        lines[8 * c : 8 * c + 8, :] = scale * (scale * loads_ref[base : base + 8, :])
        lines[24 + 8 * c : 32 + 8 * c, :] = scale * joint_ref[base : base + 8, :]
    tables = [rows_of(lines, 8 * channel) for channel in range(6)]
    for channel, values in enumerate(table_picks(tables, 8, inverse_ref[...])):
        velocity_out[8 * channel : 8 * channel + 8, :] = values


def final_kernel(
    sums_ref, step_ref, velocity_ref, base_ref, joint_ref, row_ref, velocity_out, multiplier_out, *rest
):
    velocity, cones, flat, semaphores = rest
    sums = jnp.sum(sums_ref[...], axis=0, keepdims=True)
    lane = lax.broadcasted_iota(I32, (1, LANES), 1)
    before = jnp.sum(jnp.where(lane == 0, sums, 0.0), axis=1, keepdims=True)
    after = jnp.sum(jnp.where(lane == 1, sums, 0.0), axis=1, keepdims=True)
    largest = jnp.sqrt(after + epsilon) / jnp.sqrt(before + epsilon)
    step = step_ref[0] / jnp.sqrt(largest)
    square = step * step
    velocity[...] = (2.0 * step) * (square * velocity_ref[24:48, :] - velocity_ref[0:24, :])
    first = pltpu.make_async_copy(velocity, velocity_out, semaphores.at[0])
    first.start()
    cones[...] = square * (base_ref[...] - (4.0 * square) * joint_ref[...])
    project_rows(cones)
    cones[...] = row_ref[...] * cones[...]
    for r in range(STRAINS):
        for chunk in range(CHUNKS):
            flat[8 * r + chunk : 8 * r + chunk + 1, :] = cones[
                r : r + 1, chunk * LANES : (chunk + 1) * LANES
            ]
    second = pltpu.make_async_copy(flat, multiplier_out, semaphores.at[1])
    second.start()
    first.wait()
    second.wait()


def call(body, out_shapes, scratch, *arrays, smem=(), outside_results=False, work=0):
    def space(i):
        return pltpu.SMEM if i in smem else pltpu.VMEM

    result = pltpu.HBM if outside_results else pltpu.VMEM
    return pl.pallas_call(
        body,
        out_shape=[jax.ShapeDtypeStruct(shape, kind) for shape, kind in out_shapes],
        in_specs=[pl.BlockSpec(memory_space=space(i)) for i in range(len(arrays))],
        out_specs=[pl.BlockSpec(memory_space=result) for _ in out_shapes],
        scratch_shapes=[
            entry if not isinstance(entry, tuple) else pltpu.VMEM(*entry) for entry in scratch
        ],
        cost_estimate=pl.CostEstimate(flops=work, bytes_accessed=work // 256, transcendentals=0),
        compiler_params=pltpu.CompilerParams(vmem_limit_bytes=24 * 1024 * 1024),
    )(*arrays)


def swap_pairs(axis, odd):
    count = lax.axis_size(axis)
    return [(i, (((i - odd) ^ 1) + odd) % count) for i in range(count)]


PAIRS = (("sector", 1), ("band", 1), ("sector", 0), ("band", 0))


def exchange(packets):
    return [
        lax.ppermute(packet, axis, swap_pairs(axis, odd)) for packet, (axis, odd) in zip(packets, PAIRS)
    ]


def shift_up(packet, axis):
    count = lax.axis_size(axis)
    return lax.ppermute(packet, axis, [(i, (i + 1) % count) for i in range(count)])


def per_device(blocks, connectivity, send_lists, nodal_loads, step_scale):
    packet = [((12, LANES), F32)] * 4
    nodes = ((48, LANES), F32)
    rows = ((STRAINS, 1024), F32)
    items = ((3 * ITEM_ROWS, LANES), F32)
    twice = ((6 * ITEM_ROWS, LANES), F32)
    ids = ((64, LANES), I32)
    few = ((8, LANES), I32)
    conn, key, scan, end, inverse, send = call(
        plan_kernel,
        [ids, ids, few, ((16, LANES), I32), few, few],
        [],
        connectivity,
        send_lists,
        work=4_000_000_000,
    )
    row, part, own_loads, *packets = call(
        start_kernel,
        [rows, ((96, LANES), F32), ((24, LANES), F32)] + [((30, LANES), F32)] * 4,
        [twice, twice, rows],
        blocks,
        connectivity,
        nodal_loads.reshape(24, LANES),
        send,
        key,
        scan,
        end,
    )
    row, scale, part, loads, *packets = call(
        sweep_kernel,
        [rows, nodes, nodes, nodes] + packet,
        [items, items, ((2 * STRAINS, 1024), F32), ((96, LANES), F32), rows],
        blocks,
        conn,
        key,
        scan,
        end,
        row,
        part,
        own_loads,
        *exchange(packets),
    )
    scale, base, part, *packets = call(
        target_kernel,
        [nodes, rows, ((96, LANES), F32)] + [((24, LANES), F32)] * 4,
        [twice, nodes, ((2 * STRAINS, 1024), F32), rows],
        blocks,
        conn,
        row,
        scale,
        part,
        loads,
        *exchange(packets),
    )
    joint, image, part, *packets = call(
        second_kernel,
        [nodes, rows, nodes] + packet,
        [items, ((96, LANES), F32), ((2 * STRAINS, 1024), F32)],
        blocks,
        conn,
        row,
        scale,
        part,
        *exchange(packets),
    )
    norm, part, right, above = call(
        third_kernel,
        [((1, LANES), F32), nodes] + packet[:2],
        [items, nodes, rows],
        blocks,
        conn,
        row,
        scale,
        part,
        *exchange(packets),
    )
    count = lax.axis_size("band") * lax.axis_size("sector")
    sums, lines = call(
        norm_kernel,
        [((count, LANES), F32), ((48, LANES), F32)],
        [nodes],
        part,
        norm,
        scale,
        loads,
        joint,
        inverse,
        shift_up(right, "sector"),
        shift_up(above, "band"),
    )
    sums = lax.all_to_all(sums, AXES, 0, 0, tiled=True)
    velocities, multipliers = call(
        final_kernel,
        [((24, LANES), F32), ((96, LANES), F32)],
        [((24, LANES), F32), rows, ((96, LANES), F32), pltpu.SemaphoreType.DMA((2,))],
        sums,
        step_scale,
        lines,
        base,
        image,
        row,
        smem=(1,),
        outside_results=True,
    )
    return velocities.reshape(1, 1, 3, 1024), multipliers.reshape(1, 1, STRAINS, 1024)


def solution(mesh):
    in_specs = (
        P("band", "sector", None, None, None),
        P("band", "sector", None, None),
        P("band", "sector", None, None),
        P("band", "sector", None, None),
        P(),
    )
    out_specs = (P("band", "sector", None, None), P("band", "sector", None, None))
    return jax.shard_map(
        per_device, mesh=mesh, in_specs=in_specs, out_specs=out_specs, check_vma=False
    )
```

```python
import functools

import jax
import jax.numpy as jnp
from jax import lax
from jax.experimental import pallas as pl
from jax.experimental.pallas import tpu as pltpu
from jax.sharding import PartitionSpec as P

LANES = 128
CHUNKS = 8
STRAINS = 12
NODE_ROWS = 16
ITEM_ROWS = 64
SIDES = 4
PARTS = 2
AXES = ("band", "sector")
epsilon = 1e-06
F32 = jnp.float32
I32 = jnp.int32


def tile_iota(axis):
    return lax.broadcasted_iota(I32, (8, LANES), axis)


def pick(rows, index, axis):
    dims = lax.GatherDimensionNumbers(
        offset_dims=(),
        collapsed_slice_dims=(axis,),
        start_index_map=(axis,),
        operand_batching_dims=(1 - axis,),
        start_indices_batching_dims=(1 - axis,),
    )
    return lax.gather(
        rows,
        index[..., None],
        dims,
        slice_sizes=(1, 1),
        mode=lax.GatherScatterMode.PROMISE_IN_BOUNDS,
    )


def table_picks(row_getters, rows, flat):
    rows = tuple(range(rows)) if isinstance(rows, int) else rows
    lanes = flat & (LANES - 1)
    levels = rows[-1].bit_length()
    bits = [(flat & (LANES << level)) != 0 for level in range(levels)]

    def descend(row_at, level, base):
        if level < 0:
            return pick(jnp.broadcast_to(row_at(base), (8, LANES)), lanes, 1) if base in rows else None
        low = descend(row_at, level - 1, base)
        high = descend(row_at, level - 1, base + (1 << level))
        if low is None or high is None:
            return high if low is None else low
        return jnp.where(bits[level], high, low)

    return [descend(row_at, levels - 1, 0) for row_at in row_getters]


def rows_of(ref, offset):
    return lambda row: ref[offset + row : offset + row + 1, :]


def group_shift(values, distance):
    if distance >= 8:
        return pltpu.roll(values, distance // 8, 1)
    turned = pltpu.roll(values, distance, 0)
    return jnp.where(tile_iota(0) < distance, pltpu.roll(turned, 1, 1), turned)


SCAN_STEPS = tuple(1 << step for step in range(10))
RUNS = 5
SORTED_ROWS = 8 * RUNS
LOOSE_ROWS = tuple(row for row in range(ITEM_ROWS) if row % 8 >= 3)


def sort_items(keys):
    sub, lane = tile_iota(0), tile_iota(1)
    size = 2
    while size <= 8192:
        half = size // 2
        while half >= 1:
            new = list(keys)

            def rising(register):
                if size < 8:
                    return (register & size) == 0
                if size < 64:
                    return (sub & (size // 8)) == 0
                if size < 8192:
                    return (lane & (size // 64)) == 0
                return True

            for register in range(8):
                up = rising(register)
                if half < 8:
                    other = register ^ half
                    if other < register:
                        continue
                    low = jnp.minimum(keys[register], keys[other])
                    high = jnp.maximum(keys[register], keys[other])
                    if isinstance(up, bool):
                        new[register], new[other] = (low, high) if up else (high, low)
                    else:
                        new[register] = jnp.where(up, low, high)
                        new[other] = jnp.where(up, high, low)
                    continue
                if half < 64:
                    step = half // 8
                    partner = pick(keys[register], sub ^ step, 0)
                    first = (sub & step) == 0
                else:
                    step = half // 64
                    partner = pick(keys[register], lane ^ step, 1)
                    first = (lane & step) == 0
                low = jnp.minimum(keys[register], partner)
                high = jnp.maximum(keys[register], partner)
                if isinstance(up, bool):
                    keep_low = first if up else jnp.logical_not(first)
                else:
                    keep_low = first == up
                new[register] = jnp.where(keep_low, low, high)
            keys = new
            half //= 2
        size *= 2
    return keys


def one_line(rows):
    return jnp.concatenate([rows[k : k + 1] for k in range(rows.shape[0])], axis=1)


def inverse_of(line, code, rows):
    width = line.shape[1]
    in_row = (line >> 7) == lax.broadcasted_iota(I32, (rows, width), 0)
    left = jnp.concatenate(
        [
            jnp.where(in_row, (code >> 7).astype(F32), 0.0),
            jnp.where(in_row, (code & (LANES - 1)).astype(F32), 0.0),
        ],
        axis=0,
    ).astype(jnp.bfloat16)
    in_lane = (line & (LANES - 1)) == lax.broadcasted_iota(I32, (LANES, width), 0)
    right = jnp.where(in_lane, 1.0, 0.0).astype(jnp.bfloat16)
    found = lax.dot_general(left, right, (((1,), (1,)), ((), ())), preferred_element_type=F32)
    return (found[0:rows] * 128.0 + found[rows : 2 * rows]).astype(I32)


def plan_kernel(
    conn_ref, send_ref, conn_out, key_out, scan_out, end_out, own_out, pair_out, inverse_out, send_out, keys_ref
):
    for half in range(8):
        start = (half % 2) * LANES
        send_out[half : half + 1, :] = send_ref[0, 0, half // 2 : half // 2 + 1, start : start + LANES]
    place = lax.broadcasted_iota(I32, (1, 8 * LANES), 1)
    inverse_out[...] = inverse_of(one_line(send_out[...]), place, 8)
    sub, lane = tile_iota(0), tile_iota(1)
    keys = []
    for chunk in range(CHUNKS):
        ids = conn_ref[0, 0, :, chunk * LANES : (chunk + 1) * LANES]
        (label,) = table_picks([rows_of(inverse_out, 0)], 8, ids & 1023)
        ids = jnp.where(ids < 1024, label, ids)
        conn_out[8 * chunk : 8 * chunk + 8, :] = ids
        item = ids * 8192 + (chunk * 1024 + sub * LANES + lane)
        keys.append(jnp.where(sub < 3, 2048 * 8192, item))
    first_line = jnp.concatenate([conn_out[8 * chunk : 8 * chunk + 1, :] for chunk in range(CHUNKS)], axis=1)
    own_out[...] = inverse_of(first_line, place, 8)
    pair_line = jnp.concatenate(
        [conn_out[8 * chunk + k : 8 * chunk + k + 1, :] for chunk in range(CHUNKS) for k in (1, 2)], axis=1
    )
    pair_out[...] = inverse_of(pair_line, lax.broadcasted_iota(I32, (1, 16 * LANES), 1), NODE_ROWS)
    keys = sort_items(keys)
    for register in range(8):
        keys_ref[8 * register : 8 * register + 8, :] = keys[register]
    group = lane * 8 + sub
    runs = []
    for register in range(RUNS):
        place = group * RUNS + register
        row = (place & 7) * 8 + ((place >> 3) & 7)
        (moved,) = table_picks([rows_of(keys_ref, 0)], ITEM_ROWS, row * LANES + (place >> 6))
        runs.append(moved)
        key_out[8 * register : 8 * register + 8, :] = moved
    first, last = runs[0] >> 13, runs[-1] >> 13
    scan = jnp.zeros((8, LANES), I32)
    for step, distance in enumerate(SCAN_STEPS):
        same = (group >= distance) & (group_shift(last, distance) == last)
        scan = jnp.where(same, scan | (1 << step), scan)
    same = (group >= 1) & (group_shift(last, 1) == first)
    scan_out[...] = jnp.where(same, scan | (1 << len(SCAN_STEPS)), scan)
    lane_last = jnp.broadcast_to(keys_ref[63:64, :] >> 13, (8, LANES))
    for half in range(2):
        node = (half * 8 + sub) * LANES + lane
        column = jnp.zeros((8, LANES), I32)
        for step in (64, 32, 16, 8, 4, 2, 1):
            seen = pick(lane_last, column + (step - 1), 1)
            column = jnp.where(seen <= node, column + step, column)
        count = column * 64
        before = pick(lane_last, jnp.maximum(column - 1, 0), 1)
        named = (column > 0) & (before == node)
        for row in range(ITEM_ROWS):
            seen = pick(jnp.broadcast_to(keys_ref[row : row + 1, :], (8, LANES)), column, 1) >> 13
            count = count + jnp.where(seen <= node, 1, 0)
            named = named | (seen == node)
        place = jnp.maximum(count - 1, 0)
        place = jnp.where(named, place, 0)
        share = (place * 52429) >> 18
        row = (place - share * RUNS) * 8 + (share & 7)
        end = row * LANES + (share >> 3)
        end_out[8 * half : 8 * half + 8, :] = jnp.where(named, end, 8192)


def scatter_maxima(term_ref, channels, plan, sorted_ref, out_ref):
    key_ref, scan_ref, end_ref, own_ref, pair_ref = plan
    tables = [rows_of(term_ref, ITEM_ROWS * channel) for channel in range(channels)]
    nodes = []
    for register in range(RUNS):
        key = key_ref[8 * register : 8 * register + 8, :]
        nodes.append(key >> 13)
        for channel, values in enumerate(table_picks(tables, LOOSE_ROWS, key & 8191)):
            base = SORTED_ROWS * channel + 8 * register
            sorted_ref[base : base + 8, :] = values
    scan = scan_ref[...]
    follows = [(scan & (1 << step)) != 0 for step in range(len(SCAN_STEPS) + 1)]
    for channel in range(channels):
        base = SORTED_ROWS * channel
        runs = [sorted_ref[base : base + 8, :]]
        for register in range(1, RUNS):
            same = nodes[register] == nodes[register - 1]
            here = sorted_ref[base + 8 * register : base + 8 * register + 8, :]
            runs.append(jnp.maximum(here, jnp.where(same, runs[-1], 0.0)))
        total = runs[-1]
        for step, distance in enumerate(SCAN_STEPS):
            total = jnp.maximum(total, jnp.where(follows[step], group_shift(total, distance), 0.0))
        carry = jnp.where(follows[-1], group_shift(total, 1), 0.0)
        for register in range(RUNS):
            open_run = nodes[register] == nodes[0]
            sorted_ref[base + 8 * register : base + 8 * register + 8, :] = jnp.maximum(
                runs[register], jnp.where(open_run, carry, 0.0)
            )
    sorted_tables = [rows_of(sorted_ref, SORTED_ROWS * channel) for channel in range(channels)]
    first_tables = [lambda row, at=at: at(8 * row) for at in tables]
    pair_tables = [lambda row, at=at: at((row >> 1) * 8 + (row & 1) + 1) for at in tables]
    own = table_picks(first_tables, 8, own_ref[...])
    for half in range(2):
        index = end_ref[8 * half : 8 * half + 8, :]
        loose = table_picks(sorted_tables, SORTED_ROWS, index & 8191)
        paired = table_picks(pair_tables, NODE_ROWS, pair_ref[8 * half : 8 * half + 8, :])
        for channel in range(channels):
            best = jnp.maximum(jnp.where(index < 8192, loose[channel], 0.0), paired[channel])
            if half == 0:
                best = jnp.maximum(best, own[channel])
            base = NODE_ROWS * channel + 8 * half
            out_ref[base : base + 8, :] = best


def node_picks(table_ref, channels, conn_ref, chunk):
    tables = [rows_of(table_ref, NODE_ROWS * channel) for channel in range(channels)]
    return table_picks(tables, NODE_ROWS, conn_ref[8 * chunk : 8 * chunk + 8, :])


def bf16_parts(values, count):
    parts = []
    for _ in range(count):
        part = values.astype(jnp.bfloat16).astype(F32)
        parts.append(part)
        values = values - part
    return parts


def scatter_sums(term_ref, channels, conn_ref, out_ref):
    width = 8 * LANES
    row_ids = lax.broadcasted_iota(I32, (NODE_ROWS, width), 0).astype(F32)
    lane_ids = lax.broadcasted_iota(I32, (LANES, width), 0).astype(F32)
    total = jnp.zeros((channels * PARTS * NODE_ROWS, LANES), F32)
    for chunk in range(CHUNKS):
        ids = conn_ref[8 * chunk : 8 * chunk + 8, :]
        in_row = one_line((ids >> 7).astype(F32)) == row_ids
        in_lane = one_line((ids & (LANES - 1)).astype(F32)) == lane_ids
        left = []
        for channel in range(channels):
            base = ITEM_ROWS * channel + 8 * chunk
            for part in bf16_parts(one_line(term_ref[base : base + 8, :]), PARTS):
                left.append(jnp.where(in_row, part, 0.0).astype(jnp.bfloat16))
        total = total + lax.dot_general(
            jnp.concatenate(left, axis=0),
            jnp.where(in_lane, 1.0, 0.0).astype(jnp.bfloat16),
            (((1,), (1,)), ((), ())),
            preferred_element_type=F32,
        )
    for channel in range(channels):
        base = PARTS * NODE_ROWS * channel
        out = total[base : base + NODE_ROWS]
        for part in range(1, PARTS):
            out = out + total[base + part * NODE_ROWS : base + (part + 1) * NODE_ROWS]
        out_ref[NODE_ROWS * channel : NODE_ROWS * (channel + 1), :] = out


def row_maxima(blocks_ref, picked, at, max_ref):
    for r in range(STRAINS):
        sized = [jnp.abs(blocks_ref[0, 0, r, 8 * c : 8 * c + 8, at]) for c in range(3)]
        for k, scales in enumerate(picked):
            whole = sized[0] * scales[0]
            for c in range(1, 3):
                whole = jnp.maximum(whole, sized[c] * scales[c])
            max_ref[STRAINS * k + r : STRAINS * k + r + 1, at] = jnp.max(whole, axis=0, keepdims=True)


def column_maxima(blocks_ref, row_ref, term_ref, first_channel):
    for chunk in range(CHUNKS):
        at = slice(chunk * LANES, (chunk + 1) * LANES)
        best = [jnp.zeros((8, LANES), F32)] * 3
        for r in range(STRAINS):
            row = 1.0 if row_ref is None else row_ref[r : r + 1, at]
            for c in range(3):
                size = jnp.abs(blocks_ref[0, 0, r, 8 * c : 8 * c + 8, at]) * row
                best[c] = jnp.maximum(best[c], size)
        for c in range(3):
            base = ITEM_ROWS * (first_channel + c) + 8 * chunk
            term_ref[base : base + 8, :] = best[c]


def apply_blocks(blocks_ref, table_ref, sets, conn_ref, strain_ref):
    for chunk in range(CHUNKS):
        values = node_picks(table_ref, 3 * sets, conn_ref, chunk)
        at = slice(chunk * LANES, (chunk + 1) * LANES)
        for r in range(STRAINS):
            parts = [blocks_ref[0, 0, r, 8 * c : 8 * c + 8, at] for c in range(3)]
            for k in range(sets):
                mine = values[3 * k : 3 * k + 3]
                total = parts[0] * mine[0] + parts[1] * mine[1] + parts[2] * mine[2]
                strain_ref[STRAINS * k + r : STRAINS * k + r + 1, at] = jnp.sum(
                    total, axis=0, keepdims=True
                )


def apply_transpose(blocks_ref, strain_ref, sets, term_ref):
    for chunk in range(CHUNKS):
        at = slice(chunk * LANES, (chunk + 1) * LANES)
        totals = [jnp.zeros((8, LANES), F32)] * (3 * sets)
        for r in range(STRAINS):
            parts = [blocks_ref[0, 0, r, 8 * c : 8 * c + 8, at] for c in range(3)]
            for k in range(sets):
                strain = strain_ref[STRAINS * k + r : STRAINS * k + r + 1, at]
                for c in range(3):
                    totals[3 * k + c] = totals[3 * k + c] + parts[c] * strain
        for channel in range(3 * sets):
            row = ITEM_ROWS * channel + 8 * chunk
            term_ref[row : row + 8, :] = totals[channel]


def even_places():
    return lax.axis_index("sector") % 2 == 0, lax.axis_index("band") % 2 == 0


def side_rows(part_ref, side, channel, length=2):
    base = NODE_ROWS * channel + 2 * side
    return part_ref[base : base + length, :]


def pack(part_ref, channels, packet_refs):
    even_sector, even_band = even_places()
    for slot, (even, low, high) in enumerate(
        ((even_sector, 1, 0), (even_band, 3, 2), (even_sector, 0, 1), (even_band, 2, 3))
    ):
        for channel in range(channels):
            for part in range(2):
                packet_refs[slot][4 * channel + 2 * part : 4 * channel + 2 * part + 2, :] = jnp.where(
                    even,
                    side_rows(part_ref, high + 4 * part, channel),
                    side_rows(part_ref, low + 4 * part, channel),
                )


def by_side(arrived_refs):
    even_sector, even_band = even_places()
    odd_cycle, odd_band, even_cycle, even_pair = [ref[...] for ref in arrived_refs]
    below, above = live_sides()
    return [
        jnp.where(even_sector, odd_cycle, even_cycle),
        jnp.where(even_sector, even_cycle, odd_cycle),
        jnp.where(below, jnp.where(even_band, odd_band, even_pair), 0.0),
        jnp.where(above, jnp.where(even_band, even_pair, odd_band), 0.0),
    ]


def live_sides():
    band = lax.axis_index("band")
    return [band > 0, band < lax.axis_size("band") - 1]


def unpack(part_ref, channels, arrived, merge, out_ref):
    for side in range(SIDES):
        for channel in range(channels):
            base = NODE_ROWS * channel + 2 * side
            theirs = arrived[side][4 * channel : 4 * channel + 4]
            out_ref[base : base + 2, :] = merge(part_ref[base : base + 2, :], theirs[2:4])
            out_ref[base + 8 : base + 10, :] = merge(part_ref[base + 8 : base + 10, :], theirs[0:2])


def rescale(scale, peak):
    peak = scale * peak
    seen = peak > 0.0
    return jnp.where(seen, scale / jnp.sqrt(jnp.where(seen, peak, 1.0)), 0.0)


def project_rows(ref):
    def every_third(start):
        return jnp.concatenate([ref[r : r + 1, :] for r in range(start, STRAINS, 3)], axis=0)

    top, first, second = [every_third(start) for start in range(3)]
    norm = jnp.sqrt(first * first + second * second)
    inside = norm <= top
    middle = norm > jnp.abs(top)
    factor = 0.5 * (1.0 + top / jnp.where(middle, norm, 1.0))
    gain = jnp.where(inside, 1.0, jnp.where(middle, factor, 0.0))
    top = jnp.where(inside, top, jnp.where(middle, factor * norm, 0.0))
    for start, values in enumerate((top, gain * first, gain * second)):
        for cone in range(4):
            ref[3 * cone + start : 3 * cone + start + 1, :] = values[cone : cone + 1, :]


def start_kernel(
    blocks_ref, ids_ref, loads_ref, send_ref, *rest
):
    plan, (row_out, part_out, loads_out), rest = rest[:5], rest[5:8], rest[8:]
    packets, (term, items, peaks) = rest[:4], rest[4:]
    below, above = [live.astype(F32) for live in live_sides()]
    for chunk in range(CHUNKS):
        at = slice(chunk * LANES, (chunk + 1) * LANES)
        ids = ids_ref[0, 0, :, at]
        scale = jnp.where(ids < 1536, 1.0, jnp.where(ids < 1792, below, above))
        row_maxima(blocks_ref, [[scale] * 3], at, peaks)
    row_out[...] = 1.0 / jnp.sqrt(peaks[...])
    column_maxima(blocks_ref, None, term, 0)
    column_maxima(blocks_ref, row_out, term, 3)
    scatter_maxima(term, 6, plan, items, part_out)
    pack(part_out, 6, packets)
    tables = [rows_of(loads_ref, 8 * c) for c in range(3)]
    for c, values in enumerate(table_picks(tables, 8, send_ref[...])):
        loads_out[8 * c : 8 * c + 8, :] = values
    even_sector, even_band = even_places()
    for slot, (even, low, high) in enumerate(
        ((even_sector, 1, 0), (even_band, 3, 2), (even_sector, 0, 1), (even_band, 2, 3))
    ):
        for c in range(3):
            packets[slot][24 + 2 * c : 26 + 2 * c, :] = jnp.where(
                even,
                loads_out[8 * c + 2 * high : 8 * c + 2 * high + 2, :],
                loads_out[8 * c + 2 * low : 8 * c + 2 * low + 2, :],
            )


def sweep_kernel(
    blocks_ref, conn_ref, row_ref, part_ref, own_loads, *rest
):
    plan, rest = rest[:5], rest[5:]
    arrived, rest = by_side(rest[:4]), rest[4:]
    row_out, scale_out, part_out, loads_out, rest = rest[0], rest[1], rest[2], rest[3], rest[4:]
    packets, (term, items, peaks, merged, second_row) = rest[:4], rest[4:]
    unpack(part_ref, 6, arrived, jnp.maximum, merged)
    for c in range(3):
        loads_out[NODE_ROWS * c : NODE_ROWS * c + 8, :] = own_loads[8 * c : 8 * c + 8, :]
        for side in range(SIDES):
            base = NODE_ROWS * c + 8 + 2 * side
            loads_out[base : base + 2, :] = arrived[side][24 + 2 * c : 26 + 2 * c]
    row = lax.broadcasted_iota(I32, (NODE_ROWS, LANES), 0)
    below, above = [live.astype(F32) for live in live_sides()]
    start = jnp.where(row < 12, 1.0, jnp.where(row < 14, below, above))
    for c in range(3):
        first = rescale(start, merged[NODE_ROWS * c : NODE_ROWS * (c + 1), :])
        later = NODE_ROWS * (c + 3)
        second = rescale(first, merged[later : later + NODE_ROWS, :])
        merged[NODE_ROWS * c : NODE_ROWS * (c + 1), :] = first
        merged[later : later + NODE_ROWS, :] = second
        scale_out[NODE_ROWS * c : NODE_ROWS * (c + 1), :] = second
    for chunk in range(CHUNKS):
        at = slice(chunk * LANES, (chunk + 1) * LANES)
        scales = node_picks(merged, 6, conn_ref, chunk)
        row_maxima(blocks_ref, [scales[0:3], scales[3:6]], at, peaks)
    first_row = row_ref[...]
    second_row[...] = first_row / jnp.sqrt(first_row * peaks[0:STRAINS, :])
    row_out[...] = second_row[...] / jnp.sqrt(second_row[...] * peaks[STRAINS : 2 * STRAINS, :])
    column_maxima(blocks_ref, second_row, term, 0)
    scatter_maxima(term, 3, plan, items, part_out)
    pack(part_out, 3, packets)


def target_kernel(
    blocks_ref,
    conn_ref,
    row_ref,
    scale_ref,
    part_ref,
    loads_ref,
    *rest,
):
    arrived, rest = rest[:4], rest[4:]
    scale_out, strain_out, part_out, rest = rest[0], rest[1], rest[2], rest[3:]
    packets, (term, table, strain, cones) = rest[:4], rest[4:]
    arrived = by_side(arrived)
    unpack(part_ref, 3, arrived, jnp.maximum, table)
    scale = rescale(scale_ref[...], table[...])
    scale_out[...] = scale
    table[...] = scale * (scale * loads_ref[...])
    apply_blocks(blocks_ref, table, 1, conn_ref, strain)
    row = row_ref[...]
    image = row * strain[0:STRAINS, :]
    cones[...] = image
    project_rows(cones)
    strain[0:STRAINS, :] = row * image
    strain[STRAINS : 2 * STRAINS, :] = row * cones[...]
    strain_out[...] = 3.0 * image + 2.0 * cones[...]
    apply_transpose(blocks_ref, strain, 2, term)
    scatter_sums(term, 6, conn_ref, part_out)
    part_out[0:48, :] = part_out[0:48, :] * scale
    part_out[48:96, :] = part_out[48:96, :] * scale
    pack(part_out, 6, packets)


def second_kernel(
    blocks_ref, conn_ref, row_ref, scale_ref, part_ref, *rest
):
    arrived, rest = rest[:4], rest[4:]
    joint_out, strain_out, part_out, rest = rest[0], rest[1], rest[2], rest[3:]
    packets, (term, table, strain) = rest[:4], rest[4:]
    arrived = by_side(arrived)
    unpack(part_ref, 6, arrived, jnp.add, table)
    joint_out[...] = table[48:96, :]
    scale = scale_ref[...]
    table[0:48, :] = scale * table[0:48, :]
    table[48:96, :] = scale * table[48:96, :]
    apply_blocks(blocks_ref, table, 2, conn_ref, strain)
    row = row_ref[...]
    strain_out[...] = row * strain[STRAINS : 2 * STRAINS, :]
    strain[0:STRAINS, :] = row * (row * strain[0:STRAINS, :])
    apply_transpose(blocks_ref, strain, 1, term)
    scatter_sums(term, 3, conn_ref, part_out)
    part_out[...] = part_out[...] * scale
    pack(part_out, 3, packets)


def own_square(ref):
    total = jnp.zeros((8, LANES), F32)
    for c in range(3):
        mine = ref[NODE_ROWS * c : NODE_ROWS * c + 8, :]
        total = total + mine * mine
    return jnp.sum(total, axis=0, keepdims=True)


def third_kernel(
    blocks_ref, conn_ref, row_ref, scale_ref, part_ref, *rest
):
    arrived, rest = rest[:4], rest[4:]
    norm_out, part_out, right_out, above_out, term, table, strain = rest
    unpack(part_ref, 3, by_side(arrived), jnp.add, table)
    norm_out[...] = own_square(table)
    scale = scale_ref[...]
    table[...] = scale * table[...]
    apply_blocks(blocks_ref, table, 1, conn_ref, strain)
    row = row_ref[...]
    strain[...] = row * (row * strain[...])
    apply_transpose(blocks_ref, strain, 1, term)
    scatter_sums(term, 3, conn_ref, part_out)
    part_out[...] = part_out[...] * scale
    for packet, side in ((right_out, 1), (above_out, 3)):
        for channel in range(3):
            packet[4 * channel : 4 * channel + 2, :] = side_rows(part_out, side, channel)
            packet[4 * channel + 2 : 4 * channel + 4, :] = side_rows(part_out, side + 4, channel)


def norm_kernel(
    part_ref, norm_ref, scale_ref, loads_ref, joint_ref, inverse_ref, left_ref, below_ref, *rest
):
    sums_out, velocity_out, lines = rest
    below, above = live_sides()
    squares = jnp.zeros((2, LANES), F32)
    for channel in range(3):
        for side, arrived, live in ((0, left_ref, True), (2, below_ref, below)):
            theirs = arrived[4 * channel : 4 * channel + 4, :]
            theirs = jnp.where(live, theirs, 0.0)
            own = side_rows(part_ref, side, channel) + theirs[2:4]
            copy = side_rows(part_ref, side + 4, channel) + theirs[0:2]
            squares = squares + own * own + copy * copy
        alone = jnp.where(above, 0.0, side_rows(part_ref, 3, channel))
        squares = squares + alone * alone
    first = jnp.sum(norm_ref[...], axis=1, keepdims=True)
    last = jnp.sum(jnp.sum(squares, axis=0, keepdims=True), axis=1, keepdims=True)
    lane = lax.broadcasted_iota(I32, (1, LANES), 1)
    line = jnp.where(lane == 0, first, jnp.where(lane == 1, last, 0.0))
    sums_out[...] = jnp.broadcast_to(line, sums_out.shape)
    for c in range(3):
        base = NODE_ROWS * c
        scale = scale_ref[base : base + 8, :]
        lines[8 * c : 8 * c + 8, :] = scale * (scale * loads_ref[base : base + 8, :])
        lines[24 + 8 * c : 32 + 8 * c, :] = scale * joint_ref[base : base + 8, :]
    tables = [rows_of(lines, 8 * channel) for channel in range(6)]
    for channel, values in enumerate(table_picks(tables, 8, inverse_ref[...])):
        velocity_out[8 * channel : 8 * channel + 8, :] = values


def final_kernel(
    sums_ref, step_ref, velocity_ref, base_ref, joint_ref, row_ref, velocity_out, multiplier_out, *rest
):
    velocity, cones, flat, semaphores = rest
    sums = jnp.sum(sums_ref[...], axis=0, keepdims=True)
    lane = lax.broadcasted_iota(I32, (1, LANES), 1)
    before = jnp.sum(jnp.where(lane == 0, sums, 0.0), axis=1, keepdims=True)
    after = jnp.sum(jnp.where(lane == 1, sums, 0.0), axis=1, keepdims=True)
    largest = jnp.sqrt(after + epsilon) / jnp.sqrt(before + epsilon)
    step = step_ref[0] / jnp.sqrt(largest)
    square = step * step
    velocity[...] = (2.0 * step) * (square * velocity_ref[24:48, :] - velocity_ref[0:24, :])
    first = pltpu.make_async_copy(velocity, velocity_out, semaphores.at[0])
    first.start()
    cones[...] = square * (base_ref[...] - (4.0 * square) * joint_ref[...])
    project_rows(cones)
    cones[...] = row_ref[...] * cones[...]
    for r in range(STRAINS):
        for chunk in range(CHUNKS):
            flat[8 * r + chunk : 8 * r + chunk + 1, :] = cones[
                r : r + 1, chunk * LANES : (chunk + 1) * LANES
            ]
    second = pltpu.make_async_copy(flat, multiplier_out, semaphores.at[1])
    second.start()
    first.wait()
    second.wait()


def call(body, out_shapes, scratch, *arrays, smem=(), outside_results=False, work=0):
    def space(i):
        return pltpu.SMEM if i in smem else pltpu.VMEM

    result = pltpu.HBM if outside_results else pltpu.VMEM
    return pl.pallas_call(
        body,
        out_shape=[jax.ShapeDtypeStruct(shape, kind) for shape, kind in out_shapes],
        in_specs=[pl.BlockSpec(memory_space=space(i)) for i in range(len(arrays))],
        out_specs=[pl.BlockSpec(memory_space=result) for _ in out_shapes],
        scratch_shapes=[
            entry if not isinstance(entry, tuple) else pltpu.VMEM(*entry) for entry in scratch
        ],
        cost_estimate=pl.CostEstimate(flops=work, bytes_accessed=work // 256, transcendentals=0),
        compiler_params=pltpu.CompilerParams(vmem_limit_bytes=24 * 1024 * 1024),
    )(*arrays)


def swap_pairs(axis, odd):
    count = lax.axis_size(axis)
    return [(i, (((i - odd) ^ 1) + odd) % count) for i in range(count)]


PAIRS = (("sector", 1), ("band", 1), ("sector", 0), ("band", 0))


def exchange(packets):
    return [
        lax.ppermute(packet, axis, swap_pairs(axis, odd)) for packet, (axis, odd) in zip(packets, PAIRS)
    ]


def shift_up(packet, axis):
    count = lax.axis_size(axis)
    return lax.ppermute(packet, axis, [(i, (i + 1) % count) for i in range(count)])


def per_device(blocks, connectivity, send_lists, nodal_loads, step_scale):
    packet = [((12, LANES), F32)] * 4
    nodes = ((48, LANES), F32)
    rows = ((STRAINS, 1024), F32)
    items = ((3 * ITEM_ROWS, LANES), F32)
    twice = ((6 * ITEM_ROWS, LANES), F32)
    ids = ((64, LANES), I32)
    few = ((8, LANES), I32)
    conn, *plan, inverse, send = call(
        plan_kernel,
        [ids, ((SORTED_ROWS, LANES), I32), few, ((16, LANES), I32), few, ((16, LANES), I32), few, few],
        [ids],
        connectivity,
        send_lists,
        work=4_000_000_000,
    )
    row, part, own_loads, *packets = call(
        start_kernel,
        [rows, ((96, LANES), F32), ((24, LANES), F32)] + [((30, LANES), F32)] * 4,
        [twice, ((6 * SORTED_ROWS, LANES), F32), rows],
        blocks,
        connectivity,
        nodal_loads.reshape(24, LANES),
        send,
        *plan,
    )
    row, scale, part, loads, *packets = call(
        sweep_kernel,
        [rows, nodes, nodes, nodes] + packet,
        [items, ((3 * SORTED_ROWS, LANES), F32), ((2 * STRAINS, 1024), F32), ((96, LANES), F32), rows],
        blocks,
        conn,
        row,
        part,
        own_loads,
        *plan,
        *exchange(packets),
    )
    scale, base, part, *packets = call(
        target_kernel,
        [nodes, rows, ((96, LANES), F32)] + [((24, LANES), F32)] * 4,
        [twice, nodes, ((2 * STRAINS, 1024), F32), rows],
        blocks,
        conn,
        row,
        scale,
        part,
        loads,
        *exchange(packets),
    )
    joint, image, part, *packets = call(
        second_kernel,
        [nodes, rows, nodes] + packet,
        [items, ((96, LANES), F32), ((2 * STRAINS, 1024), F32)],
        blocks,
        conn,
        row,
        scale,
        part,
        *exchange(packets),
    )
    norm, part, right, above = call(
        third_kernel,
        [((1, LANES), F32), nodes] + packet[:2],
        [items, nodes, rows],
        blocks,
        conn,
        row,
        scale,
        part,
        *exchange(packets),
    )
    count = lax.axis_size("band") * lax.axis_size("sector")
    sums, lines = call(
        norm_kernel,
        [((count, LANES), F32), ((48, LANES), F32)],
        [nodes],
        part,
        norm,
        scale,
        loads,
        joint,
        inverse,
        shift_up(right, "sector"),
        shift_up(above, "band"),
    )
    sums = lax.all_to_all(sums, AXES, 0, 0, tiled=True)
    velocities, multipliers = call(
        final_kernel,
        [((24, LANES), F32), ((96, LANES), F32)],
        [((24, LANES), F32), rows, ((96, LANES), F32), pltpu.SemaphoreType.DMA((2,))],
        sums,
        step_scale,
        lines,
        base,
        image,
        row,
        smem=(1,),
        outside_results=True,
    )
    return velocities.reshape(1, 1, 3, 1024), multipliers.reshape(1, 1, STRAINS, 1024)


def solution(mesh):
    in_specs = (
        P("band", "sector", None, None, None),
        P("band", "sector", None, None),
        P("band", "sector", None, None),
        P("band", "sector", None, None),
        P(),
    )
    out_specs = (P("band", "sector", None, None), P("band", "sector", None, None))
    return jax.shard_map(
        per_device, mesh=mesh, in_specs=in_specs, out_specs=out_specs, check_vma=False
    )
```

```python
import functools

import jax
import jax.numpy as jnp
from jax import lax
from jax.experimental import pallas as pl
from jax.experimental.pallas import tpu as pltpu
from jax.sharding import PartitionSpec as P

LANES = 128
CHUNKS = 8
STRAINS = 12
NODE_ROWS = 16
ITEM_ROWS = 64
SIDES = 4
PARTS = 2
LIMIT = 54000
AXES = ("band", "sector")
epsilon = 1e-06
F32 = jnp.float32
I32 = jnp.int32


def tile_iota(axis):
    return lax.broadcasted_iota(I32, (8, LANES), axis)


def pick(rows, index, axis):
    dims = lax.GatherDimensionNumbers(
        offset_dims=(),
        collapsed_slice_dims=(axis,),
        start_index_map=(axis,),
        operand_batching_dims=(1 - axis,),
        start_indices_batching_dims=(1 - axis,),
    )
    return lax.gather(
        rows,
        index[..., None],
        dims,
        slice_sizes=(1, 1),
        mode=lax.GatherScatterMode.PROMISE_IN_BOUNDS,
    )


def table_picks(row_getters, rows, flat):
    rows = tuple(range(rows)) if isinstance(rows, int) else rows
    lanes = flat & (LANES - 1)
    levels = rows[-1].bit_length()
    bits = [(flat & (LANES << level)) != 0 for level in range(levels)]

    def descend(row_at, level, base):
        if level < 0:
            return pick(jnp.broadcast_to(row_at(base), (8, LANES)), lanes, 1) if base in rows else None
        low = descend(row_at, level - 1, base)
        high = descend(row_at, level - 1, base + (1 << level))
        if low is None or high is None:
            return high if low is None else low
        return jnp.where(bits[level], high, low)

    return [descend(row_at, levels - 1, 0) for row_at in row_getters]


def rows_of(ref, offset):
    return lambda row: ref[offset + row : offset + row + 1, :]


def group_shift(values, distance):
    if distance >= 8:
        return pltpu.roll(values, distance // 8, 1)
    turned = pltpu.roll(values, distance, 0)
    return jnp.where(tile_iota(0) < distance, pltpu.roll(turned, 1, 1), turned)


SCAN_STEPS = tuple(1 << step for step in range(10))
RUNS = 5
SORTED_ROWS = 8 * RUNS
LOOSE_ROWS = tuple(row for row in range(ITEM_ROWS) if row % 8 >= 3)


def sort_items(keys):
    sub, lane = tile_iota(0), tile_iota(1)
    size = 2
    while size <= 8192:
        half = size // 2
        while half >= 1:
            new = list(keys)

            def rising(register):
                if size < 8:
                    return (register & size) == 0
                if size < 64:
                    return (sub & (size // 8)) == 0
                if size < 8192:
                    return (lane & (size // 64)) == 0
                return True

            for register in range(8):
                up = rising(register)
                if half < 8:
                    other = register ^ half
                    if other < register:
                        continue
                    low = jnp.minimum(keys[register], keys[other])
                    high = jnp.maximum(keys[register], keys[other])
                    if isinstance(up, bool):
                        new[register], new[other] = (low, high) if up else (high, low)
                    else:
                        new[register] = jnp.where(up, low, high)
                        new[other] = jnp.where(up, high, low)
                    continue
                if half < 64:
                    step = half // 8
                    partner = pick(keys[register], sub ^ step, 0)
                    first = (sub & step) == 0
                else:
                    step = half // 64
                    partner = pick(keys[register], lane ^ step, 1)
                    first = (lane & step) == 0
                low = jnp.minimum(keys[register], partner)
                high = jnp.maximum(keys[register], partner)
                if isinstance(up, bool):
                    keep_low = first if up else jnp.logical_not(first)
                else:
                    keep_low = first == up
                new[register] = jnp.where(keep_low, low, high)
            keys = new
            half //= 2
        size *= 2
    return keys


def one_line(rows):
    return jnp.concatenate([rows[k : k + 1] for k in range(rows.shape[0])], axis=1)


def inverse_of(line, code, rows):
    width = line.shape[1]
    in_row = (line >> 7) == lax.broadcasted_iota(I32, (rows, width), 0)
    left = jnp.concatenate(
        [
            jnp.where(in_row, (code >> 7).astype(F32), 0.0),
            jnp.where(in_row, (code & (LANES - 1)).astype(F32), 0.0),
        ],
        axis=0,
    ).astype(jnp.bfloat16)
    in_lane = (line & (LANES - 1)) == lax.broadcasted_iota(I32, (LANES, width), 0)
    right = jnp.where(in_lane, 1.0, 0.0).astype(jnp.bfloat16)
    found = lax.dot_general(left, right, (((1,), (1,)), ((), ())), preferred_element_type=F32)
    return (found[0:rows] * 128.0 + found[rows : 2 * rows]).astype(I32)


def make_plan(
    conn_ref, send_ref, conn_out, key_out, scan_out, end_out, own_out, pair_out, inverse_out, send_out, keys_ref
):
    for half in range(8):
        start = (half % 2) * LANES
        send_out[half : half + 1, :] = send_ref[0, 0, half // 2 : half // 2 + 1, start : start + LANES]
    place = lax.broadcasted_iota(I32, (1, 8 * LANES), 1)
    inverse_out[...] = inverse_of(one_line(send_out[...]), place, 8)
    sub, lane = tile_iota(0), tile_iota(1)
    keys = []
    for chunk in range(CHUNKS):
        ids = conn_ref[0, 0, :, chunk * LANES : (chunk + 1) * LANES]
        (label,) = table_picks([rows_of(inverse_out, 0)], 8, ids & 1023)
        ids = jnp.where(ids < 1024, label, ids)
        conn_out[8 * chunk : 8 * chunk + 8, :] = ids
        item = ids * 8192 + (chunk * 1024 + sub * LANES + lane)
        keys.append(jnp.where(sub < 3, 2048 * 8192, item))
    first_line = jnp.concatenate([conn_out[8 * chunk : 8 * chunk + 1, :] for chunk in range(CHUNKS)], axis=1)
    own_out[...] = inverse_of(first_line, place, 8)
    pair_line = jnp.concatenate(
        [conn_out[8 * chunk + k : 8 * chunk + k + 1, :] for chunk in range(CHUNKS) for k in (1, 2)], axis=1
    )
    pair_out[...] = inverse_of(pair_line, lax.broadcasted_iota(I32, (1, 16 * LANES), 1), NODE_ROWS)
    keys = sort_items(keys)
    for register in range(8):
        keys_ref[8 * register : 8 * register + 8, :] = keys[register]
    group = lane * 8 + sub
    runs = []
    for register in range(RUNS):
        place = group * RUNS + register
        row = (place & 7) * 8 + ((place >> 3) & 7)
        (moved,) = table_picks([rows_of(keys_ref, 0)], ITEM_ROWS, row * LANES + (place >> 6))
        runs.append(moved)
        key_out[8 * register : 8 * register + 8, :] = moved
    first, last = runs[0] >> 13, runs[-1] >> 13
    scan = jnp.zeros((8, LANES), I32)
    for step, distance in enumerate(SCAN_STEPS):
        same = (group >= distance) & (group_shift(last, distance) == last)
        scan = jnp.where(same, scan | (1 << step), scan)
    same = (group >= 1) & (group_shift(last, 1) == first)
    scan_out[...] = jnp.where(same, scan | (1 << len(SCAN_STEPS)), scan)
    lane_last = jnp.broadcast_to(keys_ref[63:64, :] >> 13, (8, LANES))
    for half in range(2):
        node = (half * 8 + sub) * LANES + lane
        column = jnp.zeros((8, LANES), I32)
        for step in (64, 32, 16, 8, 4, 2, 1):
            seen = pick(lane_last, column + (step - 1), 1)
            column = jnp.where(seen <= node, column + step, column)
        count = column * 64
        before = pick(lane_last, jnp.maximum(column - 1, 0), 1)
        named = (column > 0) & (before == node)
        for row in range(ITEM_ROWS):
            seen = pick(jnp.broadcast_to(keys_ref[row : row + 1, :], (8, LANES)), column, 1) >> 13
            count = count + jnp.where(seen <= node, 1, 0)
            named = named | (seen == node)
        place = jnp.maximum(count - 1, 0)
        place = jnp.where(named, place, 0)
        share = (place * 52429) >> 18
        row = (place - share * RUNS) * 8 + (share & 7)
        end = row * LANES + (share >> 3)
        end_out[8 * half : 8 * half + 8, :] = jnp.where(named, end, 8192)


def scatter_maxima(term_ref, channels, plan, sorted_ref, out_ref):
    key_ref, scan_ref, end_ref, own_ref, pair_ref = plan
    tables = [rows_of(term_ref, ITEM_ROWS * channel) for channel in range(channels)]
    nodes = []
    for register in range(RUNS):
        key = key_ref[8 * register : 8 * register + 8, :]
        nodes.append(key >> 13)
        for channel, values in enumerate(table_picks(tables, LOOSE_ROWS, key & 8191)):
            base = SORTED_ROWS * channel + 8 * register
            sorted_ref[base : base + 8, :] = values
    scan = scan_ref[...]
    follows = [(scan & (1 << step)) != 0 for step in range(len(SCAN_STEPS) + 1)]
    for channel in range(channels):
        base = SORTED_ROWS * channel
        runs = [sorted_ref[base : base + 8, :]]
        for register in range(1, RUNS):
            same = nodes[register] == nodes[register - 1]
            here = sorted_ref[base + 8 * register : base + 8 * register + 8, :]
            runs.append(jnp.maximum(here, jnp.where(same, runs[-1], 0.0)))
        total = runs[-1]
        for step, distance in enumerate(SCAN_STEPS):
            total = jnp.maximum(total, jnp.where(follows[step], group_shift(total, distance), 0.0))
        carry = jnp.where(follows[-1], group_shift(total, 1), 0.0)
        for register in range(RUNS):
            open_run = nodes[register] == nodes[0]
            sorted_ref[base + 8 * register : base + 8 * register + 8, :] = jnp.maximum(
                runs[register], jnp.where(open_run, carry, 0.0)
            )
    sorted_tables = [rows_of(sorted_ref, SORTED_ROWS * channel) for channel in range(channels)]
    first_tables = [lambda row, at=at: at(8 * row) for at in tables]
    pair_tables = [lambda row, at=at: at((row >> 1) * 8 + (row & 1) + 1) for at in tables]
    own = table_picks(first_tables, 8, own_ref[...])
    for half in range(2):
        index = end_ref[8 * half : 8 * half + 8, :]
        loose = table_picks(sorted_tables, SORTED_ROWS, index & 8191)
        paired = table_picks(pair_tables, NODE_ROWS, pair_ref[8 * half : 8 * half + 8, :])
        for channel in range(channels):
            best = jnp.maximum(jnp.where(index < 8192, loose[channel], 0.0), paired[channel])
            if half == 0:
                best = jnp.maximum(best, own[channel])
            base = NODE_ROWS * channel + 8 * half
            out_ref[base : base + 8, :] = best


def node_picks(table_ref, channels, conn_ref, chunk):
    tables = [rows_of(table_ref, NODE_ROWS * channel) for channel in range(channels)]
    return table_picks(tables, NODE_ROWS, conn_ref[8 * chunk : 8 * chunk + 8, :])


def bf16_parts(values, count):
    parts = []
    for _ in range(count):
        part = values.astype(jnp.bfloat16).astype(F32)
        parts.append(part)
        values = values - part
    return parts


def scatter_sums(term_ref, channels, conn_ref, out_ref):
    width = 8 * LANES
    row_ids = lax.broadcasted_iota(I32, (NODE_ROWS, width), 0).astype(F32)
    lane_ids = lax.broadcasted_iota(I32, (LANES, width), 0).astype(F32)
    total = jnp.zeros((channels * PARTS * NODE_ROWS, LANES), F32)
    for chunk in range(CHUNKS):
        ids = conn_ref[8 * chunk : 8 * chunk + 8, :]
        in_row = one_line((ids >> 7).astype(F32)) == row_ids
        in_lane = one_line((ids & (LANES - 1)).astype(F32)) == lane_ids
        left = []
        for channel in range(channels):
            base = ITEM_ROWS * channel + 8 * chunk
            for part in bf16_parts(one_line(term_ref[base : base + 8, :]), PARTS):
                left.append(jnp.where(in_row, part, 0.0).astype(jnp.bfloat16))
        total = total + lax.dot_general(
            jnp.concatenate(left, axis=0),
            jnp.where(in_lane, 1.0, 0.0).astype(jnp.bfloat16),
            (((1,), (1,)), ((), ())),
            preferred_element_type=F32,
        )
    for channel in range(channels):
        base = PARTS * NODE_ROWS * channel
        out = total[base : base + NODE_ROWS]
        for part in range(1, PARTS):
            out = out + total[base + part * NODE_ROWS : base + (part + 1) * NODE_ROWS]
        out_ref[NODE_ROWS * channel : NODE_ROWS * (channel + 1), :] = out


def row_maxima(blocks_ref, picked, at, max_ref):
    for r in range(STRAINS):
        sized = [jnp.abs(blocks_ref[0, 0, r, 8 * c : 8 * c + 8, at]) for c in range(3)]
        for k, scales in enumerate(picked):
            whole = sized[0] * scales[0]
            for c in range(1, 3):
                whole = jnp.maximum(whole, sized[c] * scales[c])
            max_ref[STRAINS * k + r : STRAINS * k + r + 1, at] = jnp.max(whole, axis=0, keepdims=True)


def column_maxima(blocks_ref, row_ref, term_ref, first_channel):
    for chunk in range(CHUNKS):
        at = slice(chunk * LANES, (chunk + 1) * LANES)
        best = [jnp.zeros((8, LANES), F32)] * 3
        for r in range(STRAINS):
            row = 1.0 if row_ref is None else row_ref[r : r + 1, at]
            for c in range(3):
                size = jnp.abs(blocks_ref[0, 0, r, 8 * c : 8 * c + 8, at]) * row
                best[c] = jnp.maximum(best[c], size)
        for c in range(3):
            base = ITEM_ROWS * (first_channel + c) + 8 * chunk
            term_ref[base : base + 8, :] = best[c]


def apply_blocks(blocks_ref, table_ref, sets, conn_ref, strain_ref):
    for chunk in range(CHUNKS):
        values = node_picks(table_ref, 3 * sets, conn_ref, chunk)
        at = slice(chunk * LANES, (chunk + 1) * LANES)
        for r in range(STRAINS):
            parts = [blocks_ref[0, 0, r, 8 * c : 8 * c + 8, at] for c in range(3)]
            for k in range(sets):
                mine = values[3 * k : 3 * k + 3]
                total = parts[0] * mine[0] + parts[1] * mine[1] + parts[2] * mine[2]
                strain_ref[STRAINS * k + r : STRAINS * k + r + 1, at] = jnp.sum(
                    total, axis=0, keepdims=True
                )


def apply_transpose(blocks_ref, strain_ref, sets, term_ref):
    for chunk in range(CHUNKS):
        at = slice(chunk * LANES, (chunk + 1) * LANES)
        totals = [jnp.zeros((8, LANES), F32)] * (3 * sets)
        for r in range(STRAINS):
            parts = [blocks_ref[0, 0, r, 8 * c : 8 * c + 8, at] for c in range(3)]
            for k in range(sets):
                strain = strain_ref[STRAINS * k + r : STRAINS * k + r + 1, at]
                for c in range(3):
                    totals[3 * k + c] = totals[3 * k + c] + parts[c] * strain
        for channel in range(3 * sets):
            row = ITEM_ROWS * channel + 8 * chunk
            term_ref[row : row + 8, :] = totals[channel]


def even_places():
    return lax.axis_index("sector") % 2 == 0, lax.axis_index("band") % 2 == 0


def side_rows(part_ref, side, channel, length=2):
    base = NODE_ROWS * channel + 2 * side
    return part_ref[base : base + length, :]


def pack(part_ref, channels, packet_refs):
    even_sector, even_band = even_places()
    for slot, (even, low, high) in enumerate(
        ((even_sector, 1, 0), (even_band, 3, 2), (even_sector, 0, 1), (even_band, 2, 3))
    ):
        for channel in range(channels):
            for part in range(2):
                packet_refs[slot][4 * channel + 2 * part : 4 * channel + 2 * part + 2, :] = jnp.where(
                    even,
                    side_rows(part_ref, high + 4 * part, channel),
                    side_rows(part_ref, low + 4 * part, channel),
                )


def by_side(arrived_refs):
    even_sector, even_band = even_places()
    odd_cycle, odd_band, even_cycle, even_pair = [ref[...] for ref in arrived_refs]
    below, above = live_sides()
    return [
        jnp.where(even_sector, odd_cycle, even_cycle),
        jnp.where(even_sector, even_cycle, odd_cycle),
        jnp.where(below, jnp.where(even_band, odd_band, even_pair), 0.0),
        jnp.where(above, jnp.where(even_band, even_pair, odd_band), 0.0),
    ]


def live_sides():
    band = lax.axis_index("band")
    return [band > 0, band < lax.axis_size("band") - 1]


def unpack(part_ref, channels, arrived, merge, out_ref):
    for side in range(SIDES):
        for channel in range(channels):
            base = NODE_ROWS * channel + 2 * side
            theirs = arrived[side][4 * channel : 4 * channel + 4]
            out_ref[base : base + 2, :] = merge(part_ref[base : base + 2, :], theirs[2:4])
            out_ref[base + 8 : base + 10, :] = merge(part_ref[base + 8 : base + 10, :], theirs[0:2])


def rescale(scale, peak):
    peak = scale * peak
    seen = peak > 0.0
    return jnp.where(seen, scale / jnp.sqrt(jnp.where(seen, peak, 1.0)), 0.0)


def project_rows(ref):
    def every_third(start):
        return jnp.concatenate([ref[r : r + 1, :] for r in range(start, STRAINS, 3)], axis=0)

    top, first, second = [every_third(start) for start in range(3)]
    norm = jnp.sqrt(first * first + second * second)
    inside = norm <= top
    middle = norm > jnp.abs(top)
    factor = 0.5 * (1.0 + top / jnp.where(middle, norm, 1.0))
    gain = jnp.where(inside, 1.0, jnp.where(middle, factor, 0.0))
    top = jnp.where(inside, top, jnp.where(middle, factor * norm, 0.0))
    for start, values in enumerate((top, gain * first, gain * second)):
        for cone in range(4):
            ref[3 * cone + start : 3 * cone + start + 1, :] = values[cone : cone + 1, :]


def start_kernel(blocks_at, ids_at, send_at, *rest):
    conn_out, plan, (inverse_out, send_out), rest = rest[0], rest[1:6], rest[6:8], rest[8:]
    (row_out, part_out), packets, rest = rest[:2], rest[2:6], rest[6:]
    blocks_ref, ids_ref, send_ref, keys, term, items, peaks, semaphores = rest
    pairs = ((ids_at, ids_ref), (send_at, send_ref), (blocks_at, blocks_ref))
    copies = [
        pltpu.make_async_copy(source, target, semaphores.at[k])
        for k, (source, target) in enumerate(pairs)
    ]
    for copy in copies:
        copy.start()
    copies[0].wait()
    copies[1].wait()
    copies[2].wait()
    make_plan(ids_ref, send_ref, conn_out, *plan, inverse_out, send_out, keys)
    below, above = [live.astype(F32) for live in live_sides()]
    for chunk in range(CHUNKS):
        at = slice(chunk * LANES, (chunk + 1) * LANES)
        ids = ids_ref[0, 0, :, at]
        scale = jnp.where(ids < 1536, 1.0, jnp.where(ids < 1792, below, above))
        row_maxima(blocks_ref, [[scale] * 3], at, peaks)
    row_out[...] = 1.0 / jnp.sqrt(peaks[...])
    column_maxima(blocks_ref, None, term, 0)
    column_maxima(blocks_ref, row_out, term, 3)
    scatter_maxima(term, 6, plan, items, part_out)
    pack(part_out, 6, packets)


def sweep_kernel(
    blocks_ref, conn_ref, row_ref, part_ref, loads_ref, send_ref, *rest
):
    plan, rest = rest[:5], rest[5:]
    arrived, rest = by_side(rest[:4]), rest[4:]
    row_out, scale_out, part_out, loads_out, rest = rest[0], rest[1], rest[2], rest[3], rest[4:]
    packets, (term, items, peaks, merged, second_row) = rest[:4], rest[4:]
    unpack(part_ref, 6, arrived, jnp.maximum, merged)
    row = lax.broadcasted_iota(I32, (NODE_ROWS, LANES), 0)
    below, above = [live.astype(F32) for live in live_sides()]
    start = jnp.where(row < 12, 1.0, jnp.where(row < 14, below, above))
    for c in range(3):
        first = rescale(start, merged[NODE_ROWS * c : NODE_ROWS * (c + 1), :])
        later = NODE_ROWS * (c + 3)
        second = rescale(first, merged[later : later + NODE_ROWS, :])
        merged[NODE_ROWS * c : NODE_ROWS * (c + 1), :] = first
        merged[later : later + NODE_ROWS, :] = second
        scale_out[NODE_ROWS * c : NODE_ROWS * (c + 1), :] = second
    for chunk in range(CHUNKS):
        at = slice(chunk * LANES, (chunk + 1) * LANES)
        scales = node_picks(merged, 6, conn_ref, chunk)
        row_maxima(blocks_ref, [scales[0:3], scales[3:6]], at, peaks)
    first_row = row_ref[...]
    second_row[...] = first_row / jnp.sqrt(first_row * peaks[0:STRAINS, :])
    row_out[...] = second_row[...] / jnp.sqrt(second_row[...] * peaks[STRAINS : 2 * STRAINS, :])
    column_maxima(blocks_ref, second_row, term, 0)
    scatter_maxima(term, 3, plan, items, part_out)
    pack(part_out, 3, packets)
    tables = [rows_of(loads_ref, 8 * c) for c in range(3)]
    for c, values in enumerate(table_picks(tables, 8, send_ref[...])):
        loads_out[8 * c : 8 * c + 8, :] = values
    even_sector, even_band = even_places()
    for slot, (even, low, high) in enumerate(
        ((even_sector, 1, 0), (even_band, 3, 2), (even_sector, 0, 1), (even_band, 2, 3))
    ):
        for c in range(3):
            packets[slot][12 + 2 * c : 14 + 2 * c, :] = jnp.where(
                even,
                loads_out[8 * c + 2 * high : 8 * c + 2 * high + 2, :],
                loads_out[8 * c + 2 * low : 8 * c + 2 * low + 2, :],
            )


def target_kernel(
    blocks_ref,
    conn_ref,
    row_ref,
    scale_ref,
    part_ref,
    loads_ref,
    *rest,
):
    arrived, rest = by_side(rest[:4]), rest[4:]
    scale_out, strain_out, part_out, rest = rest[0], rest[1], rest[2], rest[3:]
    packets, (term, table, strain, cones) = rest[:4], rest[4:]
    unpack(part_ref, 3, arrived, jnp.maximum, table)
    scale = rescale(scale_ref[...], table[...])
    scale_out[...] = scale
    for c in range(3):
        table[NODE_ROWS * c : NODE_ROWS * c + 8, :] = loads_ref[8 * c : 8 * c + 8, :]
        for side in range(SIDES):
            base = NODE_ROWS * c + 8 + 2 * side
            table[base : base + 2, :] = arrived[side][12 + 2 * c : 14 + 2 * c]
    table[...] = scale * (scale * table[...])
    apply_blocks(blocks_ref, table, 1, conn_ref, strain)
    row = row_ref[...]
    image = row * strain[0:STRAINS, :]
    cones[...] = image
    project_rows(cones)
    strain[0:STRAINS, :] = row * image
    strain[STRAINS : 2 * STRAINS, :] = row * cones[...]
    strain_out[...] = 3.0 * image + 2.0 * cones[...]
    apply_transpose(blocks_ref, strain, 2, term)
    scatter_sums(term, 6, conn_ref, part_out)
    part_out[0:48, :] = part_out[0:48, :] * scale
    part_out[48:96, :] = part_out[48:96, :] * scale
    pack(part_out, 6, packets)


def second_kernel(
    blocks_ref, conn_ref, row_ref, scale_ref, part_ref, *rest
):
    arrived, rest = rest[:4], rest[4:]
    joint_out, strain_out, part_out, rest = rest[0], rest[1], rest[2], rest[3:]
    packets, (term, table, strain) = rest[:4], rest[4:]
    arrived = by_side(arrived)
    unpack(part_ref, 6, arrived, jnp.add, table)
    joint_out[...] = table[48:96, :]
    scale = scale_ref[...]
    table[0:48, :] = scale * table[0:48, :]
    table[48:96, :] = scale * table[48:96, :]
    apply_blocks(blocks_ref, table, 2, conn_ref, strain)
    row = row_ref[...]
    strain_out[...] = row * strain[STRAINS : 2 * STRAINS, :]
    strain[0:STRAINS, :] = row * (row * strain[0:STRAINS, :])
    apply_transpose(blocks_ref, strain, 1, term)
    scatter_sums(term, 3, conn_ref, part_out)
    part_out[...] = part_out[...] * scale
    pack(part_out, 3, packets)


def own_square(ref):
    total = jnp.zeros((8, LANES), F32)
    for c in range(3):
        mine = ref[NODE_ROWS * c : NODE_ROWS * c + 8, :]
        total = total + mine * mine
    return jnp.sum(total, axis=0, keepdims=True)


def third_kernel(
    blocks_ref, conn_ref, row_ref, scale_ref, part_ref, *rest
):
    arrived, rest = rest[:4], rest[4:]
    norm_out, part_out, right_out, above_out, term, table, strain = rest
    unpack(part_ref, 3, by_side(arrived), jnp.add, table)
    norm_out[...] = own_square(table)
    scale = scale_ref[...]
    table[...] = scale * table[...]
    apply_blocks(blocks_ref, table, 1, conn_ref, strain)
    row = row_ref[...]
    strain[...] = row * (row * strain[...])
    apply_transpose(blocks_ref, strain, 1, term)
    scatter_sums(term, 3, conn_ref, part_out)
    part_out[...] = part_out[...] * scale
    for packet, side in ((right_out, 1), (above_out, 3)):
        for channel in range(3):
            packet[4 * channel : 4 * channel + 2, :] = side_rows(part_out, side, channel)
            packet[4 * channel + 2 : 4 * channel + 4, :] = side_rows(part_out, side + 4, channel)


def norm_kernel(part_ref, norm_ref, left_ref, below_ref, sums_out):
    below, above = live_sides()
    squares = jnp.zeros((2, LANES), F32)
    for channel in range(3):
        for side, arrived, live in ((0, left_ref, True), (2, below_ref, below)):
            theirs = arrived[4 * channel : 4 * channel + 4, :]
            theirs = jnp.where(live, theirs, 0.0)
            own = side_rows(part_ref, side, channel) + theirs[2:4]
            copy = side_rows(part_ref, side + 4, channel) + theirs[0:2]
            squares = squares + own * own + copy * copy
        alone = jnp.where(above, 0.0, side_rows(part_ref, 3, channel))
        squares = squares + alone * alone
    last = jnp.sum(squares, axis=0, keepdims=True)
    first = norm_ref[...]
    lane = lax.broadcasted_iota(I32, (1, LANES), 1)
    line = jnp.where(lane < 64, first + pltpu.roll(first, 64, 1), last + pltpu.roll(last, 64, 1))
    sums_out[...] = jnp.broadcast_to(line, sums_out.shape)


def lines_kernel(scale_ref, loads_ref, joint_ref, inverse_ref, velocity_out, lines):
    for c in range(3):
        base = NODE_ROWS * c
        scale = scale_ref[base : base + 8, :]
        lines[8 * c : 8 * c + 8, :] = scale * (scale * loads_ref[8 * c : 8 * c + 8, :])
        lines[24 + 8 * c : 32 + 8 * c, :] = scale * joint_ref[base : base + 8, :]
    tables = [rows_of(lines, 8 * channel) for channel in range(6)]
    for channel, values in enumerate(table_picks(tables, 8, inverse_ref[...])):
        velocity_out[8 * channel : 8 * channel + 8, :] = values


def final_kernel(
    sums_ref, step_ref, velocity_ref, base_ref, joint_ref, row_ref, velocity_out, multiplier_out, *rest
):
    velocity, cones, flat, semaphores = rest
    sums = jnp.sum(sums_ref[...], axis=0, keepdims=True)
    lane = lax.broadcasted_iota(I32, (1, LANES), 1)
    before = jnp.sum(jnp.where(lane < 64, sums, 0.0), axis=1, keepdims=True)
    after = jnp.sum(jnp.where(lane < 64, 0.0, sums), axis=1, keepdims=True)
    largest = jnp.sqrt(after + epsilon) / jnp.sqrt(before + epsilon)
    step = step_ref[0] / jnp.sqrt(largest)
    square = step * step
    velocity[...] = (2.0 * step) * (square * velocity_ref[24:48, :] - velocity_ref[0:24, :])
    first = pltpu.make_async_copy(velocity, velocity_out, semaphores.at[0])
    first.start()
    cones[...] = square * (base_ref[...] - (4.0 * square) * joint_ref[...])
    project_rows(cones)
    cones[...] = row_ref[...] * cones[...]
    for r in range(STRAINS):
        for chunk in range(CHUNKS):
            flat[8 * r + chunk : 8 * r + chunk + 1, :] = cones[
                r : r + 1, chunk * LANES : (chunk + 1) * LANES
            ]
    second = pltpu.make_async_copy(flat, multiplier_out, semaphores.at[1])
    second.start()
    first.wait()
    second.wait()


def call(body, out_shapes, scratch, *arrays, smem=(), outside=(), outside_results=False, work=0, limit=24 * 1024):
    def space(i):
        return pltpu.SMEM if i in smem else pltpu.HBM if i in outside else pltpu.VMEM

    result = pltpu.HBM if outside_results else pltpu.VMEM
    return pl.pallas_call(
        body,
        out_shape=[jax.ShapeDtypeStruct(shape, kind) for shape, kind in out_shapes],
        in_specs=[pl.BlockSpec(memory_space=space(i)) for i in range(len(arrays))],
        out_specs=[pl.BlockSpec(memory_space=result) for _ in out_shapes],
        scratch_shapes=[
            entry if not isinstance(entry, tuple) else pltpu.VMEM(*entry) for entry in scratch
        ],
        cost_estimate=pl.CostEstimate(flops=work, bytes_accessed=work // 256, transcendentals=0),
        compiler_params=pltpu.CompilerParams(vmem_limit_bytes=limit * 1024),
    )(*arrays)


def swap_pairs(axis, odd):
    count = lax.axis_size(axis)
    return [(i, (((i - odd) ^ 1) + odd) % count) for i in range(count)]


PAIRS = (("sector", 1), ("band", 1), ("sector", 0), ("band", 0))


def exchange(packets):
    return [
        lax.ppermute(packet, axis, swap_pairs(axis, odd)) for packet, (axis, odd) in zip(packets, PAIRS)
    ]


def shift_up(packet, axis):
    count = lax.axis_size(axis)
    return lax.ppermute(packet, axis, [(i, (i + 1) % count) for i in range(count)])


def per_device(blocks, connectivity, send_lists, nodal_loads, step_scale):
    packet = [((12, LANES), F32)] * 4
    nodes = ((48, LANES), F32)
    rows = ((STRAINS, 1024), F32)
    items = ((3 * ITEM_ROWS, LANES), F32)
    twice = ((6 * ITEM_ROWS, LANES), F32)
    ids = ((64, LANES), I32)
    few = ((8, LANES), I32)
    conn, *rest = call(
        start_kernel,
        [ids, ((SORTED_ROWS, LANES), I32), few, ((16, LANES), I32), few, ((16, LANES), I32), few, few]
        + [rows, ((96, LANES), F32)]
        + [((24, LANES), F32)] * 4,
        [
            ((1, 1, STRAINS, 24, 1024), F32),
            ((1, 1, 8, 1024), I32),
            ((1, 1, SIDES, 256), I32),
            ids,
            twice,
            ((6 * SORTED_ROWS, LANES), F32),
            rows,
            pltpu.SemaphoreType.DMA((3,)),
        ],
        blocks,
        connectivity,
        send_lists,
        outside=(0, 1, 2),
        limit=LIMIT,
        work=12_000_000_000,
    )
    plan, (inverse, send, row, part), packets = rest[:5], rest[5:9], rest[9:]
    row, scale, part, loads, *packets = call(
        sweep_kernel,
        [rows, nodes, nodes, ((24, LANES), F32)] + [((18, LANES), F32)] * 4,
        [items, ((3 * SORTED_ROWS, LANES), F32), ((2 * STRAINS, 1024), F32), ((96, LANES), F32), rows],
        blocks,
        conn,
        row,
        part,
        nodal_loads.reshape(24, LANES),
        send,
        *plan,
        *exchange(packets),
    )
    scale, base, part, *packets = call(
        target_kernel,
        [nodes, rows, ((96, LANES), F32)] + [((24, LANES), F32)] * 4,
        [twice, nodes, ((2 * STRAINS, 1024), F32), rows],
        blocks,
        conn,
        row,
        scale,
        part,
        loads,
        *exchange(packets),
    )
    joint, image, part, *packets = call(
        second_kernel,
        [nodes, rows, nodes] + packet,
        [items, ((96, LANES), F32), ((2 * STRAINS, 1024), F32)],
        blocks,
        conn,
        row,
        scale,
        part,
        *exchange(packets),
    )
    norm, part, right, above = call(
        third_kernel,
        [((1, LANES), F32), nodes] + packet[:2],
        [items, nodes, rows],
        blocks,
        conn,
        row,
        scale,
        part,
        *exchange(packets),
    )
    count = lax.axis_size("band") * lax.axis_size("sector")
    (sums,) = call(
        norm_kernel,
        [((count, LANES), F32)],
        [],
        part,
        norm,
        shift_up(right, "sector"),
        shift_up(above, "band"),
    )
    (lines,) = call(
        lines_kernel,
        [((48, LANES), F32)],
        [nodes],
        scale,
        loads,
        joint,
        inverse,
        work=600_000_000,
    )
    sums = lax.all_to_all(sums, AXES, 0, 0, tiled=True)
    velocities, multipliers = call(
        final_kernel,
        [((24, LANES), F32), ((96, LANES), F32)],
        [((24, LANES), F32), rows, ((96, LANES), F32), pltpu.SemaphoreType.DMA((2,))],
        sums,
        step_scale,
        lines,
        base,
        image,
        row,
        smem=(1,),
        outside_results=True,
    )
    return velocities.reshape(1, 1, 3, 1024), multipliers.reshape(1, 1, STRAINS, 1024)


def solution(mesh):
    in_specs = (
        P("band", "sector", None, None, None),
        P("band", "sector", None, None),
        P("band", "sector", None, None),
        P("band", "sector", None, None),
        P(),
    )
    out_specs = (P("band", "sector", None, None), P("band", "sector", None, None))
    return jax.shard_map(
        per_device, mesh=mesh, in_specs=in_specs, out_specs=out_specs, check_vma=False
    )
```

```python
import functools

import jax
import jax.numpy as jnp
from jax import lax
from jax.experimental import pallas as pl
from jax.experimental.pallas import tpu as pltpu
from jax.sharding import PartitionSpec as P

LANES = 128
CHUNKS = 8
STRAINS = 12
NODE_ROWS = 16
ITEM_ROWS = 64
SIDES = 4
PARTS = 2
BESIDE = 1_000_000_000
LIMIT = 54000
AXES = ("band", "sector")
epsilon = 1e-06
F32 = jnp.float32
I32 = jnp.int32


def tile_iota(axis):
    return lax.broadcasted_iota(I32, (8, LANES), axis)


def pick(rows, index, axis):
    dims = lax.GatherDimensionNumbers(
        offset_dims=(),
        collapsed_slice_dims=(axis,),
        start_index_map=(axis,),
        operand_batching_dims=(1 - axis,),
        start_indices_batching_dims=(1 - axis,),
    )
    return lax.gather(
        rows,
        index[..., None],
        dims,
        slice_sizes=(1, 1),
        mode=lax.GatherScatterMode.PROMISE_IN_BOUNDS,
    )


def table_picks(row_getters, rows, flat):
    rows = tuple(range(rows)) if isinstance(rows, int) else rows
    lanes = flat & (LANES - 1)
    levels = rows[-1].bit_length()
    bits = [(flat & (LANES << level)) != 0 for level in range(levels)]

    def descend(row_at, level, base):
        if level < 0:
            return pick(jnp.broadcast_to(row_at(base), (8, LANES)), lanes, 1) if base in rows else None
        low = descend(row_at, level - 1, base)
        high = descend(row_at, level - 1, base + (1 << level))
        if low is None or high is None:
            return high if low is None else low
        return jnp.where(bits[level], high, low)

    return [descend(row_at, levels - 1, 0) for row_at in row_getters]


def rows_of(ref, offset):
    return lambda row: ref[offset + row : offset + row + 1, :]


def group_shift(values, distance):
    if distance >= 8:
        return pltpu.roll(values, distance // 8, 1)
    turned = pltpu.roll(values, distance, 0)
    return jnp.where(tile_iota(0) < distance, pltpu.roll(turned, 1, 1), turned)


SCAN_STEPS = tuple(1 << step for step in range(10))
RUNS = 5
SORTED_ROWS = 8 * RUNS
LOOSE_ROWS = tuple(row for row in range(ITEM_ROWS) if row % 8 >= 3)


def sort_items(keys):
    sub, lane = tile_iota(0), tile_iota(1)
    size = 2
    while size <= 8192:
        half = size // 2
        while half >= 1:
            new = list(keys)

            def rising(register):
                if size < 8:
                    return (register & size) == 0
                if size < 64:
                    return (sub & (size // 8)) == 0
                if size < 8192:
                    return (lane & (size // 64)) == 0
                return True

            for register in range(8):
                up = rising(register)
                if half < 8:
                    other = register ^ half
                    if other < register:
                        continue
                    low = jnp.minimum(keys[register], keys[other])
                    high = jnp.maximum(keys[register], keys[other])
                    if isinstance(up, bool):
                        new[register], new[other] = (low, high) if up else (high, low)
                    else:
                        new[register] = jnp.where(up, low, high)
                        new[other] = jnp.where(up, high, low)
                    continue
                if half < 64:
                    step = half // 8
                    partner = pick(keys[register], sub ^ step, 0)
                    first = (sub & step) == 0
                else:
                    step = half // 64
                    partner = pick(keys[register], lane ^ step, 1)
                    first = (lane & step) == 0
                low = jnp.minimum(keys[register], partner)
                high = jnp.maximum(keys[register], partner)
                if isinstance(up, bool):
                    keep_low = first if up else jnp.logical_not(first)
                else:
                    keep_low = first == up
                new[register] = jnp.where(keep_low, low, high)
            keys = new
            half //= 2
        size *= 2
    return keys


def one_line(rows):
    return jnp.concatenate([rows[k : k + 1] for k in range(rows.shape[0])], axis=1)


def inverse_of(line, code, rows):
    width = line.shape[1]
    in_row = (line >> 7) == lax.broadcasted_iota(I32, (rows, width), 0)
    left = jnp.concatenate(
        [
            jnp.where(in_row, (code >> 7).astype(F32), 0.0),
            jnp.where(in_row, (code & (LANES - 1)).astype(F32), 0.0),
        ],
        axis=0,
    ).astype(jnp.bfloat16)
    in_lane = (line & (LANES - 1)) == lax.broadcasted_iota(I32, (LANES, width), 0)
    right = jnp.where(in_lane, 1.0, 0.0).astype(jnp.bfloat16)
    found = lax.dot_general(left, right, (((1,), (1,)), ((), ())), preferred_element_type=F32)
    return (found[0:rows] * 128.0 + found[rows : 2 * rows]).astype(I32)


def relabel(conn_ref, send_ref, conn_out, own_out, pair_out, inverse_out, send_out):
    for half in range(8):
        start = (half % 2) * LANES
        send_out[half : half + 1, :] = send_ref[0, 0, half // 2 : half // 2 + 1, start : start + LANES]
    place = lax.broadcasted_iota(I32, (1, 8 * LANES), 1)
    inverse_out[...] = inverse_of(one_line(send_out[...]), place, 8)
    sub, lane = tile_iota(0), tile_iota(1)
    keys = []
    for chunk in range(CHUNKS):
        ids = conn_ref[0, 0, :, chunk * LANES : (chunk + 1) * LANES]
        (label,) = table_picks([rows_of(inverse_out, 0)], 8, ids & 1023)
        ids = jnp.where(ids < 1024, label, ids)
        conn_out[8 * chunk : 8 * chunk + 8, :] = ids
        item = ids * 8192 + (chunk * 1024 + sub * LANES + lane)
        keys.append(jnp.where(sub < 3, 2048 * 8192, item))
    first_line = jnp.concatenate([conn_out[8 * chunk : 8 * chunk + 1, :] for chunk in range(CHUNKS)], axis=1)
    own_out[...] = inverse_of(first_line, place, 8)
    pair_line = jnp.concatenate(
        [conn_out[8 * chunk + k : 8 * chunk + k + 1, :] for chunk in range(CHUNKS) for k in (1, 2)], axis=1
    )
    pair_out[...] = inverse_of(pair_line, lax.broadcasted_iota(I32, (1, 16 * LANES), 1), NODE_ROWS)
    return keys


def make_order(keys, key_out, scan_out, end_out, keys_ref):
    sub, lane = tile_iota(0), tile_iota(1)
    keys = sort_items(keys)
    for register in range(8):
        keys_ref[8 * register : 8 * register + 8, :] = keys[register]
    group = lane * 8 + sub
    runs = []
    for register in range(RUNS):
        place = group * RUNS + register
        row = (place & 7) * 8 + ((place >> 3) & 7)
        (moved,) = table_picks([rows_of(keys_ref, 0)], ITEM_ROWS, row * LANES + (place >> 6))
        runs.append(moved)
        key_out[8 * register : 8 * register + 8, :] = moved
    first, last = runs[0] >> 13, runs[-1] >> 13
    scan = jnp.zeros((8, LANES), I32)
    for step, distance in enumerate(SCAN_STEPS):
        same = (group >= distance) & (group_shift(last, distance) == last)
        scan = jnp.where(same, scan | (1 << step), scan)
    same = (group >= 1) & (group_shift(last, 1) == first)
    scan_out[...] = jnp.where(same, scan | (1 << len(SCAN_STEPS)), scan)
    lane_last = jnp.broadcast_to(keys_ref[63:64, :] >> 13, (8, LANES))
    for half in range(2):
        node = (half * 8 + sub) * LANES + lane
        column = jnp.zeros((8, LANES), I32)
        for step in (64, 32, 16, 8, 4, 2, 1):
            seen = pick(lane_last, column + (step - 1), 1)
            column = jnp.where(seen <= node, column + step, column)
        count = column * 64
        before = pick(lane_last, jnp.maximum(column - 1, 0), 1)
        named = (column > 0) & (before == node)
        for row in range(ITEM_ROWS):
            seen = pick(jnp.broadcast_to(keys_ref[row : row + 1, :], (8, LANES)), column, 1) >> 13
            count = count + jnp.where(seen <= node, 1, 0)
            named = named | (seen == node)
        place = jnp.maximum(count - 1, 0)
        place = jnp.where(named, place, 0)
        share = (place * 52429) >> 18
        row = (place - share * RUNS) * 8 + (share & 7)
        end = row * LANES + (share >> 3)
        end_out[8 * half : 8 * half + 8, :] = jnp.where(named, end, 8192)


def scatter_maxima(term_ref, channels, plan, sorted_ref, out_ref):
    key_ref, scan_ref, end_ref, own_ref, pair_ref = plan
    tables = [rows_of(term_ref, ITEM_ROWS * channel) for channel in range(channels)]
    nodes = []
    for register in range(RUNS):
        key = key_ref[8 * register : 8 * register + 8, :]
        nodes.append(key >> 13)
        for channel, values in enumerate(table_picks(tables, LOOSE_ROWS, key & 8191)):
            base = SORTED_ROWS * channel + 8 * register
            sorted_ref[base : base + 8, :] = values
    scan = scan_ref[...]
    follows = [(scan & (1 << step)) != 0 for step in range(len(SCAN_STEPS) + 1)]
    for channel in range(channels):
        base = SORTED_ROWS * channel
        runs = [sorted_ref[base : base + 8, :]]
        for register in range(1, RUNS):
            same = nodes[register] == nodes[register - 1]
            here = sorted_ref[base + 8 * register : base + 8 * register + 8, :]
            runs.append(jnp.maximum(here, jnp.where(same, runs[-1], 0.0)))
        total = runs[-1]
        for step, distance in enumerate(SCAN_STEPS):
            total = jnp.maximum(total, jnp.where(follows[step], group_shift(total, distance), 0.0))
        carry = jnp.where(follows[-1], group_shift(total, 1), 0.0)
        for register in range(RUNS):
            open_run = nodes[register] == nodes[0]
            sorted_ref[base + 8 * register : base + 8 * register + 8, :] = jnp.maximum(
                runs[register], jnp.where(open_run, carry, 0.0)
            )
    sorted_tables = [rows_of(sorted_ref, SORTED_ROWS * channel) for channel in range(channels)]
    first_tables = [lambda row, at=at: at(8 * row) for at in tables]
    pair_tables = [lambda row, at=at: at((row >> 1) * 8 + (row & 1) + 1) for at in tables]
    own = table_picks(first_tables, 8, own_ref[...])
    for half in range(2):
        index = end_ref[8 * half : 8 * half + 8, :]
        loose = table_picks(sorted_tables, SORTED_ROWS, index & 8191)
        paired = table_picks(pair_tables, NODE_ROWS, pair_ref[8 * half : 8 * half + 8, :])
        for channel in range(channels):
            best = jnp.maximum(jnp.where(index < 8192, loose[channel], 0.0), paired[channel])
            if half == 0:
                best = jnp.maximum(best, own[channel])
            base = NODE_ROWS * channel + 8 * half
            out_ref[base : base + 8, :] = best


def node_picks(table_ref, channels, conn_ref, chunk):
    tables = [rows_of(table_ref, NODE_ROWS * channel) for channel in range(channels)]
    return table_picks(tables, NODE_ROWS, conn_ref[8 * chunk : 8 * chunk + 8, :])


def bf16_parts(values, count):
    parts = []
    for _ in range(count):
        part = values.astype(jnp.bfloat16).astype(F32)
        parts.append(part)
        values = values - part
    return parts


def scatter_sums(term_ref, channels, conn_ref, out_ref):
    width = 8 * LANES
    row_ids = lax.broadcasted_iota(I32, (NODE_ROWS, width), 0).astype(F32)
    lane_ids = lax.broadcasted_iota(I32, (LANES, width), 0).astype(F32)
    total = jnp.zeros((channels * PARTS * NODE_ROWS, LANES), F32)
    for chunk in range(CHUNKS):
        ids = conn_ref[8 * chunk : 8 * chunk + 8, :]
        in_row = one_line((ids >> 7).astype(F32)) == row_ids
        in_lane = one_line((ids & (LANES - 1)).astype(F32)) == lane_ids
        left = []
        for channel in range(channels):
            base = ITEM_ROWS * channel + 8 * chunk
            for part in bf16_parts(one_line(term_ref[base : base + 8, :]), PARTS):
                left.append(jnp.where(in_row, part, 0.0).astype(jnp.bfloat16))
        total = total + lax.dot_general(
            jnp.concatenate(left, axis=0),
            jnp.where(in_lane, 1.0, 0.0).astype(jnp.bfloat16),
            (((1,), (1,)), ((), ())),
            preferred_element_type=F32,
        )
    for channel in range(channels):
        base = PARTS * NODE_ROWS * channel
        out = total[base : base + NODE_ROWS]
        for part in range(1, PARTS):
            out = out + total[base + part * NODE_ROWS : base + (part + 1) * NODE_ROWS]
        out_ref[NODE_ROWS * channel : NODE_ROWS * (channel + 1), :] = out


def row_maxima(blocks_ref, picked, at, max_ref):
    for r in range(STRAINS):
        sized = [jnp.abs(blocks_ref[0, 0, r, 8 * c : 8 * c + 8, at]) for c in range(3)]
        for k, scales in enumerate(picked):
            whole = sized[0] * scales[0]
            for c in range(1, 3):
                whole = jnp.maximum(whole, sized[c] * scales[c])
            max_ref[STRAINS * k + r : STRAINS * k + r + 1, at] = jnp.max(whole, axis=0, keepdims=True)


def column_maxima(blocks_ref, row_ref, term_ref, first_channel):
    for chunk in range(CHUNKS):
        at = slice(chunk * LANES, (chunk + 1) * LANES)
        best = [jnp.zeros((8, LANES), F32)] * 3
        for r in range(STRAINS):
            row = 1.0 if row_ref is None else row_ref[r : r + 1, at]
            for c in range(3):
                size = jnp.abs(blocks_ref[0, 0, r, 8 * c : 8 * c + 8, at]) * row
                best[c] = jnp.maximum(best[c], size)
        for c in range(3):
            base = ITEM_ROWS * (first_channel + c) + 8 * chunk
            term_ref[base : base + 8, :] = best[c]


def apply_blocks(blocks_ref, table_ref, sets, conn_ref, strain_ref):
    for chunk in range(CHUNKS):
        values = node_picks(table_ref, 3 * sets, conn_ref, chunk)
        at = slice(chunk * LANES, (chunk + 1) * LANES)
        for r in range(STRAINS):
            parts = [blocks_ref[0, 0, r, 8 * c : 8 * c + 8, at] for c in range(3)]
            for k in range(sets):
                mine = values[3 * k : 3 * k + 3]
                total = parts[0] * mine[0] + parts[1] * mine[1] + parts[2] * mine[2]
                strain_ref[STRAINS * k + r : STRAINS * k + r + 1, at] = jnp.sum(
                    total, axis=0, keepdims=True
                )


def apply_transpose(blocks_ref, strain_ref, sets, term_ref):
    for chunk in range(CHUNKS):
        at = slice(chunk * LANES, (chunk + 1) * LANES)
        totals = [jnp.zeros((8, LANES), F32)] * (3 * sets)
        for r in range(STRAINS):
            parts = [blocks_ref[0, 0, r, 8 * c : 8 * c + 8, at] for c in range(3)]
            for k in range(sets):
                strain = strain_ref[STRAINS * k + r : STRAINS * k + r + 1, at]
                for c in range(3):
                    totals[3 * k + c] = totals[3 * k + c] + parts[c] * strain
        for channel in range(3 * sets):
            row = ITEM_ROWS * channel + 8 * chunk
            term_ref[row : row + 8, :] = totals[channel]


def even_places():
    return lax.axis_index("sector") % 2 == 0, lax.axis_index("band") % 2 == 0


def side_rows(part_ref, side, channel, length=2):
    base = NODE_ROWS * channel + 2 * side
    return part_ref[base : base + length, :]


def pack(part_ref, channels, packet_refs):
    even_sector, even_band = even_places()
    for slot, (even, low, high) in enumerate(
        ((even_sector, 1, 0), (even_band, 3, 2), (even_sector, 0, 1), (even_band, 2, 3))
    ):
        for channel in range(channels):
            for part in range(2):
                packet_refs[slot][4 * channel + 2 * part : 4 * channel + 2 * part + 2, :] = jnp.where(
                    even,
                    side_rows(part_ref, high + 4 * part, channel),
                    side_rows(part_ref, low + 4 * part, channel),
                )


def by_side(arrived_refs):
    even_sector, even_band = even_places()
    odd_cycle, odd_band, even_cycle, even_pair = [ref[...] for ref in arrived_refs]
    below, above = live_sides()
    return [
        jnp.where(even_sector, odd_cycle, even_cycle),
        jnp.where(even_sector, even_cycle, odd_cycle),
        jnp.where(below, jnp.where(even_band, odd_band, even_pair), 0.0),
        jnp.where(above, jnp.where(even_band, even_pair, odd_band), 0.0),
    ]


def live_sides():
    band = lax.axis_index("band")
    return [band > 0, band < lax.axis_size("band") - 1]


def unpack(part_ref, channels, arrived, merge, out_ref):
    for side in range(SIDES):
        for channel in range(channels):
            base = NODE_ROWS * channel + 2 * side
            theirs = arrived[side][4 * channel : 4 * channel + 4]
            out_ref[base : base + 2, :] = merge(part_ref[base : base + 2, :], theirs[2:4])
            out_ref[base + 8 : base + 10, :] = merge(part_ref[base + 8 : base + 10, :], theirs[0:2])


def rescale(scale, peak):
    peak = scale * peak
    seen = peak > 0.0
    return jnp.where(seen, scale / jnp.sqrt(jnp.where(seen, peak, 1.0)), 0.0)


def project_rows(ref):
    def every_third(start):
        return jnp.concatenate([ref[r : r + 1, :] for r in range(start, STRAINS, 3)], axis=0)

    top, first, second = [every_third(start) for start in range(3)]
    norm = jnp.sqrt(first * first + second * second)
    inside = norm <= top
    middle = norm > jnp.abs(top)
    factor = 0.5 * (1.0 + top / jnp.where(middle, norm, 1.0))
    gain = jnp.where(inside, 1.0, jnp.where(middle, factor, 0.0))
    top = jnp.where(inside, top, jnp.where(middle, factor * norm, 0.0))
    for start, values in enumerate((top, gain * first, gain * second)):
        for cone in range(4):
            ref[3 * cone + start : 3 * cone + start + 1, :] = values[cone : cone + 1, :]


def start_kernel(blocks_at, ids_at, send_at, *rest):
    conn_out, plan, (inverse_out, send_out), rest = rest[0], rest[1:6], rest[6:8], rest[8:]
    (row_out, part_out), packets, rest = rest[:2], rest[2:6], rest[6:]
    blocks_ref, ids_ref, send_ref, keys, term, items, peaks, semaphores = rest
    pairs = ((ids_at, ids_ref), (send_at, send_ref), (blocks_at, blocks_ref))
    copies = [
        pltpu.make_async_copy(source, target, semaphores.at[k])
        for k, (source, target) in enumerate(pairs)
    ]
    for copy in copies:
        copy.start()
    copies[0].wait()
    copies[1].wait()
    first_keys = relabel(ids_ref, send_ref, conn_out, *plan[3:], inverse_out, send_out)
    copies[2].wait()
    below, above = [live.astype(F32) for live in live_sides()]
    for chunk in range(CHUNKS):
        at = slice(chunk * LANES, (chunk + 1) * LANES)
        ids = ids_ref[0, 0, :, at]
        scale = jnp.where(ids < 1536, 1.0, jnp.where(ids < 1792, below, above))
        row_maxima(blocks_ref, [[scale] * 3], at, peaks)
    row_out[...] = 1.0 / jnp.sqrt(peaks[...])
    column_maxima(blocks_ref, None, term, 0)
    column_maxima(blocks_ref, row_out, term, 3)
    make_order(first_keys, *plan[:3], keys)
    scatter_maxima(term, 6, plan, items, part_out)
    pack(part_out, 6, packets)


def sweep_kernel(
    blocks_ref, conn_ref, row_ref, part_ref, loads_ref, send_ref, *rest
):
    plan, rest = rest[:5], rest[5:]
    arrived, rest = by_side(rest[:4]), rest[4:]
    row_out, scale_out, part_out, loads_out, rest = rest[0], rest[1], rest[2], rest[3], rest[4:]
    packets, (term, items, peaks, merged) = rest[:4], rest[4:]
    unpack(part_ref, 6, arrived, jnp.maximum, merged)
    row = lax.broadcasted_iota(I32, (NODE_ROWS, LANES), 0)
    below, above = [live.astype(F32) for live in live_sides()]
    start = jnp.where(row < 12, 1.0, jnp.where(row < 14, below, above))
    for c in range(3):
        first = rescale(start, merged[NODE_ROWS * c : NODE_ROWS * (c + 1), :])
        later = NODE_ROWS * (c + 3)
        second = rescale(first, merged[later : later + NODE_ROWS, :])
        merged[NODE_ROWS * c : NODE_ROWS * (c + 1), :] = first
        scale_out[NODE_ROWS * c : NODE_ROWS * (c + 1), :] = second
    for chunk in range(CHUNKS):
        at = slice(chunk * LANES, (chunk + 1) * LANES)
        row_maxima(blocks_ref, [node_picks(merged, 3, conn_ref, chunk)], at, peaks)
    row_out[...] = row_ref[...] / jnp.sqrt(row_ref[...] * peaks[...])
    column_maxima(blocks_ref, row_out, term, 0)
    scatter_maxima(term, 3, plan, items, part_out)
    pack(part_out, 3, packets)
    tables = [rows_of(loads_ref, 8 * c) for c in range(3)]
    for c, values in enumerate(table_picks(tables, 8, send_ref[...])):
        loads_out[8 * c : 8 * c + 8, :] = values
    even_sector, even_band = even_places()
    for slot, (even, low, high) in enumerate(
        ((even_sector, 1, 0), (even_band, 3, 2), (even_sector, 0, 1), (even_band, 2, 3))
    ):
        for c in range(3):
            packets[slot][12 + 2 * c : 14 + 2 * c, :] = jnp.where(
                even,
                loads_out[8 * c + 2 * high : 8 * c + 2 * high + 2, :],
                loads_out[8 * c + 2 * low : 8 * c + 2 * low + 2, :],
            )


def row_kernel(blocks_ref, conn_ref, row_ref, scale_ref, row_out, peaks):
    for chunk in range(CHUNKS):
        at = slice(chunk * LANES, (chunk + 1) * LANES)
        row_maxima(blocks_ref, [node_picks(scale_ref, 3, conn_ref, chunk)], at, peaks)
    row_out[...] = row_ref[...] / jnp.sqrt(row_ref[...] * peaks[...])


def target_kernel(blocks_ref, conn_ref, row_ref, scale_ref, part_ref, loads_ref, *rest):
    arrived, rest = by_side(rest[:4]), rest[4:]
    scale_out, image_out, part_out, rest = rest[0], rest[1], rest[2], rest[3:]
    packets, (term, table, strain) = rest[:4], rest[4:]
    unpack(part_ref, 3, arrived, jnp.maximum, table)
    scale = rescale(scale_ref[...], table[...])
    scale_out[...] = scale
    for c in range(3):
        table[NODE_ROWS * c : NODE_ROWS * c + 8, :] = loads_ref[8 * c : 8 * c + 8, :]
        for side in range(SIDES):
            base = NODE_ROWS * c + 8 + 2 * side
            table[base : base + 2, :] = arrived[side][12 + 2 * c : 14 + 2 * c]
    table[...] = scale * (scale * table[...])
    apply_blocks(blocks_ref, table, 1, conn_ref, strain)
    row = row_ref[...]
    image = row * strain[...]
    image_out[...] = image
    strain[...] = row * image
    apply_transpose(blocks_ref, strain, 1, term)
    scatter_sums(term, 3, conn_ref, part_out)
    part_out[...] = part_out[...] * scale
    pack(part_out, 3, packets)


def cone_kernel(blocks_ref, conn_ref, row_ref, scale_ref, image_ref, base_out, part_out, term, strain):
    strain[...] = image_ref[...]
    project_rows(strain)
    base_out[...] = 3.0 * image_ref[...] + 2.0 * strain[...]
    strain[...] = row_ref[...] * strain[...]
    apply_transpose(blocks_ref, strain, 1, term)
    scatter_sums(term, 3, conn_ref, part_out)
    part_out[...] = part_out[...] * scale_ref[...]


def second_kernel(blocks_ref, conn_ref, row_ref, scale_ref, part_ref, joint_ref, *rest):
    arrived, rest = by_side(rest[:4]), rest[4:]
    part_out, packets, (term, table, strain) = rest[0], rest[1:5], rest[5:]
    unpack(part_ref, 3, arrived, jnp.add, table)
    scale = scale_ref[...]
    table[...] = scale * table[...]
    apply_blocks(blocks_ref, table, 1, conn_ref, strain)
    row = row_ref[...]
    strain[...] = row * (row * strain[...])
    apply_transpose(blocks_ref, strain, 1, term)
    scatter_sums(term, 3, conn_ref, part_out)
    part_out[0:48, :] = part_out[0:48, :] * scale
    part_out[48:96, :] = joint_ref[...]
    pack(part_out, 6, packets)


def joint_kernel(blocks_ref, conn_ref, row_ref, scale_ref, joint_ref, line_ref, image_out, table, strain):
    table[...] = scale_ref[...] * joint_ref[...]
    apply_blocks(blocks_ref, table, 1, conn_ref, strain)
    image_out[...] = row_ref[...] * strain[...]


def own_square(ref):
    total = jnp.zeros((8, LANES), F32)
    for c in range(3):
        mine = ref[NODE_ROWS * c : NODE_ROWS * c + 8, :]
        total = total + mine * mine
    return jnp.sum(total, axis=0, keepdims=True)


def third_kernel(
    blocks_ref, conn_ref, row_ref, scale_ref, part_ref, *rest
):
    arrived, rest = by_side(rest[:4]), rest[4:]
    norm_out, joint_out, part_out, right_out, above_out, term, table, strain = rest
    unpack(part_ref, 6, arrived, jnp.add, table)
    norm_out[...] = own_square(table)
    joint_out[...] = table[48:96, :]
    scale = scale_ref[...]
    table[0:48, :] = scale * table[0:48, :]
    apply_blocks(blocks_ref, table, 1, conn_ref, strain)
    row = row_ref[...]
    strain[...] = row * (row * strain[...])
    apply_transpose(blocks_ref, strain, 1, term)
    scatter_sums(term, 3, conn_ref, part_out)
    part_out[...] = part_out[...] * scale
    for packet, side in ((right_out, 1), (above_out, 3)):
        for channel in range(3):
            packet[4 * channel : 4 * channel + 2, :] = side_rows(part_out, side, channel)
            packet[4 * channel + 2 : 4 * channel + 4, :] = side_rows(part_out, side + 4, channel)


def norm_kernel(part_ref, norm_ref, left_ref, below_ref, sums_out, line_out):
    below, above = live_sides()
    squares = jnp.zeros((2, LANES), F32)
    for channel in range(3):
        for side, arrived, live in ((0, left_ref, True), (2, below_ref, below)):
            theirs = arrived[4 * channel : 4 * channel + 4, :]
            theirs = jnp.where(live, theirs, 0.0)
            own = side_rows(part_ref, side, channel) + theirs[2:4]
            copy = side_rows(part_ref, side + 4, channel) + theirs[0:2]
            squares = squares + own * own + copy * copy
        alone = jnp.where(above, 0.0, side_rows(part_ref, 3, channel))
        squares = squares + alone * alone
    last = jnp.sum(squares, axis=0, keepdims=True)
    first = norm_ref[...]
    lane = lax.broadcasted_iota(I32, (1, LANES), 1)
    line = jnp.where(lane < 64, first + pltpu.roll(first, 64, 1), last + pltpu.roll(last, 64, 1))
    sums_out[...] = jnp.broadcast_to(line, sums_out.shape)
    line_out[...] = line


def lines_kernel(scale_ref, loads_ref, joint_ref, inverse_ref, line_ref, velocity_out, lines):
    for c in range(3):
        base = NODE_ROWS * c
        scale = scale_ref[base : base + 8, :]
        lines[8 * c : 8 * c + 8, :] = scale * (scale * loads_ref[8 * c : 8 * c + 8, :])
        lines[24 + 8 * c : 32 + 8 * c, :] = scale * joint_ref[base : base + 8, :]
    tables = [rows_of(lines, 8 * channel) for channel in range(6)]
    for channel, values in enumerate(table_picks(tables, 8, inverse_ref[...])):
        velocity_out[8 * channel : 8 * channel + 8, :] = values


def final_kernel(
    sums_ref, step_ref, velocity_ref, base_ref, joint_ref, row_ref, velocity_out, multiplier_out, *rest
):
    velocity, cones, flat, semaphores = rest
    sums = jnp.sum(sums_ref[...], axis=0, keepdims=True)
    lane = lax.broadcasted_iota(I32, (1, LANES), 1)
    before = jnp.sum(jnp.where(lane < 64, sums, 0.0), axis=1, keepdims=True)
    after = jnp.sum(jnp.where(lane < 64, 0.0, sums), axis=1, keepdims=True)
    largest = jnp.sqrt(after + epsilon) / jnp.sqrt(before + epsilon)
    step = step_ref[0] / jnp.sqrt(largest)
    square = step * step
    velocity[...] = (2.0 * step) * (square * velocity_ref[24:48, :] - velocity_ref[0:24, :])
    first = pltpu.make_async_copy(velocity, velocity_out, semaphores.at[0])
    first.start()
    cones[...] = square * (base_ref[...] - (4.0 * square) * joint_ref[...])
    project_rows(cones)
    cones[...] = row_ref[...] * cones[...]
    for r in range(STRAINS):
        for chunk in range(CHUNKS):
            flat[8 * r + chunk : 8 * r + chunk + 1, :] = cones[
                r : r + 1, chunk * LANES : (chunk + 1) * LANES
            ]
    second = pltpu.make_async_copy(flat, multiplier_out, semaphores.at[1])
    second.start()
    first.wait()
    second.wait()


def call(body, out_shapes, scratch, *arrays, smem=(), outside=(), outside_results=False, work=0, limit=24 * 1024):
    def space(i):
        return pltpu.SMEM if i in smem else pltpu.HBM if i in outside else pltpu.VMEM

    result = pltpu.HBM if outside_results else pltpu.VMEM
    return pl.pallas_call(
        body,
        out_shape=[jax.ShapeDtypeStruct(shape, kind) for shape, kind in out_shapes],
        in_specs=[pl.BlockSpec(memory_space=space(i)) for i in range(len(arrays))],
        out_specs=[pl.BlockSpec(memory_space=result) for _ in out_shapes],
        scratch_shapes=[
            entry if not isinstance(entry, tuple) else pltpu.VMEM(*entry) for entry in scratch
        ],
        cost_estimate=pl.CostEstimate(flops=work, bytes_accessed=work // 256, transcendentals=0),
        compiler_params=pltpu.CompilerParams(vmem_limit_bytes=limit * 1024),
    )(*arrays)


def swap_pairs(axis, odd):
    count = lax.axis_size(axis)
    return [(i, (((i - odd) ^ 1) + odd) % count) for i in range(count)]


PAIRS = (("sector", 1), ("band", 1), ("sector", 0), ("band", 0))


def exchange(packets):
    return [
        lax.ppermute(packet, axis, swap_pairs(axis, odd)) for packet, (axis, odd) in zip(packets, PAIRS)
    ]


def shift_up(packet, axis):
    count = lax.axis_size(axis)
    return lax.ppermute(packet, axis, [(i, (i + 1) % count) for i in range(count)])


def per_device(blocks, connectivity, send_lists, nodal_loads, step_scale):
    packet = [((12, LANES), F32)] * 4
    nodes = ((48, LANES), F32)
    rows = ((STRAINS, 1024), F32)
    items = ((3 * ITEM_ROWS, LANES), F32)
    twice = ((6 * ITEM_ROWS, LANES), F32)
    ids = ((64, LANES), I32)
    few = ((8, LANES), I32)
    conn, *rest = call(
        start_kernel,
        [ids, ((SORTED_ROWS, LANES), I32), few, ((16, LANES), I32), few, ((16, LANES), I32), few, few]
        + [rows, ((96, LANES), F32)]
        + [((24, LANES), F32)] * 4,
        [
            ((1, 1, STRAINS, 24, 1024), F32),
            ((1, 1, 8, 1024), I32),
            ((1, 1, SIDES, 256), I32),
            ids,
            twice,
            ((6 * SORTED_ROWS, LANES), F32),
            rows,
            pltpu.SemaphoreType.DMA((3,)),
        ],
        blocks,
        connectivity,
        send_lists,
        outside=(0, 1, 2),
        limit=LIMIT,
        work=12_000_000_000,
    )
    plan, (inverse, send, row, part), packets = rest[:5], rest[5:9], rest[9:]
    row, scale, part, loads, *packets = call(
        sweep_kernel,
        [rows, nodes, nodes, ((24, LANES), F32)] + [((18, LANES), F32)] * 4,
        [items, ((3 * SORTED_ROWS, LANES), F32), rows, ((96, LANES), F32)],
        blocks,
        conn,
        row,
        part,
        nodal_loads.reshape(24, LANES),
        send,
        *plan,
        *exchange(packets),
    )
    (row,) = call(row_kernel, [rows], [rows], blocks, conn, row, scale, work=BESIDE)
    scale, image, part, *packets = call(
        target_kernel,
        [nodes, rows, nodes] + packet,
        [items, nodes, rows],
        blocks,
        conn,
        row,
        scale,
        part,
        loads,
        *exchange(packets),
    )
    base, joint = call(
        cone_kernel, [rows, nodes], [items, rows], blocks, conn, row, scale, image, work=BESIDE
    )
    part, *packets = call(
        second_kernel,
        [((96, LANES), F32)] + [((24, LANES), F32)] * 4,
        [items, nodes, rows],
        blocks,
        conn,
        row,
        scale,
        part,
        joint,
        *exchange(packets),
    )
    norm, joint, part, right, above = call(
        third_kernel,
        [((1, LANES), F32), nodes, nodes] + packet[:2],
        [items, ((96, LANES), F32), rows],
        blocks,
        conn,
        row,
        scale,
        part,
        *exchange(packets),
    )
    count = lax.axis_size("band") * lax.axis_size("sector")
    sums, line = call(
        norm_kernel,
        [((count, LANES), F32), ((1, LANES), F32)],
        [],
        part,
        norm,
        shift_up(right, "sector"),
        shift_up(above, "band"),
    )
    (image,) = call(
        joint_kernel, [rows], [nodes, rows], blocks, conn, row, scale, joint, line, work=BESIDE
    )
    (lines,) = call(
        lines_kernel,
        [((48, LANES), F32)],
        [nodes],
        scale,
        loads,
        joint,
        inverse,
        line,
        work=BESIDE,
    )
    sums = lax.all_to_all(sums, AXES, 0, 0, tiled=True)
    velocities, multipliers = call(
        final_kernel,
        [((24, LANES), F32), ((96, LANES), F32)],
        [((24, LANES), F32), rows, ((96, LANES), F32), pltpu.SemaphoreType.DMA((2,))],
        sums,
        step_scale,
        lines,
        base,
        image,
        row,
        smem=(1,),
        outside_results=True,
    )
    return velocities.reshape(1, 1, 3, 1024), multipliers.reshape(1, 1, STRAINS, 1024)


def solution(mesh):
    in_specs = (
        P("band", "sector", None, None, None),
        P("band", "sector", None, None),
        P("band", "sector", None, None),
        P("band", "sector", None, None),
        P(),
    )
    out_specs = (P("band", "sector", None, None), P("band", "sector", None, None))
    return jax.shard_map(
        per_device, mesh=mesh, in_specs=in_specs, out_specs=out_specs, check_vma=False
    )
```

```python
import functools

import jax
import jax.numpy as jnp
from jax import lax
from jax.experimental import pallas as pl
from jax.experimental.pallas import tpu as pltpu
from jax.sharding import PartitionSpec as P

LANES = 128
CHUNKS = 8
STRAINS = 12
NODE_ROWS = 16
ITEM_ROWS = 64
SIDES = 4
PARTS = 2
BESIDE = 1_000_000_000
LIMIT = 54000
AXES = ("band", "sector")
epsilon = 1e-06
F32 = jnp.float32
I32 = jnp.int32


def tile_iota(axis):
    return lax.broadcasted_iota(I32, (8, LANES), axis)


def pick(rows, index, axis):
    dims = lax.GatherDimensionNumbers(
        offset_dims=(),
        collapsed_slice_dims=(axis,),
        start_index_map=(axis,),
        operand_batching_dims=(1 - axis,),
        start_indices_batching_dims=(1 - axis,),
    )
    return lax.gather(
        rows,
        index[..., None],
        dims,
        slice_sizes=(1, 1),
        mode=lax.GatherScatterMode.PROMISE_IN_BOUNDS,
    )


def table_picks(row_getters, rows, flat):
    rows = tuple(range(rows)) if isinstance(rows, int) else rows
    lanes = flat & (LANES - 1)
    levels = rows[-1].bit_length()
    bits = [(flat & (LANES << level)) != 0 for level in range(levels)]

    def descend(row_at, level, base):
        if level < 0:
            return pick(jnp.broadcast_to(row_at(base), (8, LANES)), lanes, 1) if base in rows else None
        low = descend(row_at, level - 1, base)
        high = descend(row_at, level - 1, base + (1 << level))
        if low is None or high is None:
            return high if low is None else low
        return jnp.where(bits[level], high, low)

    return [descend(row_at, levels - 1, 0) for row_at in row_getters]


def rows_of(ref, offset):
    return lambda row: ref[offset + row : offset + row + 1, :]


def group_shift(values, distance):
    if distance >= 8:
        return pltpu.roll(values, distance // 8, 1)
    turned = pltpu.roll(values, distance, 0)
    return jnp.where(tile_iota(0) < distance, pltpu.roll(turned, 1, 1), turned)


SCAN_STEPS = tuple(1 << step for step in range(10))
RUNS = 5
SORT_FIRST = 64
SORTED_ROWS = 8 * RUNS
LOOSE_ROWS = tuple(row for row in range(ITEM_ROWS) if row % 8 >= 3)


def sort_items(keys, size, last):
    sub, lane = tile_iota(0), tile_iota(1)
    while size <= last:
        half = size // 2
        while half >= 1:
            new = list(keys)

            def rising(register):
                if size < 8:
                    return (register & size) == 0
                if size < 64:
                    return (sub & (size // 8)) == 0
                if size < 8192:
                    return (lane & (size // 64)) == 0
                return True

            for register in range(8):
                up = rising(register)
                if half < 8:
                    other = register ^ half
                    if other < register:
                        continue
                    low = jnp.minimum(keys[register], keys[other])
                    high = jnp.maximum(keys[register], keys[other])
                    if isinstance(up, bool):
                        new[register], new[other] = (low, high) if up else (high, low)
                    else:
                        new[register] = jnp.where(up, low, high)
                        new[other] = jnp.where(up, high, low)
                    continue
                if half < 64:
                    step = half // 8
                    partner = pick(keys[register], sub ^ step, 0)
                    first = (sub & step) == 0
                else:
                    step = half // 64
                    partner = pick(keys[register], lane ^ step, 1)
                    first = (lane & step) == 0
                low = jnp.minimum(keys[register], partner)
                high = jnp.maximum(keys[register], partner)
                if isinstance(up, bool):
                    keep_low = first if up else jnp.logical_not(first)
                else:
                    keep_low = first == up
                new[register] = jnp.where(keep_low, low, high)
            keys = new
            half //= 2
        size *= 2
    return keys


def one_line(rows):
    return jnp.concatenate([rows[k : k + 1] for k in range(rows.shape[0])], axis=1)


def inverse_of(line, code, rows):
    width = line.shape[1]
    in_row = (line >> 7) == lax.broadcasted_iota(I32, (rows, width), 0)
    left = jnp.concatenate(
        [
            jnp.where(in_row, (code >> 7).astype(F32), 0.0),
            jnp.where(in_row, (code & (LANES - 1)).astype(F32), 0.0),
        ],
        axis=0,
    ).astype(jnp.bfloat16)
    in_lane = (line & (LANES - 1)) == lax.broadcasted_iota(I32, (LANES, width), 0)
    right = jnp.where(in_lane, 1.0, 0.0).astype(jnp.bfloat16)
    found = lax.dot_general(left, right, (((1,), (1,)), ((), ())), preferred_element_type=F32)
    return (found[0:rows] * 128.0 + found[rows : 2 * rows]).astype(I32)


def relabel_kernel(ids_ref, send_ref, conn_out, inverse_out):
    place = lax.broadcasted_iota(I32, (1, 8 * LANES), 1)
    inverse_out[...] = inverse_of(one_line(send_ref[...]), place, 8)
    for chunk in range(CHUNKS):
        ids = ids_ref[0, 0, :, chunk * LANES : (chunk + 1) * LANES]
        (label,) = table_picks([rows_of(inverse_out, 0)], 8, ids & 1023)
        conn_out[8 * chunk : 8 * chunk + 8, :] = jnp.where(ids < 1024, label, ids)


def to_lists(source_ref, channels, send_ref, out_ref):
    tables = [rows_of(source_ref, NODE_ROWS * channel) for channel in range(channels)]
    for channel, values in enumerate(table_picks(tables, 8, send_ref[...])):
        base = NODE_ROWS * channel
        out_ref[base : base + 8, :] = values
        out_ref[base + 8 : base + 16, :] = source_ref[base + 8 : base + 16, :]


def first_keys(ids_ref, own_out, pair_out):
    place = lax.broadcasted_iota(I32, (1, 8 * LANES), 1)
    own_out[...] = inverse_of(ids_ref[0, 0, 0:1, :], place, 8)
    pair_line = jnp.concatenate(
        [
            ids_ref[0, 0, k : k + 1, chunk * LANES : (chunk + 1) * LANES]
            for chunk in range(CHUNKS)
            for k in (1, 2)
        ],
        axis=1,
    )
    pair_out[...] = inverse_of(pair_line, lax.broadcasted_iota(I32, (1, 16 * LANES), 1), NODE_ROWS)
    sub, lane = tile_iota(0), tile_iota(1)
    keys = []
    for chunk in range(CHUNKS):
        ids = ids_ref[0, 0, :, chunk * LANES : (chunk + 1) * LANES]
        item = ids * 8192 + (chunk * 1024 + sub * LANES + lane)
        keys.append(jnp.where(sub < 3, 2048 * 8192, item))
    return keys


def make_order(keys, key_out, scan_out, end_out, keys_ref):
    sub, lane = tile_iota(0), tile_iota(1)
    keys = sort_items(keys, 2 * SORT_FIRST, 8192)
    for register in range(8):
        keys_ref[8 * register : 8 * register + 8, :] = keys[register]
    group = lane * 8 + sub
    runs = []
    for register in range(RUNS):
        place = group * RUNS + register
        row = (place & 7) * 8 + ((place >> 3) & 7)
        (moved,) = table_picks([rows_of(keys_ref, 0)], ITEM_ROWS, row * LANES + (place >> 6))
        runs.append(moved)
        key_out[8 * register : 8 * register + 8, :] = moved
    first, last = runs[0] >> 13, runs[-1] >> 13
    scan = jnp.zeros((8, LANES), I32)
    for step, distance in enumerate(SCAN_STEPS):
        same = (group >= distance) & (group_shift(last, distance) == last)
        scan = jnp.where(same, scan | (1 << step), scan)
    same = (group >= 1) & (group_shift(last, 1) == first)
    scan_out[...] = jnp.where(same, scan | (1 << len(SCAN_STEPS)), scan)
    lane_last = jnp.broadcast_to(keys_ref[63:64, :] >> 13, (8, LANES))
    for half in range(2):
        node = (half * 8 + sub) * LANES + lane
        column = jnp.zeros((8, LANES), I32)
        for step in (64, 32, 16, 8, 4, 2, 1):
            seen = pick(lane_last, column + (step - 1), 1)
            column = jnp.where(seen <= node, column + step, column)
        count = column * 64
        before = pick(lane_last, jnp.maximum(column - 1, 0), 1)
        named = (column > 0) & (before == node)
        for row in range(ITEM_ROWS):
            seen = pick(jnp.broadcast_to(keys_ref[row : row + 1, :], (8, LANES)), column, 1) >> 13
            count = count + jnp.where(seen <= node, 1, 0)
            named = named | (seen == node)
        place = jnp.maximum(count - 1, 0)
        place = jnp.where(named, place, 0)
        share = (place * 52429) >> 18
        row = (place - share * RUNS) * 8 + (share & 7)
        end = row * LANES + (share >> 3)
        end_out[8 * half : 8 * half + 8, :] = jnp.where(named, end, 8192)


def scatter_maxima(term_ref, channels, plan, sorted_ref, out_ref):
    key_ref, scan_ref, end_ref, own_ref, pair_ref = plan
    tables = [rows_of(term_ref, ITEM_ROWS * channel) for channel in range(channels)]
    nodes = []
    for register in range(RUNS):
        key = key_ref[8 * register : 8 * register + 8, :]
        nodes.append(key >> 13)
        for channel, values in enumerate(table_picks(tables, LOOSE_ROWS, key & 8191)):
            base = SORTED_ROWS * channel + 8 * register
            sorted_ref[base : base + 8, :] = values
    scan = scan_ref[...]
    follows = [(scan & (1 << step)) != 0 for step in range(len(SCAN_STEPS) + 1)]
    runs = []
    for channel in range(channels):
        base = SORTED_ROWS * channel
        mine = [sorted_ref[base : base + 8, :]]
        for register in range(1, RUNS):
            same = nodes[register] == nodes[register - 1]
            here = sorted_ref[base + 8 * register : base + 8 * register + 8, :]
            mine.append(jnp.maximum(here, jnp.where(same, mine[-1], 0.0)))
        runs.append(mine)
    totals = [mine[-1] for mine in runs]
    for step, distance in enumerate(SCAN_STEPS):
        totals = [
            jnp.maximum(total, jnp.where(follows[step], group_shift(total, distance), 0.0))
            for total in totals
        ]
    carries = [jnp.where(follows[-1], group_shift(total, 1), 0.0) for total in totals]
    for channel in range(channels):
        base = SORTED_ROWS * channel
        for register in range(RUNS):
            open_run = nodes[register] == nodes[0]
            sorted_ref[base + 8 * register : base + 8 * register + 8, :] = jnp.maximum(
                runs[channel][register], jnp.where(open_run, carries[channel], 0.0)
            )
    sorted_tables = [rows_of(sorted_ref, SORTED_ROWS * channel) for channel in range(channels)]
    first_tables = [lambda row, at=at: at(8 * row) for at in tables]
    pair_tables = [lambda row, at=at: at((row >> 1) * 8 + (row & 1) + 1) for at in tables]
    own = table_picks(first_tables, 8, own_ref[...])
    for half in range(2):
        index = end_ref[8 * half : 8 * half + 8, :]
        loose = table_picks(sorted_tables, SORTED_ROWS, index & 8191)
        paired = table_picks(pair_tables, NODE_ROWS, pair_ref[8 * half : 8 * half + 8, :])
        for channel in range(channels):
            best = jnp.maximum(jnp.where(index < 8192, loose[channel], 0.0), paired[channel])
            if half == 0:
                best = jnp.maximum(best, own[channel])
            base = NODE_ROWS * channel + 8 * half
            out_ref[base : base + 8, :] = best


def node_picks(table_ref, channels, conn_ref, chunk):
    tables = [rows_of(table_ref, NODE_ROWS * channel) for channel in range(channels)]
    return table_picks(tables, NODE_ROWS, conn_ref[8 * chunk : 8 * chunk + 8, :])


def bf16_parts(values, count):
    parts = []
    for _ in range(count):
        part = values.astype(jnp.bfloat16).astype(F32)
        parts.append(part)
        values = values - part
    return parts


def scatter_sums(term_ref, channels, conn_ref, out_ref):
    width = 8 * LANES
    row_ids = lax.broadcasted_iota(I32, (NODE_ROWS, width), 0).astype(F32)
    lane_ids = lax.broadcasted_iota(I32, (LANES, width), 0).astype(F32)
    total = jnp.zeros((channels * PARTS * NODE_ROWS, LANES), F32)
    for chunk in range(CHUNKS):
        ids = conn_ref[8 * chunk : 8 * chunk + 8, :]
        in_row = one_line((ids >> 7).astype(F32)) == row_ids
        in_lane = one_line((ids & (LANES - 1)).astype(F32)) == lane_ids
        left = []
        for channel in range(channels):
            base = ITEM_ROWS * channel + 8 * chunk
            for part in bf16_parts(one_line(term_ref[base : base + 8, :]), PARTS):
                left.append(jnp.where(in_row, part, 0.0).astype(jnp.bfloat16))
        total = total + lax.dot_general(
            jnp.concatenate(left, axis=0),
            jnp.where(in_lane, 1.0, 0.0).astype(jnp.bfloat16),
            (((1,), (1,)), ((), ())),
            preferred_element_type=F32,
        )
    for channel in range(channels):
        base = PARTS * NODE_ROWS * channel
        out = total[base : base + NODE_ROWS]
        for part in range(1, PARTS):
            out = out + total[base + part * NODE_ROWS : base + (part + 1) * NODE_ROWS]
        out_ref[NODE_ROWS * channel : NODE_ROWS * (channel + 1), :] = out


def row_maxima(blocks_ref, picked, at, max_ref):
    for r in range(STRAINS):
        sized = [jnp.abs(blocks_ref[0, 0, r, 8 * c : 8 * c + 8, at]) for c in range(3)]
        for k, scales in enumerate(picked):
            whole = sized[0] * scales[0]
            for c in range(1, 3):
                whole = jnp.maximum(whole, sized[c] * scales[c])
            max_ref[STRAINS * k + r : STRAINS * k + r + 1, at] = jnp.max(whole, axis=0, keepdims=True)


def column_maxima(blocks_ref, row_ref, term_ref, first_channel):
    for chunk in range(CHUNKS):
        at = slice(chunk * LANES, (chunk + 1) * LANES)
        best = [jnp.zeros((8, LANES), F32)] * 3
        for r in range(STRAINS):
            row = 1.0 if row_ref is None else row_ref[r : r + 1, at]
            for c in range(3):
                size = jnp.abs(blocks_ref[0, 0, r, 8 * c : 8 * c + 8, at]) * row
                best[c] = jnp.maximum(best[c], size)
        for c in range(3):
            base = ITEM_ROWS * (first_channel + c) + 8 * chunk
            term_ref[base : base + 8, :] = best[c]


def apply_blocks(blocks_ref, table_ref, sets, conn_ref, strain_ref):
    for chunk in range(CHUNKS):
        values = node_picks(table_ref, 3 * sets, conn_ref, chunk)
        at = slice(chunk * LANES, (chunk + 1) * LANES)
        for r in range(STRAINS):
            parts = [blocks_ref[0, 0, r, 8 * c : 8 * c + 8, at] for c in range(3)]
            for k in range(sets):
                mine = values[3 * k : 3 * k + 3]
                total = parts[0] * mine[0] + parts[1] * mine[1] + parts[2] * mine[2]
                strain_ref[STRAINS * k + r : STRAINS * k + r + 1, at] = jnp.sum(
                    total, axis=0, keepdims=True
                )


def apply_transpose(blocks_ref, strain_ref, sets, term_ref):
    for chunk in range(CHUNKS):
        at = slice(chunk * LANES, (chunk + 1) * LANES)
        totals = [jnp.zeros((8, LANES), F32)] * (3 * sets)
        for r in range(STRAINS):
            parts = [blocks_ref[0, 0, r, 8 * c : 8 * c + 8, at] for c in range(3)]
            for k in range(sets):
                strain = strain_ref[STRAINS * k + r : STRAINS * k + r + 1, at]
                for c in range(3):
                    totals[3 * k + c] = totals[3 * k + c] + parts[c] * strain
        for channel in range(3 * sets):
            row = ITEM_ROWS * channel + 8 * chunk
            term_ref[row : row + 8, :] = totals[channel]


def even_places():
    return lax.axis_index("sector") % 2 == 0, lax.axis_index("band") % 2 == 0


def side_rows(part_ref, side, channel, length=2):
    base = NODE_ROWS * channel + 2 * side
    return part_ref[base : base + length, :]


def pack(part_ref, channels, packet_refs):
    even_sector, even_band = even_places()
    for slot, (even, low, high) in enumerate(
        ((even_sector, 1, 0), (even_band, 3, 2), (even_sector, 0, 1), (even_band, 2, 3))
    ):
        for channel in range(channels):
            for part in range(2):
                packet_refs[slot][4 * channel + 2 * part : 4 * channel + 2 * part + 2, :] = jnp.where(
                    even,
                    side_rows(part_ref, high + 4 * part, channel),
                    side_rows(part_ref, low + 4 * part, channel),
                )


def by_side(arrived_refs):
    even_sector, even_band = even_places()
    odd_cycle, odd_band, even_cycle, even_pair = [ref[...] for ref in arrived_refs]
    below, above = live_sides()
    return [
        jnp.where(even_sector, odd_cycle, even_cycle),
        jnp.where(even_sector, even_cycle, odd_cycle),
        jnp.where(below, jnp.where(even_band, odd_band, even_pair), 0.0),
        jnp.where(above, jnp.where(even_band, even_pair, odd_band), 0.0),
    ]


def live_sides():
    band = lax.axis_index("band")
    return [band > 0, band < lax.axis_size("band") - 1]


def unpack(part_ref, channels, arrived, merge, out_ref):
    for side in range(SIDES):
        for channel in range(channels):
            base = NODE_ROWS * channel + 2 * side
            theirs = arrived[side][4 * channel : 4 * channel + 4]
            out_ref[base : base + 2, :] = merge(part_ref[base : base + 2, :], theirs[2:4])
            out_ref[base + 8 : base + 10, :] = merge(part_ref[base + 8 : base + 10, :], theirs[0:2])


def rescale(scale, peak):
    peak = scale * peak
    seen = peak > 0.0
    return jnp.where(seen, scale / jnp.sqrt(jnp.where(seen, peak, 1.0)), 0.0)


def project_rows(ref):
    def every_third(start):
        return jnp.concatenate([ref[r : r + 1, :] for r in range(start, STRAINS, 3)], axis=0)

    top, first, second = [every_third(start) for start in range(3)]
    norm = jnp.sqrt(first * first + second * second)
    inside = norm <= top
    middle = norm > jnp.abs(top)
    factor = 0.5 * (1.0 + top / jnp.where(middle, norm, 1.0))
    gain = jnp.where(inside, 1.0, jnp.where(middle, factor, 0.0))
    top = jnp.where(inside, top, jnp.where(middle, factor * norm, 0.0))
    for start, values in enumerate((top, gain * first, gain * second)):
        for cone in range(4):
            ref[3 * cone + start : 3 * cone + start + 1, :] = values[cone : cone + 1, :]


def start_kernel(blocks_at, ids_ref, *rest):
    plan, (row_out, part_out), rest = rest[:5], rest[5:7], rest[7:]
    blocks_ref, keys_ref, term, items, peaks, semaphore = rest
    copy = pltpu.make_async_copy(blocks_at, blocks_ref, semaphore)
    copy.start()
    keys = sort_items(first_keys(ids_ref, *plan[3:]), 2, SORT_FIRST)
    copy.wait()
    below, above = [live.astype(F32) for live in live_sides()]
    for chunk in range(CHUNKS):
        at = slice(chunk * LANES, (chunk + 1) * LANES)
        ids = ids_ref[0, 0, :, at]
        scale = jnp.where(ids < 1536, 1.0, jnp.where(ids < 1792, below, above))
        row_maxima(blocks_ref, [[scale] * 3], at, peaks)
    row_out[...] = 1.0 / jnp.sqrt(peaks[...])
    column_maxima(blocks_ref, None, term, 0)
    column_maxima(blocks_ref, row_out, term, 3)
    make_order(keys, *plan[:3], keys_ref)
    scatter_maxima(term, 6, plan, items, part_out)


def pack_kernel(part_ref, lists_ref, send_out, part_out, *packets):
    for half in range(8):
        start = (half % 2) * LANES
        send_out[half : half + 1, :] = lists_ref[0, 0, half // 2 : half // 2 + 1, start : start + LANES]
    to_lists(part_ref, 6, send_out, part_out)
    pack(part_out, 6, packets)


def sweep_kernel(
    blocks_ref, conn_ref, row_ref, part_ref, loads_ref, send_ref, *rest
):
    plan, rest = rest[:5], rest[5:]
    arrived, rest = by_side(rest[:4]), rest[4:]
    row_out, scale_out, part_out, loads_out, rest = rest[0], rest[1], rest[2], rest[3], rest[4:]
    packets, (term, items, peaks, merged) = rest[:4], rest[4:]
    unpack(part_ref, 6, arrived, jnp.maximum, merged)
    row = lax.broadcasted_iota(I32, (NODE_ROWS, LANES), 0)
    below, above = [live.astype(F32) for live in live_sides()]
    start = jnp.where(row < 12, 1.0, jnp.where(row < 14, below, above))
    for c in range(3):
        first = rescale(start, merged[NODE_ROWS * c : NODE_ROWS * (c + 1), :])
        later = NODE_ROWS * (c + 3)
        second = rescale(first, merged[later : later + NODE_ROWS, :])
        merged[NODE_ROWS * c : NODE_ROWS * (c + 1), :] = first
        scale_out[NODE_ROWS * c : NODE_ROWS * (c + 1), :] = second
    for chunk in range(CHUNKS):
        at = slice(chunk * LANES, (chunk + 1) * LANES)
        row_maxima(blocks_ref, [node_picks(merged, 3, conn_ref, chunk)], at, peaks)
    row_out[...] = row_ref[...] / jnp.sqrt(row_ref[...] * peaks[...])
    column_maxima(blocks_ref, row_out, term, 0)
    scatter_maxima(term, 3, plan, items, merged)
    to_lists(merged, 3, send_ref, part_out)
    pack(part_out, 3, packets)
    tables = [rows_of(loads_ref, 8 * c) for c in range(3)]
    for c, values in enumerate(table_picks(tables, 8, send_ref[...])):
        loads_out[8 * c : 8 * c + 8, :] = values
    even_sector, even_band = even_places()
    for slot, (even, low, high) in enumerate(
        ((even_sector, 1, 0), (even_band, 3, 2), (even_sector, 0, 1), (even_band, 2, 3))
    ):
        for c in range(3):
            packets[slot][12 + 2 * c : 14 + 2 * c, :] = jnp.where(
                even,
                loads_out[8 * c + 2 * high : 8 * c + 2 * high + 2, :],
                loads_out[8 * c + 2 * low : 8 * c + 2 * low + 2, :],
            )


def row_kernel(blocks_ref, conn_ref, row_ref, scale_ref, row_out, peaks):
    for chunk in range(CHUNKS):
        at = slice(chunk * LANES, (chunk + 1) * LANES)
        row_maxima(blocks_ref, [node_picks(scale_ref, 3, conn_ref, chunk)], at, peaks)
    row_out[...] = row_ref[...] / jnp.sqrt(row_ref[...] * peaks[...])


def target_kernel(blocks_ref, conn_ref, row_ref, scale_ref, part_ref, loads_ref, *rest):
    arrived, rest = by_side(rest[:4]), rest[4:]
    scale_out, image_out, part_out, rest = rest[0], rest[1], rest[2], rest[3:]
    packets, (term, table, strain) = rest[:4], rest[4:]
    unpack(part_ref, 3, arrived, jnp.maximum, table)
    scale = rescale(scale_ref[...], table[...])
    scale_out[...] = scale
    for c in range(3):
        table[NODE_ROWS * c : NODE_ROWS * c + 8, :] = loads_ref[8 * c : 8 * c + 8, :]
        for side in range(SIDES):
            base = NODE_ROWS * c + 8 + 2 * side
            table[base : base + 2, :] = arrived[side][12 + 2 * c : 14 + 2 * c]
    table[...] = scale * (scale * table[...])
    apply_blocks(blocks_ref, table, 1, conn_ref, strain)
    row = row_ref[...]
    image = row * strain[...]
    image_out[...] = image
    strain[...] = row * image
    apply_transpose(blocks_ref, strain, 1, term)
    scatter_sums(term, 3, conn_ref, part_out)
    part_out[...] = part_out[...] * scale
    pack(part_out, 3, packets)


def cone_kernel(blocks_ref, conn_ref, row_ref, scale_ref, image_ref, base_out, part_out, term, strain):
    strain[...] = image_ref[...]
    project_rows(strain)
    base_out[...] = 3.0 * image_ref[...] + 2.0 * strain[...]
    strain[...] = row_ref[...] * strain[...]
    apply_transpose(blocks_ref, strain, 1, term)
    scatter_sums(term, 3, conn_ref, part_out)
    part_out[...] = part_out[...] * scale_ref[...]


def second_kernel(blocks_ref, conn_ref, row_ref, scale_ref, part_ref, joint_ref, *rest):
    arrived, rest = by_side(rest[:4]), rest[4:]
    part_out, packets, (term, table, strain) = rest[0], rest[1:5], rest[5:]
    unpack(part_ref, 3, arrived, jnp.add, table)
    scale = scale_ref[...]
    table[...] = scale * table[...]
    apply_blocks(blocks_ref, table, 1, conn_ref, strain)
    row = row_ref[...]
    strain[...] = row * (row * strain[...])
    apply_transpose(blocks_ref, strain, 1, term)
    scatter_sums(term, 3, conn_ref, part_out)
    part_out[0:48, :] = part_out[0:48, :] * scale
    part_out[48:96, :] = joint_ref[...]
    pack(part_out, 6, packets)


def joint_kernel(blocks_ref, conn_ref, row_ref, scale_ref, joint_ref, line_ref, image_out, table, strain):
    table[...] = scale_ref[...] * joint_ref[...]
    apply_blocks(blocks_ref, table, 1, conn_ref, strain)
    image_out[...] = row_ref[...] * strain[...]


def own_square(ref):
    total = jnp.zeros((8, LANES), F32)
    for c in range(3):
        mine = ref[NODE_ROWS * c : NODE_ROWS * c + 8, :]
        total = total + mine * mine
    return jnp.sum(total, axis=0, keepdims=True)


def third_kernel(
    blocks_ref, conn_ref, row_ref, scale_ref, part_ref, *rest
):
    arrived, rest = by_side(rest[:4]), rest[4:]
    norm_out, joint_out, part_out, right_out, above_out, term, table, strain = rest
    unpack(part_ref, 6, arrived, jnp.add, table)
    norm_out[...] = own_square(table)
    joint_out[...] = table[48:96, :]
    scale = scale_ref[...]
    table[0:48, :] = scale * table[0:48, :]
    apply_blocks(blocks_ref, table, 1, conn_ref, strain)
    row = row_ref[...]
    strain[...] = row * (row * strain[...])
    apply_transpose(blocks_ref, strain, 1, term)
    scatter_sums(term, 3, conn_ref, part_out)
    part_out[...] = part_out[...] * scale
    for packet, side in ((right_out, 1), (above_out, 3)):
        for channel in range(3):
            packet[4 * channel : 4 * channel + 2, :] = side_rows(part_out, side, channel)
            packet[4 * channel + 2 : 4 * channel + 4, :] = side_rows(part_out, side + 4, channel)


def norm_kernel(part_ref, norm_ref, left_ref, below_ref, sums_out, line_out):
    below, above = live_sides()
    squares = jnp.zeros((2, LANES), F32)
    for channel in range(3):
        for side, arrived, live in ((0, left_ref, True), (2, below_ref, below)):
            theirs = arrived[4 * channel : 4 * channel + 4, :]
            theirs = jnp.where(live, theirs, 0.0)
            own = side_rows(part_ref, side, channel) + theirs[2:4]
            copy = side_rows(part_ref, side + 4, channel) + theirs[0:2]
            squares = squares + own * own + copy * copy
        alone = jnp.where(above, 0.0, side_rows(part_ref, 3, channel))
        squares = squares + alone * alone
    last = jnp.sum(squares, axis=0, keepdims=True)
    first = norm_ref[...]
    lane = lax.broadcasted_iota(I32, (1, LANES), 1)
    line = jnp.where(lane < 64, first + pltpu.roll(first, 64, 1), last + pltpu.roll(last, 64, 1))
    sums_out[...] = jnp.broadcast_to(line, sums_out.shape)
    line_out[...] = line


def lines_kernel(scale_ref, loads_ref, joint_ref, inverse_ref, line_ref, velocity_out, lines):
    for c in range(3):
        base = NODE_ROWS * c
        scale = scale_ref[base : base + 8, :]
        lines[8 * c : 8 * c + 8, :] = scale * (scale * loads_ref[8 * c : 8 * c + 8, :])
        lines[24 + 8 * c : 32 + 8 * c, :] = scale * joint_ref[base : base + 8, :]
    tables = [rows_of(lines, 8 * channel) for channel in range(6)]
    for channel, values in enumerate(table_picks(tables, 8, inverse_ref[...])):
        velocity_out[8 * channel : 8 * channel + 8, :] = values


def final_kernel(
    sums_ref, step_ref, velocity_ref, base_ref, joint_ref, row_ref, velocity_out, multiplier_out, *rest
):
    velocity, cones, flat, semaphores = rest
    sums = jnp.sum(sums_ref[...], axis=0, keepdims=True)
    lane = lax.broadcasted_iota(I32, (1, LANES), 1)
    before = jnp.sum(jnp.where(lane < 64, sums, 0.0), axis=1, keepdims=True)
    after = jnp.sum(jnp.where(lane < 64, 0.0, sums), axis=1, keepdims=True)
    largest = jnp.sqrt(after + epsilon) / jnp.sqrt(before + epsilon)
    step = step_ref[0] / jnp.sqrt(largest)
    square = step * step
    velocity[...] = (2.0 * step) * (square * velocity_ref[24:48, :] - velocity_ref[0:24, :])
    first = pltpu.make_async_copy(velocity, velocity_out, semaphores.at[0])
    first.start()
    cones[...] = square * (base_ref[...] - (4.0 * square) * joint_ref[...])
    project_rows(cones)
    cones[...] = row_ref[...] * cones[...]
    for r in range(STRAINS):
        for chunk in range(CHUNKS):
            flat[8 * r + chunk : 8 * r + chunk + 1, :] = cones[
                r : r + 1, chunk * LANES : (chunk + 1) * LANES
            ]
    second = pltpu.make_async_copy(flat, multiplier_out, semaphores.at[1])
    second.start()
    first.wait()
    second.wait()


def call(body, out_shapes, scratch, *arrays, smem=(), outside=(), outside_results=False, work=0, limit=24 * 1024):
    def space(i):
        return pltpu.SMEM if i in smem else pltpu.HBM if i in outside else pltpu.VMEM

    result = pltpu.HBM if outside_results else pltpu.VMEM
    return pl.pallas_call(
        body,
        out_shape=[jax.ShapeDtypeStruct(shape, kind) for shape, kind in out_shapes],
        in_specs=[pl.BlockSpec(memory_space=space(i)) for i in range(len(arrays))],
        out_specs=[pl.BlockSpec(memory_space=result) for _ in out_shapes],
        scratch_shapes=[
            entry if not isinstance(entry, tuple) else pltpu.VMEM(*entry) for entry in scratch
        ],
        cost_estimate=pl.CostEstimate(flops=work, bytes_accessed=work // 256, transcendentals=0),
        compiler_params=pltpu.CompilerParams(vmem_limit_bytes=limit * 1024),
    )(*arrays)


def swap_pairs(axis, odd):
    count = lax.axis_size(axis)
    return [(i, (((i - odd) ^ 1) + odd) % count) for i in range(count)]


PAIRS = (("sector", 1), ("band", 1), ("sector", 0), ("band", 0))


def exchange(packets):
    return [
        lax.ppermute(packet, axis, swap_pairs(axis, odd)) for packet, (axis, odd) in zip(packets, PAIRS)
    ]


def shift_up(packet, axis):
    count = lax.axis_size(axis)
    return lax.ppermute(packet, axis, [(i, (i + 1) % count) for i in range(count)])


def per_device(blocks, connectivity, send_lists, nodal_loads, step_scale):
    packet = [((12, LANES), F32)] * 4
    nodes = ((48, LANES), F32)
    rows = ((STRAINS, 1024), F32)
    items = ((3 * ITEM_ROWS, LANES), F32)
    twice = ((6 * ITEM_ROWS, LANES), F32)
    ids = ((64, LANES), I32)
    few = ((8, LANES), I32)
    *plan, row, part = call(
        start_kernel,
        [((SORTED_ROWS, LANES), I32), few, ((16, LANES), I32), few, ((16, LANES), I32)]
        + [rows, ((96, LANES), F32)],
        [
            ((1, 1, STRAINS, 24, 1024), F32),
            ids,
            twice,
            ((6 * SORTED_ROWS, LANES), F32),
            rows,
            pltpu.SemaphoreType.DMA,
        ],
        blocks,
        connectivity,
        outside=(0,),
        limit=LIMIT,
        work=12_000_000_000,
    )
    send, part, *packets = call(
        pack_kernel,
        [few, ((96, LANES), F32)] + [((24, LANES), F32)] * 4,
        [],
        part,
        send_lists,
    )
    conn, inverse = call(relabel_kernel, [ids, few], [], connectivity, send, work=BESIDE)
    row, scale, part, loads, *packets = call(
        sweep_kernel,
        [rows, nodes, nodes, ((24, LANES), F32)] + [((18, LANES), F32)] * 4,
        [items, ((3 * SORTED_ROWS, LANES), F32), rows, ((96, LANES), F32)],
        blocks,
        conn,
        row,
        part,
        nodal_loads.reshape(24, LANES),
        send,
        *plan,
        *exchange(packets),
    )
    (row,) = call(row_kernel, [rows], [rows], blocks, conn, row, scale, work=BESIDE)
    scale, image, part, *packets = call(
        target_kernel,
        [nodes, rows, nodes] + packet,
        [items, nodes, rows],
        blocks,
        conn,
        row,
        scale,
        part,
        loads,
        *exchange(packets),
    )
    base, joint = call(
        cone_kernel, [rows, nodes], [items, rows], blocks, conn, row, scale, image, work=BESIDE
    )
    part, *packets = call(
        second_kernel,
        [((96, LANES), F32)] + [((24, LANES), F32)] * 4,
        [items, nodes, rows],
        blocks,
        conn,
        row,
        scale,
        part,
        joint,
        *exchange(packets),
    )
    norm, joint, part, right, above = call(
        third_kernel,
        [((1, LANES), F32), nodes, nodes] + packet[:2],
        [items, ((96, LANES), F32), rows],
        blocks,
        conn,
        row,
        scale,
        part,
        *exchange(packets),
    )
    count = lax.axis_size("band") * lax.axis_size("sector")
    sums, line = call(
        norm_kernel,
        [((count, LANES), F32), ((1, LANES), F32)],
        [],
        part,
        norm,
        shift_up(right, "sector"),
        shift_up(above, "band"),
    )
    (image,) = call(
        joint_kernel, [rows], [nodes, rows], blocks, conn, row, scale, joint, line, work=BESIDE
    )
    (lines,) = call(
        lines_kernel,
        [((48, LANES), F32)],
        [nodes],
        scale,
        loads,
        joint,
        inverse,
        line,
        work=BESIDE,
    )
    sums = lax.all_to_all(sums, AXES, 0, 0, tiled=True)
    velocities, multipliers = call(
        final_kernel,
        [((24, LANES), F32), ((96, LANES), F32)],
        [((24, LANES), F32), rows, ((96, LANES), F32), pltpu.SemaphoreType.DMA((2,))],
        sums,
        step_scale,
        lines,
        base,
        image,
        row,
        smem=(1,),
        outside_results=True,
    )
    return velocities.reshape(1, 1, 3, 1024), multipliers.reshape(1, 1, STRAINS, 1024)


def solution(mesh):
    in_specs = (
        P("band", "sector", None, None, None),
        P("band", "sector", None, None),
        P("band", "sector", None, None),
        P("band", "sector", None, None),
        P(),
    )
    out_specs = (P("band", "sector", None, None), P("band", "sector", None, None))
    return jax.shard_map(
        per_device, mesh=mesh, in_specs=in_specs, out_specs=out_specs, check_vma=False
    )
```

```python
import functools

import jax
import jax.numpy as jnp
from jax import lax
from jax.experimental import pallas as pl
from jax.experimental.pallas import tpu as pltpu
from jax.sharding import PartitionSpec as P

LANES = 128
CHUNKS = 8
STRAINS = 12
NODE_ROWS = 16
ITEM_ROWS = 64
SIDES = 4
PARTS = 2
BESIDE = 1_000_000_000
LIMIT = 54000
AXES = ("band", "sector")
epsilon = 1e-06
F32 = jnp.float32
I32 = jnp.int32


def tile_iota(axis):
    return lax.broadcasted_iota(I32, (8, LANES), axis)


def pick(rows, index, axis):
    dims = lax.GatherDimensionNumbers(
        offset_dims=(),
        collapsed_slice_dims=(axis,),
        start_index_map=(axis,),
        operand_batching_dims=(1 - axis,),
        start_indices_batching_dims=(1 - axis,),
    )
    return lax.gather(
        rows,
        index[..., None],
        dims,
        slice_sizes=(1, 1),
        mode=lax.GatherScatterMode.PROMISE_IN_BOUNDS,
    )


def table_picks(row_getters, rows, flat):
    rows = tuple(range(rows)) if isinstance(rows, int) else rows
    lanes = flat & (LANES - 1)
    levels = rows[-1].bit_length()
    bits = [(flat & (LANES << level)) != 0 for level in range(levels)]

    def descend(row_at, level, base):
        if level < 0:
            return pick(jnp.broadcast_to(row_at(base), (8, LANES)), lanes, 1) if base in rows else None
        low = descend(row_at, level - 1, base)
        high = descend(row_at, level - 1, base + (1 << level))
        if low is None or high is None:
            return high if low is None else low
        return jnp.where(bits[level], high, low)

    return [descend(row_at, levels - 1, 0) for row_at in row_getters]


def rows_of(ref, offset):
    return lambda row: ref[offset + row : offset + row + 1, :]


def group_shift(values, distance):
    if distance >= 8:
        return pltpu.roll(values, distance // 8, 1)
    turned = pltpu.roll(values, distance, 0)
    return jnp.where(tile_iota(0) < distance, pltpu.roll(turned, 1, 1), turned)


SCAN_STEPS = tuple(1 << step for step in range(10))
RUNS = 5
NEAR_STEPS = 2
SORT_FIRST = 512
SORTED_ROWS = 8 * RUNS
LOOSE_ROWS = tuple(row for row in range(ITEM_ROWS) if row % 8 >= 3)


def sort_items(keys, size, last):
    sub, lane = tile_iota(0), tile_iota(1)
    while size <= last:
        half = size // 2
        while half >= 1:
            new = list(keys)

            def rising(register):
                if size < 8:
                    return (register & size) == 0
                if size < 64:
                    return (sub & (size // 8)) == 0
                if size < 8192:
                    return (lane & (size // 64)) == 0
                return True

            for register in range(8):
                up = rising(register)
                if half < 8:
                    other = register ^ half
                    if other < register:
                        continue
                    low = jnp.minimum(keys[register], keys[other])
                    high = jnp.maximum(keys[register], keys[other])
                    if isinstance(up, bool):
                        new[register], new[other] = (low, high) if up else (high, low)
                    else:
                        new[register] = jnp.where(up, low, high)
                        new[other] = jnp.where(up, high, low)
                    continue
                if half < 64:
                    step = half // 8
                    partner = pick(keys[register], sub ^ step, 0)
                    first = (sub & step) == 0
                else:
                    step = half // 64
                    partner = pick(keys[register], lane ^ step, 1)
                    first = (lane & step) == 0
                low = jnp.minimum(keys[register], partner)
                high = jnp.maximum(keys[register], partner)
                if isinstance(up, bool):
                    keep_low = first if up else jnp.logical_not(first)
                else:
                    keep_low = first == up
                new[register] = jnp.where(keep_low, low, high)
            keys = new
            half //= 2
        size *= 2
    return keys


def one_line(rows):
    return jnp.concatenate([rows[k : k + 1] for k in range(rows.shape[0])], axis=1)


def inverse_of(line, code, rows):
    width = line.shape[1]
    in_row = (line >> 7) == lax.broadcasted_iota(I32, (rows, width), 0)
    left = jnp.concatenate(
        [
            jnp.where(in_row, (code >> 7).astype(F32), 0.0),
            jnp.where(in_row, (code & (LANES - 1)).astype(F32), 0.0),
        ],
        axis=0,
    ).astype(jnp.bfloat16)
    in_lane = (line & (LANES - 1)) == lax.broadcasted_iota(I32, (LANES, width), 0)
    right = jnp.where(in_lane, 1.0, 0.0).astype(jnp.bfloat16)
    found = lax.dot_general(left, right, (((1,), (1,)), ((), ())), preferred_element_type=F32)
    return (found[0:rows] * 128.0 + found[rows : 2 * rows]).astype(I32)


def relabel_kernel(ids_ref, send_ref, conn_out, inverse_out):
    place = lax.broadcasted_iota(I32, (1, 8 * LANES), 1)
    inverse_out[...] = inverse_of(one_line(send_ref[...]), place, 8)
    for chunk in range(CHUNKS):
        ids = ids_ref[0, 0, :, chunk * LANES : (chunk + 1) * LANES]
        (label,) = table_picks([rows_of(inverse_out, 0)], 8, ids & 1023)
        conn_out[8 * chunk : 8 * chunk + 8, :] = jnp.where(ids < 1024, label, ids)


def to_lists(source_ref, channels, send_ref, out_ref):
    tables = [rows_of(source_ref, NODE_ROWS * channel) for channel in range(channels)]
    for channel, values in enumerate(table_picks(tables, 8, send_ref[...])):
        base = NODE_ROWS * channel
        out_ref[base : base + 8, :] = values
        out_ref[base + 8 : base + 16, :] = source_ref[base + 8 : base + 16, :]


def first_keys(ids_ref, own_out, pair_out):
    place = lax.broadcasted_iota(I32, (1, 8 * LANES), 1)
    own_out[...] = inverse_of(ids_ref[0, 0, 0:1, :], place, 8)
    pair_line = jnp.concatenate(
        [
            ids_ref[0, 0, k : k + 1, chunk * LANES : (chunk + 1) * LANES]
            for chunk in range(CHUNKS)
            for k in (1, 2)
        ],
        axis=1,
    )
    pair_out[...] = inverse_of(pair_line, lax.broadcasted_iota(I32, (1, 16 * LANES), 1), NODE_ROWS)
    sub, lane = tile_iota(0), tile_iota(1)
    keys = []
    for chunk in range(CHUNKS):
        ids = ids_ref[0, 0, :, chunk * LANES : (chunk + 1) * LANES]
        item = ids * 8192 + (chunk * 1024 + sub * LANES + lane)
        keys.append(jnp.where(sub < 3, 2048 * 8192, item))
    return keys


def make_order(keys, key_out, scan_out, end_out, keys_ref):
    sub, lane = tile_iota(0), tile_iota(1)
    keys = sort_items(keys, 2 * SORT_FIRST, 8192)
    for register in range(8):
        keys_ref[8 * register : 8 * register + 8, :] = keys[register]
    group = lane * 8 + sub
    runs = []
    for register in range(RUNS):
        place = group * RUNS + register
        row = (place & 7) * 8 + ((place >> 3) & 7)
        (moved,) = table_picks([rows_of(keys_ref, 0)], ITEM_ROWS, row * LANES + (place >> 6))
        runs.append(moved)
        key_out[8 * register : 8 * register + 8, :] = moved
    first, last = runs[0] >> 13, runs[-1] >> 13
    scan = jnp.zeros((8, LANES), I32)
    for step, distance in enumerate(SCAN_STEPS):
        same = (group >= distance) & (group_shift(last, distance) == last)
        scan = jnp.where(same, scan | (1 << step), scan)
    same = (group >= 1) & (group_shift(last, 1) == first)
    scan_out[...] = jnp.where(same, scan | (1 << len(SCAN_STEPS)), scan)
    lane_last = jnp.broadcast_to(keys_ref[63:64, :] >> 13, (8, LANES))
    for half in range(2):
        node = (half * 8 + sub) * LANES + lane
        column = jnp.zeros((8, LANES), I32)
        for step in (64, 32, 16, 8, 4, 2, 1):
            seen = pick(lane_last, column + (step - 1), 1)
            column = jnp.where(seen <= node, column + step, column)
        count = column * 64
        before = pick(lane_last, jnp.maximum(column - 1, 0), 1)
        named = (column > 0) & (before == node)
        for row in range(ITEM_ROWS):
            seen = pick(jnp.broadcast_to(keys_ref[row : row + 1, :], (8, LANES)), column, 1) >> 13
            count = count + jnp.where(seen <= node, 1, 0)
            named = named | (seen == node)
        place = jnp.maximum(count - 1, 0)
        place = jnp.where(named, place, 0)
        share = (place * 52429) >> 18
        row = (place - share * RUNS) * 8 + (share & 7)
        end = row * LANES + (share >> 3)
        end_out[8 * half : 8 * half + 8, :] = jnp.where(named, end, 8192)


def scatter_maxima(term_ref, channels, plan, sorted_ref, total_ref, out_ref):
    key_ref, scan_ref, end_ref, own_ref, pair_ref = plan
    tables = [rows_of(term_ref, ITEM_ROWS * channel) for channel in range(channels)]
    nodes = []
    for register in range(RUNS):
        key = key_ref[8 * register : 8 * register + 8, :]
        nodes.append(key >> 13)
        for channel, values in enumerate(table_picks(tables, LOOSE_ROWS, key & 8191)):
            base = SORTED_ROWS * channel + 8 * register
            sorted_ref[base : base + 8, :] = values
    scan = scan_ref[...]
    reach = (scan & ((1 << len(SCAN_STEPS)) - (1 << NEAR_STEPS))).astype(F32)
    far = jnp.max(reach) > 0.0
    follows = [(scan & (1 << step)) != 0 for step in range(len(SCAN_STEPS) + 1)]
    runs = []
    for channel in range(channels):
        base = SORTED_ROWS * channel
        mine = [sorted_ref[base : base + 8, :]]
        for register in range(1, RUNS):
            same = nodes[register] == nodes[register - 1]
            here = sorted_ref[base + 8 * register : base + 8 * register + 8, :]
            mine.append(jnp.maximum(here, jnp.where(same, mine[-1], 0.0)))
        runs.append(mine)

    def joined(totals, steps):
        for step in steps:
            shifted = [group_shift(total, SCAN_STEPS[step]) for total in totals]
            totals = [
                jnp.maximum(total, jnp.where(follows[step], other, 0.0))
                for total, other in zip(totals, shifted)
            ]
        return totals

    totals = joined([mine[-1] for mine in runs], range(NEAR_STEPS))
    for channel, total in enumerate(totals):
        total_ref[8 * channel : 8 * channel + 8, :] = total

    @pl.when(far)
    def _():
        mine = [total_ref[8 * channel : 8 * channel + 8, :] for channel in range(channels)]
        for channel, total in enumerate(joined(mine, range(NEAR_STEPS, len(SCAN_STEPS)))):
            total_ref[8 * channel : 8 * channel + 8, :] = total

    totals = [total_ref[8 * channel : 8 * channel + 8, :] for channel in range(channels)]
    carries = [jnp.where(follows[-1], group_shift(total, 1), 0.0) for total in totals]
    for channel in range(channels):
        base = SORTED_ROWS * channel
        for register in range(RUNS):
            open_run = nodes[register] == nodes[0]
            sorted_ref[base + 8 * register : base + 8 * register + 8, :] = jnp.maximum(
                runs[channel][register], jnp.where(open_run, carries[channel], 0.0)
            )
    sorted_tables = [rows_of(sorted_ref, SORTED_ROWS * channel) for channel in range(channels)]
    first_tables = [lambda row, at=at: at(8 * row) for at in tables]
    pair_tables = [lambda row, at=at: at((row >> 1) * 8 + (row & 1) + 1) for at in tables]
    own = table_picks(first_tables, 8, own_ref[...])
    for half in range(2):
        index = end_ref[8 * half : 8 * half + 8, :]
        loose = table_picks(sorted_tables, SORTED_ROWS, index & 8191)
        paired = table_picks(pair_tables, NODE_ROWS, pair_ref[8 * half : 8 * half + 8, :])
        for channel in range(channels):
            best = jnp.maximum(jnp.where(index < 8192, loose[channel], 0.0), paired[channel])
            if half == 0:
                best = jnp.maximum(best, own[channel])
            base = NODE_ROWS * channel + 8 * half
            out_ref[base : base + 8, :] = best


def node_picks(table_ref, channels, conn_ref, chunk):
    tables = [rows_of(table_ref, NODE_ROWS * channel) for channel in range(channels)]
    return table_picks(tables, NODE_ROWS, conn_ref[8 * chunk : 8 * chunk + 8, :])


def bf16_parts(values, count):
    parts = []
    for _ in range(count):
        part = values.astype(jnp.bfloat16).astype(F32)
        parts.append(part)
        values = values - part
    return parts


def scatter_sums(term_ref, channels, conn_ref, out_ref):
    width = 8 * LANES
    row_ids = lax.broadcasted_iota(I32, (NODE_ROWS, width), 0).astype(F32)
    lane_ids = lax.broadcasted_iota(I32, (LANES, width), 0).astype(F32)
    total = jnp.zeros((channels * PARTS * NODE_ROWS, LANES), F32)
    for chunk in range(CHUNKS):
        ids = conn_ref[8 * chunk : 8 * chunk + 8, :]
        in_row = one_line((ids >> 7).astype(F32)) == row_ids
        in_lane = one_line((ids & (LANES - 1)).astype(F32)) == lane_ids
        left = []
        for channel in range(channels):
            base = ITEM_ROWS * channel + 8 * chunk
            for part in bf16_parts(one_line(term_ref[base : base + 8, :]), PARTS):
                left.append(jnp.where(in_row, part, 0.0).astype(jnp.bfloat16))
        total = total + lax.dot_general(
            jnp.concatenate(left, axis=0),
            jnp.where(in_lane, 1.0, 0.0).astype(jnp.bfloat16),
            (((1,), (1,)), ((), ())),
            preferred_element_type=F32,
        )
    for channel in range(channels):
        base = PARTS * NODE_ROWS * channel
        out = total[base : base + NODE_ROWS]
        for part in range(1, PARTS):
            out = out + total[base + part * NODE_ROWS : base + (part + 1) * NODE_ROWS]
        out_ref[NODE_ROWS * channel : NODE_ROWS * (channel + 1), :] = out


def row_maxima(blocks_ref, picked, at, max_ref):
    for r in range(STRAINS):
        sized = [jnp.abs(blocks_ref[0, 0, r, 8 * c : 8 * c + 8, at]) for c in range(3)]
        for k, scales in enumerate(picked):
            whole = sized[0] * scales[0]
            for c in range(1, 3):
                whole = jnp.maximum(whole, sized[c] * scales[c])
            max_ref[STRAINS * k + r : STRAINS * k + r + 1, at] = jnp.max(whole, axis=0, keepdims=True)


def column_maxima(blocks_ref, row_ref, term_ref, first_channel):
    for chunk in range(CHUNKS):
        at = slice(chunk * LANES, (chunk + 1) * LANES)
        best = [jnp.zeros((8, LANES), F32)] * 3
        for r in range(STRAINS):
            row = 1.0 if row_ref is None else row_ref[r : r + 1, at]
            for c in range(3):
                size = jnp.abs(blocks_ref[0, 0, r, 8 * c : 8 * c + 8, at]) * row
                best[c] = jnp.maximum(best[c], size)
        for c in range(3):
            base = ITEM_ROWS * (first_channel + c) + 8 * chunk
            term_ref[base : base + 8, :] = best[c]


def apply_blocks(blocks_ref, table_ref, sets, conn_ref, strain_ref):
    for chunk in range(CHUNKS):
        values = node_picks(table_ref, 3 * sets, conn_ref, chunk)
        at = slice(chunk * LANES, (chunk + 1) * LANES)
        for r in range(STRAINS):
            parts = [blocks_ref[0, 0, r, 8 * c : 8 * c + 8, at] for c in range(3)]
            for k in range(sets):
                mine = values[3 * k : 3 * k + 3]
                total = parts[0] * mine[0] + parts[1] * mine[1] + parts[2] * mine[2]
                strain_ref[STRAINS * k + r : STRAINS * k + r + 1, at] = jnp.sum(
                    total, axis=0, keepdims=True
                )


def apply_transpose(blocks_ref, strain_ref, sets, term_ref):
    for chunk in range(CHUNKS):
        at = slice(chunk * LANES, (chunk + 1) * LANES)
        totals = [jnp.zeros((8, LANES), F32)] * (3 * sets)
        for r in range(STRAINS):
            parts = [blocks_ref[0, 0, r, 8 * c : 8 * c + 8, at] for c in range(3)]
            for k in range(sets):
                strain = strain_ref[STRAINS * k + r : STRAINS * k + r + 1, at]
                for c in range(3):
                    totals[3 * k + c] = totals[3 * k + c] + parts[c] * strain
        for channel in range(3 * sets):
            row = ITEM_ROWS * channel + 8 * chunk
            term_ref[row : row + 8, :] = totals[channel]


def even_places():
    return lax.axis_index("sector") % 2 == 0, lax.axis_index("band") % 2 == 0


def side_rows(part_ref, side, channel, length=2):
    base = NODE_ROWS * channel + 2 * side
    return part_ref[base : base + length, :]


def pack(part_ref, channels, packet_refs):
    even_sector, even_band = even_places()
    for slot, (even, low, high) in enumerate(
        ((even_sector, 1, 0), (even_band, 3, 2), (even_sector, 0, 1), (even_band, 2, 3))
    ):
        for channel in range(channels):
            for part in range(2):
                packet_refs[slot][4 * channel + 2 * part : 4 * channel + 2 * part + 2, :] = jnp.where(
                    even,
                    side_rows(part_ref, high + 4 * part, channel),
                    side_rows(part_ref, low + 4 * part, channel),
                )


def by_side(arrived_refs):
    even_sector, even_band = even_places()
    odd_cycle, odd_band, even_cycle, even_pair = [ref[...] for ref in arrived_refs]
    below, above = live_sides()
    return [
        jnp.where(even_sector, odd_cycle, even_cycle),
        jnp.where(even_sector, even_cycle, odd_cycle),
        jnp.where(below, jnp.where(even_band, odd_band, even_pair), 0.0),
        jnp.where(above, jnp.where(even_band, even_pair, odd_band), 0.0),
    ]


def live_sides():
    band = lax.axis_index("band")
    return [band > 0, band < lax.axis_size("band") - 1]


def unpack(part_ref, channels, arrived, merge, out_ref):
    for side in range(SIDES):
        for channel in range(channels):
            base = NODE_ROWS * channel + 2 * side
            theirs = arrived[side][4 * channel : 4 * channel + 4]
            out_ref[base : base + 2, :] = merge(part_ref[base : base + 2, :], theirs[2:4])
            out_ref[base + 8 : base + 10, :] = merge(part_ref[base + 8 : base + 10, :], theirs[0:2])


def rescale(scale, peak):
    peak = scale * peak
    seen = peak > 0.0
    return jnp.where(seen, scale / jnp.sqrt(jnp.where(seen, peak, 1.0)), 0.0)


def project_rows(ref):
    def every_third(start):
        return jnp.concatenate([ref[r : r + 1, :] for r in range(start, STRAINS, 3)], axis=0)

    top, first, second = [every_third(start) for start in range(3)]
    norm = jnp.sqrt(first * first + second * second)
    inside = norm <= top
    middle = norm > jnp.abs(top)
    factor = 0.5 * (1.0 + top / jnp.where(middle, norm, 1.0))
    gain = jnp.where(inside, 1.0, jnp.where(middle, factor, 0.0))
    top = jnp.where(inside, top, jnp.where(middle, factor * norm, 0.0))
    for start, values in enumerate((top, gain * first, gain * second)):
        for cone in range(4):
            ref[3 * cone + start : 3 * cone + start + 1, :] = values[cone : cone + 1, :]


def start_kernel(blocks_at, ids_ref, *rest):
    plan, (row_out, part_out), rest = rest[:5], rest[5:7], rest[7:]
    blocks_ref, keys_ref, term, items, totals, peaks, semaphore = rest
    copy = pltpu.make_async_copy(blocks_at, blocks_ref, semaphore)
    copy.start()
    keys = sort_items(first_keys(ids_ref, *plan[3:]), 2, SORT_FIRST)
    copy.wait()
    below, above = [live.astype(F32) for live in live_sides()]
    for chunk in range(CHUNKS):
        at = slice(chunk * LANES, (chunk + 1) * LANES)
        ids = ids_ref[0, 0, :, at]
        scale = jnp.where(ids < 1536, 1.0, jnp.where(ids < 1792, below, above))
        row_maxima(blocks_ref, [[scale] * 3], at, peaks)
    row_out[...] = 1.0 / jnp.sqrt(peaks[...])
    column_maxima(blocks_ref, None, term, 0)
    column_maxima(blocks_ref, row_out, term, 3)
    make_order(keys, *plan[:3], keys_ref)
    scatter_maxima(term, 6, plan, items, totals, part_out)


def pack_kernel(part_ref, lists_ref, send_out, part_out, *packets):
    for half in range(8):
        start = (half % 2) * LANES
        send_out[half : half + 1, :] = lists_ref[0, 0, half // 2 : half // 2 + 1, start : start + LANES]
    to_lists(part_ref, 6, send_out, part_out)
    pack(part_out, 6, packets)


def sweep_kernel(
    blocks_ref, conn_ref, row_ref, part_ref, loads_ref, send_ref, *rest
):
    plan, rest = rest[:5], rest[5:]
    arrived, rest = by_side(rest[:4]), rest[4:]
    row_out, scale_out, part_out, loads_out, rest = rest[0], rest[1], rest[2], rest[3], rest[4:]
    packets, (term, items, totals, peaks, merged) = rest[:4], rest[4:]
    unpack(part_ref, 6, arrived, jnp.maximum, merged)
    row = lax.broadcasted_iota(I32, (NODE_ROWS, LANES), 0)
    below, above = [live.astype(F32) for live in live_sides()]
    start = jnp.where(row < 12, 1.0, jnp.where(row < 14, below, above))
    for c in range(3):
        first = rescale(start, merged[NODE_ROWS * c : NODE_ROWS * (c + 1), :])
        later = NODE_ROWS * (c + 3)
        second = rescale(first, merged[later : later + NODE_ROWS, :])
        merged[NODE_ROWS * c : NODE_ROWS * (c + 1), :] = first
        scale_out[NODE_ROWS * c : NODE_ROWS * (c + 1), :] = second
    for chunk in range(CHUNKS):
        at = slice(chunk * LANES, (chunk + 1) * LANES)
        row_maxima(blocks_ref, [node_picks(merged, 3, conn_ref, chunk)], at, peaks)
    row_out[...] = row_ref[...] / jnp.sqrt(row_ref[...] * peaks[...])
    column_maxima(blocks_ref, row_out, term, 0)
    scatter_maxima(term, 3, plan, items, totals, merged)
    to_lists(merged, 3, send_ref, part_out)
    pack(part_out, 3, packets)
    tables = [rows_of(loads_ref, 8 * c) for c in range(3)]
    for c, values in enumerate(table_picks(tables, 8, send_ref[...])):
        loads_out[8 * c : 8 * c + 8, :] = values
    even_sector, even_band = even_places()
    for slot, (even, low, high) in enumerate(
        ((even_sector, 1, 0), (even_band, 3, 2), (even_sector, 0, 1), (even_band, 2, 3))
    ):
        for c in range(3):
            packets[slot][12 + 2 * c : 14 + 2 * c, :] = jnp.where(
                even,
                loads_out[8 * c + 2 * high : 8 * c + 2 * high + 2, :],
                loads_out[8 * c + 2 * low : 8 * c + 2 * low + 2, :],
            )


def row_kernel(blocks_ref, conn_ref, row_ref, scale_ref, row_out, peaks):
    for chunk in range(CHUNKS):
        at = slice(chunk * LANES, (chunk + 1) * LANES)
        row_maxima(blocks_ref, [node_picks(scale_ref, 3, conn_ref, chunk)], at, peaks)
    row_out[...] = row_ref[...] / jnp.sqrt(row_ref[...] * peaks[...])


def target_kernel(blocks_ref, conn_ref, row_ref, scale_ref, part_ref, loads_ref, *rest):
    arrived, rest = by_side(rest[:4]), rest[4:]
    scale_out, image_out, part_out, rest = rest[0], rest[1], rest[2], rest[3:]
    packets, (term, table, strain) = rest[:4], rest[4:]
    unpack(part_ref, 3, arrived, jnp.maximum, table)
    scale = rescale(scale_ref[...], table[...])
    scale_out[...] = scale
    for c in range(3):
        table[NODE_ROWS * c : NODE_ROWS * c + 8, :] = loads_ref[8 * c : 8 * c + 8, :]
        for side in range(SIDES):
            base = NODE_ROWS * c + 8 + 2 * side
            table[base : base + 2, :] = arrived[side][12 + 2 * c : 14 + 2 * c]
    table[...] = scale * (scale * table[...])
    apply_blocks(blocks_ref, table, 1, conn_ref, strain)
    row = row_ref[...]
    image = row * strain[...]
    image_out[...] = image
    strain[...] = row * image
    apply_transpose(blocks_ref, strain, 1, term)
    scatter_sums(term, 3, conn_ref, part_out)
    part_out[...] = part_out[...] * scale
    pack(part_out, 3, packets)


def cone_kernel(blocks_ref, conn_ref, row_ref, scale_ref, image_ref, base_out, part_out, term, strain):
    strain[...] = image_ref[...]
    project_rows(strain)
    base_out[...] = 3.0 * image_ref[...] + 2.0 * strain[...]
    strain[...] = row_ref[...] * strain[...]
    apply_transpose(blocks_ref, strain, 1, term)
    scatter_sums(term, 3, conn_ref, part_out)
    part_out[...] = part_out[...] * scale_ref[...]


def second_kernel(blocks_ref, conn_ref, row_ref, scale_ref, part_ref, joint_ref, *rest):
    arrived, rest = by_side(rest[:4]), rest[4:]
    part_out, packets, (term, table, strain) = rest[0], rest[1:5], rest[5:]
    unpack(part_ref, 3, arrived, jnp.add, table)
    scale = scale_ref[...]
    table[...] = scale * table[...]
    apply_blocks(blocks_ref, table, 1, conn_ref, strain)
    row = row_ref[...]
    strain[...] = row * (row * strain[...])
    apply_transpose(blocks_ref, strain, 1, term)
    scatter_sums(term, 3, conn_ref, part_out)
    part_out[0:48, :] = part_out[0:48, :] * scale
    part_out[48:96, :] = joint_ref[...]
    pack(part_out, 6, packets)


def joint_kernel(blocks_ref, conn_ref, row_ref, scale_ref, joint_ref, line_ref, image_out, table, strain):
    table[...] = scale_ref[...] * joint_ref[...]
    apply_blocks(blocks_ref, table, 1, conn_ref, strain)
    image_out[...] = row_ref[...] * strain[...]


def own_square(ref):
    total = jnp.zeros((8, LANES), F32)
    for c in range(3):
        mine = ref[NODE_ROWS * c : NODE_ROWS * c + 8, :]
        total = total + mine * mine
    return jnp.sum(total, axis=0, keepdims=True)


def third_kernel(
    blocks_ref, conn_ref, row_ref, scale_ref, part_ref, *rest
):
    arrived, rest = by_side(rest[:4]), rest[4:]
    norm_out, joint_out, part_out, right_out, above_out, term, table, strain = rest
    unpack(part_ref, 6, arrived, jnp.add, table)
    norm_out[...] = own_square(table)
    joint_out[...] = table[48:96, :]
    scale = scale_ref[...]
    table[0:48, :] = scale * table[0:48, :]
    apply_blocks(blocks_ref, table, 1, conn_ref, strain)
    row = row_ref[...]
    strain[...] = row * (row * strain[...])
    apply_transpose(blocks_ref, strain, 1, term)
    scatter_sums(term, 3, conn_ref, part_out)
    part_out[...] = part_out[...] * scale
    for packet, side in ((right_out, 1), (above_out, 3)):
        for channel in range(3):
            packet[4 * channel : 4 * channel + 2, :] = side_rows(part_out, side, channel)
            packet[4 * channel + 2 : 4 * channel + 4, :] = side_rows(part_out, side + 4, channel)


def norm_kernel(part_ref, norm_ref, left_ref, below_ref, sums_out, line_out):
    below, above = live_sides()
    squares = jnp.zeros((2, LANES), F32)
    for channel in range(3):
        for side, arrived, live in ((0, left_ref, True), (2, below_ref, below)):
            theirs = arrived[4 * channel : 4 * channel + 4, :]
            theirs = jnp.where(live, theirs, 0.0)
            own = side_rows(part_ref, side, channel) + theirs[2:4]
            copy = side_rows(part_ref, side + 4, channel) + theirs[0:2]
            squares = squares + own * own + copy * copy
        alone = jnp.where(above, 0.0, side_rows(part_ref, 3, channel))
        squares = squares + alone * alone
    last = jnp.sum(squares, axis=0, keepdims=True)
    first = norm_ref[...]
    lane = lax.broadcasted_iota(I32, (1, LANES), 1)
    line = jnp.where(lane < 64, first + pltpu.roll(first, 64, 1), last + pltpu.roll(last, 64, 1))
    sums_out[...] = jnp.broadcast_to(line, sums_out.shape)
    line_out[...] = line


def lines_kernel(scale_ref, loads_ref, joint_ref, inverse_ref, line_ref, velocity_out, lines):
    for c in range(3):
        base = NODE_ROWS * c
        scale = scale_ref[base : base + 8, :]
        lines[8 * c : 8 * c + 8, :] = scale * (scale * loads_ref[8 * c : 8 * c + 8, :])
        lines[24 + 8 * c : 32 + 8 * c, :] = scale * joint_ref[base : base + 8, :]
    tables = [rows_of(lines, 8 * channel) for channel in range(6)]
    for channel, values in enumerate(table_picks(tables, 8, inverse_ref[...])):
        velocity_out[8 * channel : 8 * channel + 8, :] = values


def final_kernel(
    sums_ref, step_ref, velocity_ref, base_ref, joint_ref, row_ref, velocity_out, multiplier_out, *rest
):
    velocity, cones, flat, semaphores = rest
    sums = jnp.sum(sums_ref[...], axis=0, keepdims=True)
    lane = lax.broadcasted_iota(I32, (1, LANES), 1)
    before = jnp.sum(jnp.where(lane < 64, sums, 0.0), axis=1, keepdims=True)
    after = jnp.sum(jnp.where(lane < 64, 0.0, sums), axis=1, keepdims=True)
    largest = jnp.sqrt(after + epsilon) / jnp.sqrt(before + epsilon)
    step = step_ref[0] / jnp.sqrt(largest)
    square = step * step
    velocity[...] = (2.0 * step) * (square * velocity_ref[24:48, :] - velocity_ref[0:24, :])
    first = pltpu.make_async_copy(velocity, velocity_out, semaphores.at[0])
    first.start()
    cones[...] = square * (base_ref[...] - (4.0 * square) * joint_ref[...])
    project_rows(cones)
    cones[...] = row_ref[...] * cones[...]
    for r in range(STRAINS):
        for chunk in range(CHUNKS):
            flat[8 * r + chunk : 8 * r + chunk + 1, :] = cones[
                r : r + 1, chunk * LANES : (chunk + 1) * LANES
            ]
    second = pltpu.make_async_copy(flat, multiplier_out, semaphores.at[1])
    second.start()
    first.wait()
    second.wait()


def call(body, out_shapes, scratch, *arrays, smem=(), outside=(), outside_results=False, work=0, limit=24 * 1024):
    def space(i):
        return pltpu.SMEM if i in smem else pltpu.HBM if i in outside else pltpu.VMEM

    result = pltpu.HBM if outside_results else pltpu.VMEM
    return pl.pallas_call(
        body,
        out_shape=[jax.ShapeDtypeStruct(shape, kind) for shape, kind in out_shapes],
        in_specs=[pl.BlockSpec(memory_space=space(i)) for i in range(len(arrays))],
        out_specs=[pl.BlockSpec(memory_space=result) for _ in out_shapes],
        scratch_shapes=[
            entry if not isinstance(entry, tuple) else pltpu.VMEM(*entry) for entry in scratch
        ],
        cost_estimate=pl.CostEstimate(flops=work, bytes_accessed=work // 256, transcendentals=0),
        compiler_params=pltpu.CompilerParams(vmem_limit_bytes=limit * 1024),
    )(*arrays)


def swap_pairs(axis, odd):
    count = lax.axis_size(axis)
    return [(i, (((i - odd) ^ 1) + odd) % count) for i in range(count)]


PAIRS = (("sector", 1), ("band", 1), ("sector", 0), ("band", 0))


def exchange(packets):
    return [
        lax.ppermute(packet, axis, swap_pairs(axis, odd)) for packet, (axis, odd) in zip(packets, PAIRS)
    ]


def shift_up(packet, axis):
    count = lax.axis_size(axis)
    return lax.ppermute(packet, axis, [(i, (i + 1) % count) for i in range(count)])


def per_device(blocks, connectivity, send_lists, nodal_loads, step_scale):
    packet = [((12, LANES), F32)] * 4
    nodes = ((48, LANES), F32)
    rows = ((STRAINS, 1024), F32)
    items = ((3 * ITEM_ROWS, LANES), F32)
    twice = ((6 * ITEM_ROWS, LANES), F32)
    ids = ((64, LANES), I32)
    few = ((8, LANES), I32)
    *plan, row, part = call(
        start_kernel,
        [((SORTED_ROWS, LANES), I32), few, ((16, LANES), I32), few, ((16, LANES), I32)]
        + [rows, ((96, LANES), F32)],
        [
            ((1, 1, STRAINS, 24, 1024), F32),
            ids,
            twice,
            ((6 * SORTED_ROWS, LANES), F32),
            nodes,
            rows,
            pltpu.SemaphoreType.DMA,
        ],
        blocks,
        connectivity,
        outside=(0,),
        limit=LIMIT,
        work=12_000_000_000,
    )
    send, part, *packets = call(
        pack_kernel,
        [few, ((96, LANES), F32)] + [((24, LANES), F32)] * 4,
        [],
        part,
        send_lists,
    )
    conn, inverse = call(relabel_kernel, [ids, few], [], connectivity, send, work=BESIDE)
    row, scale, part, loads, *packets = call(
        sweep_kernel,
        [rows, nodes, nodes, ((24, LANES), F32)] + [((18, LANES), F32)] * 4,
        [items, ((3 * SORTED_ROWS, LANES), F32), ((24, LANES), F32), rows, ((96, LANES), F32)],
        blocks,
        conn,
        row,
        part,
        nodal_loads.reshape(24, LANES),
        send,
        *plan,
        *exchange(packets),
    )
    (row,) = call(row_kernel, [rows], [rows], blocks, conn, row, scale, work=BESIDE)
    scale, image, part, *packets = call(
        target_kernel,
        [nodes, rows, nodes] + packet,
        [items, nodes, rows],
        blocks,
        conn,
        row,
        scale,
        part,
        loads,
        *exchange(packets),
    )
    base, joint = call(
        cone_kernel, [rows, nodes], [items, rows], blocks, conn, row, scale, image, work=BESIDE
    )
    part, *packets = call(
        second_kernel,
        [((96, LANES), F32)] + [((24, LANES), F32)] * 4,
        [items, nodes, rows],
        blocks,
        conn,
        row,
        scale,
        part,
        joint,
        *exchange(packets),
    )
    norm, joint, part, right, above = call(
        third_kernel,
        [((1, LANES), F32), nodes, nodes] + packet[:2],
        [items, ((96, LANES), F32), rows],
        blocks,
        conn,
        row,
        scale,
        part,
        *exchange(packets),
    )
    count = lax.axis_size("band") * lax.axis_size("sector")
    sums, line = call(
        norm_kernel,
        [((count, LANES), F32), ((1, LANES), F32)],
        [],
        part,
        norm,
        shift_up(right, "sector"),
        shift_up(above, "band"),
    )
    (image,) = call(
        joint_kernel, [rows], [nodes, rows], blocks, conn, row, scale, joint, line, work=BESIDE
    )
    (lines,) = call(
        lines_kernel,
        [((48, LANES), F32)],
        [nodes],
        scale,
        loads,
        joint,
        inverse,
        line,
        work=BESIDE,
    )
    sums = lax.all_to_all(sums, AXES, 0, 0, tiled=True)
    velocities, multipliers = call(
        final_kernel,
        [((24, LANES), F32), ((96, LANES), F32)],
        [((24, LANES), F32), rows, ((96, LANES), F32), pltpu.SemaphoreType.DMA((2,))],
        sums,
        step_scale,
        lines,
        base,
        image,
        row,
        smem=(1,),
        outside_results=True,
    )
    return velocities.reshape(1, 1, 3, 1024), multipliers.reshape(1, 1, STRAINS, 1024)


def solution(mesh):
    in_specs = (
        P("band", "sector", None, None, None),
        P("band", "sector", None, None),
        P("band", "sector", None, None),
        P("band", "sector", None, None),
        P(),
    )
    out_specs = (P("band", "sector", None, None), P("band", "sector", None, None))
    return jax.shard_map(
        per_device, mesh=mesh, in_specs=in_specs, out_specs=out_specs, check_vma=False
    )
```

```python
import functools

import jax
import jax.numpy as jnp
from jax import lax
from jax.experimental import pallas as pl
from jax.experimental.pallas import tpu as pltpu
from jax.sharding import PartitionSpec as P

LANES = 128
CHUNKS = 8
STRAINS = 12
NODE_ROWS = 16
ITEM_ROWS = 64
SIDES = 4
PARTS = 2
BESIDE = 1_000_000_000
LIMIT = 54000
AXES = ("band", "sector")
epsilon = 1e-06
F32 = jnp.float32
I32 = jnp.int32


def tile_iota(axis):
    return lax.broadcasted_iota(I32, (8, LANES), axis)


def pick(rows, index, axis):
    dims = lax.GatherDimensionNumbers(
        offset_dims=(),
        collapsed_slice_dims=(axis,),
        start_index_map=(axis,),
        operand_batching_dims=(1 - axis,),
        start_indices_batching_dims=(1 - axis,),
    )
    return lax.gather(
        rows,
        index[..., None],
        dims,
        slice_sizes=(1, 1),
        mode=lax.GatherScatterMode.PROMISE_IN_BOUNDS,
    )


def table_picks(row_getters, rows, flat):
    rows = tuple(range(rows)) if isinstance(rows, int) else rows
    lanes = flat & (LANES - 1)
    levels = rows[-1].bit_length()
    bits = [(flat & (LANES << level)) != 0 for level in range(levels)]

    def descend(row_at, level, base):
        if level < 0:
            return pick(jnp.broadcast_to(row_at(base), (8, LANES)), lanes, 1) if base in rows else None
        low = descend(row_at, level - 1, base)
        high = descend(row_at, level - 1, base + (1 << level))
        if low is None or high is None:
            return high if low is None else low
        return jnp.where(bits[level], high, low)

    return [descend(row_at, levels - 1, 0) for row_at in row_getters]


def rows_of(ref, offset):
    return lambda row: ref[offset + row : offset + row + 1, :]


def group_shift(values, distance):
    if distance >= 8:
        return pltpu.roll(values, distance // 8, 1)
    turned = pltpu.roll(values, distance, 0)
    return jnp.where(tile_iota(0) < distance, pltpu.roll(turned, 1, 1), turned)


SCAN_STEPS = tuple(1 << step for step in range(10))
RUNS = 5
NEAR_STEPS = 2
SORT_FIRST = 512
SORTED_ROWS = 8 * RUNS
LOOSE_ROWS = tuple(row for row in range(ITEM_ROWS) if row % 8 >= 3)


def sort_items(keys, size, last):
    sub, lane = tile_iota(0), tile_iota(1)
    while size <= last:
        half = size // 2
        while half >= 1:
            new = list(keys)

            def rising(register):
                if size < 8:
                    return (register & size) == 0
                if size < 64:
                    return (sub & (size // 8)) == 0
                if size < 8192:
                    return (lane & (size // 64)) == 0
                return True

            for register in range(8):
                up = rising(register)
                if half < 8:
                    other = register ^ half
                    if other < register:
                        continue
                    low = jnp.minimum(keys[register], keys[other])
                    high = jnp.maximum(keys[register], keys[other])
                    if isinstance(up, bool):
                        new[register], new[other] = (low, high) if up else (high, low)
                    else:
                        new[register] = jnp.where(up, low, high)
                        new[other] = jnp.where(up, high, low)
                    continue
                if half < 64:
                    step = half // 8
                    partner = pick(keys[register], sub ^ step, 0)
                    first = (sub & step) == 0
                else:
                    step = half // 64
                    partner = pick(keys[register], lane ^ step, 1)
                    first = (lane & step) == 0
                low = jnp.minimum(keys[register], partner)
                high = jnp.maximum(keys[register], partner)
                if isinstance(up, bool):
                    keep_low = first if up else jnp.logical_not(first)
                else:
                    keep_low = first == up
                new[register] = jnp.where(keep_low, low, high)
            keys = new
            half //= 2
        size *= 2
    return keys


def one_line(rows):
    return jnp.concatenate([rows[k : k + 1] for k in range(rows.shape[0])], axis=1)


def inverse_of(line, code, rows):
    width = line.shape[1]
    in_row = (line >> 7) == lax.broadcasted_iota(I32, (rows, width), 0)
    left = jnp.concatenate(
        [
            jnp.where(in_row, (code >> 7).astype(F32), 0.0),
            jnp.where(in_row, (code & (LANES - 1)).astype(F32), 0.0),
        ],
        axis=0,
    ).astype(jnp.bfloat16)
    in_lane = (line & (LANES - 1)) == lax.broadcasted_iota(I32, (LANES, width), 0)
    right = jnp.where(in_lane, 1.0, 0.0).astype(jnp.bfloat16)
    found = lax.dot_general(left, right, (((1,), (1,)), ((), ())), preferred_element_type=F32)
    return (found[0:rows] * 128.0 + found[rows : 2 * rows]).astype(I32)


def relabel_kernel(ids_ref, send_ref, conn_out, inverse_out):
    place = lax.broadcasted_iota(I32, (1, 8 * LANES), 1)
    inverse_out[...] = inverse_of(one_line(send_ref[...]), place, 8)
    for chunk in range(CHUNKS):
        ids = ids_ref[0, 0, :, chunk * LANES : (chunk + 1) * LANES]
        (label,) = table_picks([rows_of(inverse_out, 0)], 8, ids & 1023)
        conn_out[8 * chunk : 8 * chunk + 8, :] = jnp.where(ids < 1024, label, ids)


def to_lists(source_ref, channels, send_ref, out_ref):
    tables = [rows_of(source_ref, NODE_ROWS * channel) for channel in range(channels)]
    for channel, values in enumerate(table_picks(tables, 8, send_ref[...])):
        base = NODE_ROWS * channel
        out_ref[base : base + 8, :] = values
        out_ref[base + 8 : base + 16, :] = source_ref[base + 8 : base + 16, :]


def first_keys(ids_ref, own_out, pair_out):
    place = lax.broadcasted_iota(I32, (1, 8 * LANES), 1)
    own_out[...] = inverse_of(ids_ref[0, 0, 0:1, :], place, 8)
    pair_line = jnp.concatenate(
        [
            ids_ref[0, 0, k : k + 1, chunk * LANES : (chunk + 1) * LANES]
            for chunk in range(CHUNKS)
            for k in (1, 2)
        ],
        axis=1,
    )
    pair_out[...] = inverse_of(pair_line, lax.broadcasted_iota(I32, (1, 16 * LANES), 1), NODE_ROWS)
    sub, lane = tile_iota(0), tile_iota(1)
    keys = []
    for chunk in range(CHUNKS):
        ids = ids_ref[0, 0, :, chunk * LANES : (chunk + 1) * LANES]
        item = ids * 8192 + (chunk * 1024 + sub * LANES + lane)
        keys.append(jnp.where(sub < 3, 2048 * 8192, item))
    return keys


def make_order(keys, key_out, scan_out, end_out, keys_ref):
    sub, lane = tile_iota(0), tile_iota(1)
    keys = sort_items(keys, 2 * SORT_FIRST, 8192)
    for register in range(8):
        keys_ref[8 * register : 8 * register + 8, :] = keys[register]
    group = lane * 8 + sub
    runs = []
    for register in range(RUNS):
        place = group * RUNS + register
        row = (place & 7) * 8 + ((place >> 3) & 7)
        (moved,) = table_picks([rows_of(keys_ref, 0)], ITEM_ROWS, row * LANES + (place >> 6))
        runs.append(moved)
        key_out[8 * register : 8 * register + 8, :] = moved
    first, last = runs[0] >> 13, runs[-1] >> 13
    scan = jnp.zeros((8, LANES), I32)
    for step, distance in enumerate(SCAN_STEPS):
        same = (group >= distance) & (group_shift(last, distance) == last)
        scan = jnp.where(same, scan | (1 << step), scan)
    same = (group >= 1) & (group_shift(last, 1) == first)
    scan_out[...] = jnp.where(same, scan | (1 << len(SCAN_STEPS)), scan)
    lane_last = jnp.broadcast_to(keys_ref[63:64, :] >> 13, (8, LANES))
    for half in range(2):
        node = (half * 8 + sub) * LANES + lane
        column = jnp.zeros((8, LANES), I32)
        for step in (64, 32, 16, 8, 4, 2, 1):
            seen = pick(lane_last, column + (step - 1), 1)
            column = jnp.where(seen <= node, column + step, column)
        count = column * 64
        before = pick(lane_last, jnp.maximum(column - 1, 0), 1)
        named = (column > 0) & (before == node)
        for row in range(ITEM_ROWS):
            seen = pick(jnp.broadcast_to(keys_ref[row : row + 1, :], (8, LANES)), column, 1) >> 13
            count = count + jnp.where(seen <= node, 1, 0)
            named = named | (seen == node)
        place = jnp.maximum(count - 1, 0)
        place = jnp.where(named, place, 0)
        share = (place * 52429) >> 18
        row = (place - share * RUNS) * 8 + (share & 7)
        end = row * LANES + (share >> 3)
        end_out[8 * half : 8 * half + 8, :] = jnp.where(named, end, 8192)


def scatter_maxima(term_ref, channels, plan, sorted_ref, total_ref, out_ref):
    key_ref, scan_ref, end_ref, own_ref, pair_ref = plan
    tables = [rows_of(term_ref, ITEM_ROWS * channel) for channel in range(channels)]
    nodes = []
    for register in range(RUNS):
        key = key_ref[8 * register : 8 * register + 8, :]
        nodes.append(key >> 13)
        for channel, values in enumerate(table_picks(tables, LOOSE_ROWS, key & 8191)):
            base = SORTED_ROWS * channel + 8 * register
            sorted_ref[base : base + 8, :] = values
    scan = scan_ref[...]
    reach = (scan & ((1 << len(SCAN_STEPS)) - (1 << NEAR_STEPS))).astype(F32)
    far = jnp.max(reach) > 0.0
    follows = [(scan & (1 << step)) != 0 for step in range(len(SCAN_STEPS) + 1)]
    runs = []
    for channel in range(channels):
        base = SORTED_ROWS * channel
        mine = [sorted_ref[base : base + 8, :]]
        for register in range(1, RUNS):
            same = nodes[register] == nodes[register - 1]
            here = sorted_ref[base + 8 * register : base + 8 * register + 8, :]
            mine.append(jnp.maximum(here, jnp.where(same, mine[-1], 0.0)))
        runs.append(mine)

    def joined(totals, steps):
        for step in steps:
            shifted = [group_shift(total, SCAN_STEPS[step]) for total in totals]
            totals = [
                jnp.maximum(total, jnp.where(follows[step], other, 0.0))
                for total, other in zip(totals, shifted)
            ]
        return totals

    totals = joined([mine[-1] for mine in runs], range(NEAR_STEPS))
    for channel, total in enumerate(totals):
        total_ref[8 * channel : 8 * channel + 8, :] = total

    @pl.when(far)
    def _():
        mine = [total_ref[8 * channel : 8 * channel + 8, :] for channel in range(channels)]
        for channel, total in enumerate(joined(mine, range(NEAR_STEPS, len(SCAN_STEPS)))):
            total_ref[8 * channel : 8 * channel + 8, :] = total

    totals = [total_ref[8 * channel : 8 * channel + 8, :] for channel in range(channels)]
    carries = [jnp.where(follows[-1], group_shift(total, 1), 0.0) for total in totals]
    for channel in range(channels):
        base = SORTED_ROWS * channel
        for register in range(RUNS):
            open_run = nodes[register] == nodes[0]
            sorted_ref[base + 8 * register : base + 8 * register + 8, :] = jnp.maximum(
                runs[channel][register], jnp.where(open_run, carries[channel], 0.0)
            )
    sorted_tables = [rows_of(sorted_ref, SORTED_ROWS * channel) for channel in range(channels)]
    first_tables = [lambda row, at=at: at(8 * row) for at in tables]
    pair_tables = [lambda row, at=at: at((row >> 1) * 8 + (row & 1) + 1) for at in tables]
    own = table_picks(first_tables, 8, own_ref[...])
    for half in range(2):
        index = end_ref[8 * half : 8 * half + 8, :]
        loose = table_picks(sorted_tables, SORTED_ROWS, index & 8191)
        paired = table_picks(pair_tables, NODE_ROWS, pair_ref[8 * half : 8 * half + 8, :])
        for channel in range(channels):
            best = jnp.maximum(jnp.where(index < 8192, loose[channel], 0.0), paired[channel])
            if half == 0:
                best = jnp.maximum(best, own[channel])
            base = NODE_ROWS * channel + 8 * half
            out_ref[base : base + 8, :] = best


def node_picks(table_ref, channels, conn_ref, chunk):
    tables = [rows_of(table_ref, NODE_ROWS * channel) for channel in range(channels)]
    return table_picks(tables, NODE_ROWS, conn_ref[8 * chunk : 8 * chunk + 8, :])


def bf16_parts(values, count):
    parts = []
    for _ in range(count):
        part = values.astype(jnp.bfloat16).astype(F32)
        parts.append(part)
        values = values - part
    return parts


def scatter_sums(term_ref, channels, conn_ref, out_ref):
    width = 8 * LANES
    row_ids = lax.broadcasted_iota(I32, (NODE_ROWS, width), 0).astype(F32)
    lane_ids = lax.broadcasted_iota(I32, (LANES, width), 0).astype(F32)
    total = jnp.zeros((channels * PARTS * NODE_ROWS, LANES), F32)
    for chunk in range(CHUNKS):
        ids = conn_ref[8 * chunk : 8 * chunk + 8, :]
        in_row = one_line((ids >> 7).astype(F32)) == row_ids
        in_lane = one_line((ids & (LANES - 1)).astype(F32)) == lane_ids
        left = []
        for channel in range(channels):
            base = ITEM_ROWS * channel + 8 * chunk
            for part in bf16_parts(one_line(term_ref[base : base + 8, :]), PARTS):
                left.append(jnp.where(in_row, part, 0.0).astype(jnp.bfloat16))
        total = total + lax.dot_general(
            jnp.concatenate(left, axis=0),
            jnp.where(in_lane, 1.0, 0.0).astype(jnp.bfloat16),
            (((1,), (1,)), ((), ())),
            preferred_element_type=F32,
        )
    for channel in range(channels):
        base = PARTS * NODE_ROWS * channel
        out = total[base : base + NODE_ROWS]
        for part in range(1, PARTS):
            out = out + total[base + part * NODE_ROWS : base + (part + 1) * NODE_ROWS]
        out_ref[NODE_ROWS * channel : NODE_ROWS * (channel + 1), :] = out


def fold_rows(rows, merge, ref, first, at):
    sub = tile_iota(0)

    def fold(low, high, step):
        here = (sub & step) == 0
        return merge(
            jnp.where(here, low, high), pick(jnp.where(here, high, low), sub ^ step, 0)
        )

    pairs = [fold(rows[r], rows[r + 4], 4) for r in (0, 2, 1, 3)]
    fours = [fold(pairs[0], pairs[1], 2), fold(pairs[2], pairs[3], 2)]
    ref[first : first + 8, at] = fold(fours[0], fours[1], 1)
    rest = fold(fold(rows[8], rows[9], 4), fold(rows[10], rows[11], 4), 2)
    rest = merge(rest, pick(rest, sub ^ 1, 0))
    for r, place in enumerate((0, 4, 2, 6)):
        ref[first + 8 + r : first + 9 + r, at] = rest[place : place + 1, :]


def row_maxima(blocks_ref, scales, at, max_ref):
    whole = []
    for r in range(STRAINS):
        sized = [jnp.abs(blocks_ref[0, 0, r, 8 * c : 8 * c + 8, at]) * scales[c] for c in range(3)]
        whole.append(jnp.maximum(jnp.maximum(sized[0], sized[1]), sized[2]))
    fold_rows(whole, jnp.maximum, max_ref, 0, at)


def column_maxima(blocks_ref, row_ref, term_ref, first_channel):
    for chunk in range(CHUNKS):
        at = slice(chunk * LANES, (chunk + 1) * LANES)
        best = [jnp.zeros((8, LANES), F32)] * 3
        for r in range(STRAINS):
            row = 1.0 if row_ref is None else row_ref[r : r + 1, at]
            for c in range(3):
                size = jnp.abs(blocks_ref[0, 0, r, 8 * c : 8 * c + 8, at]) * row
                best[c] = jnp.maximum(best[c], size)
        for c in range(3):
            base = ITEM_ROWS * (first_channel + c) + 8 * chunk
            term_ref[base : base + 8, :] = best[c]


def apply_blocks(blocks_ref, table_ref, conn_ref, strain_ref):
    for chunk in range(CHUNKS):
        values = node_picks(table_ref, 3, conn_ref, chunk)
        at = slice(chunk * LANES, (chunk + 1) * LANES)
        totals = []
        for r in range(STRAINS):
            parts = [blocks_ref[0, 0, r, 8 * c : 8 * c + 8, at] * values[c] for c in range(3)]
            totals.append(parts[0] + parts[1] + parts[2])
        fold_rows(totals, jnp.add, strain_ref, 0, at)


def apply_transpose(blocks_ref, strain_ref, sets, term_ref):
    for chunk in range(CHUNKS):
        at = slice(chunk * LANES, (chunk + 1) * LANES)
        totals = [jnp.zeros((8, LANES), F32)] * (3 * sets)
        for r in range(STRAINS):
            parts = [blocks_ref[0, 0, r, 8 * c : 8 * c + 8, at] for c in range(3)]
            for k in range(sets):
                strain = strain_ref[STRAINS * k + r : STRAINS * k + r + 1, at]
                for c in range(3):
                    totals[3 * k + c] = totals[3 * k + c] + parts[c] * strain
        for channel in range(3 * sets):
            row = ITEM_ROWS * channel + 8 * chunk
            term_ref[row : row + 8, :] = totals[channel]


def even_places():
    return lax.axis_index("sector") % 2 == 0, lax.axis_index("band") % 2 == 0


def side_rows(part_ref, side, channel, length=2):
    base = NODE_ROWS * channel + 2 * side
    return part_ref[base : base + length, :]


def pack(part_ref, channels, packet_refs):
    even_sector, even_band = even_places()
    for slot, (even, low, high) in enumerate(
        ((even_sector, 1, 0), (even_band, 3, 2), (even_sector, 0, 1), (even_band, 2, 3))
    ):
        for channel in range(channels):
            for part in range(2):
                packet_refs[slot][4 * channel + 2 * part : 4 * channel + 2 * part + 2, :] = jnp.where(
                    even,
                    side_rows(part_ref, high + 4 * part, channel),
                    side_rows(part_ref, low + 4 * part, channel),
                )


def by_side(arrived_refs):
    even_sector, even_band = even_places()
    odd_cycle, odd_band, even_cycle, even_pair = [ref[...] for ref in arrived_refs]
    below, above = live_sides()
    return [
        jnp.where(even_sector, odd_cycle, even_cycle),
        jnp.where(even_sector, even_cycle, odd_cycle),
        jnp.where(below, jnp.where(even_band, odd_band, even_pair), 0.0),
        jnp.where(above, jnp.where(even_band, even_pair, odd_band), 0.0),
    ]


def live_sides():
    band = lax.axis_index("band")
    return [band > 0, band < lax.axis_size("band") - 1]


def unpack(part_ref, channels, arrived, merge, out_ref):
    for side in range(SIDES):
        for channel in range(channels):
            base = NODE_ROWS * channel + 2 * side
            theirs = arrived[side][4 * channel : 4 * channel + 4]
            out_ref[base : base + 2, :] = merge(part_ref[base : base + 2, :], theirs[2:4])
            out_ref[base + 8 : base + 10, :] = merge(part_ref[base + 8 : base + 10, :], theirs[0:2])


def rescale(scale, peak):
    peak = scale * peak
    seen = peak > 0.0
    return jnp.where(seen, scale / jnp.sqrt(jnp.where(seen, peak, 1.0)), 0.0)


def project_rows(ref):
    def every_third(start):
        return jnp.concatenate([ref[r : r + 1, :] for r in range(start, STRAINS, 3)], axis=0)

    top, first, second = [every_third(start) for start in range(3)]
    norm = jnp.sqrt(first * first + second * second)
    inside = norm <= top
    middle = norm > jnp.abs(top)
    factor = 0.5 * (1.0 + top / jnp.where(middle, norm, 1.0))
    gain = jnp.where(inside, 1.0, jnp.where(middle, factor, 0.0))
    top = jnp.where(inside, top, jnp.where(middle, factor * norm, 0.0))
    for start, values in enumerate((top, gain * first, gain * second)):
        for cone in range(4):
            ref[3 * cone + start : 3 * cone + start + 1, :] = values[cone : cone + 1, :]


def start_kernel(blocks_at, ids_ref, *rest):
    plan, (row_out, part_out), rest = rest[:5], rest[5:7], rest[7:]
    blocks_ref, keys_ref, term, items, totals, peaks, semaphore = rest
    copy = pltpu.make_async_copy(blocks_at, blocks_ref, semaphore)
    copy.start()
    keys = sort_items(first_keys(ids_ref, *plan[3:]), 2, SORT_FIRST)
    copy.wait()
    below, above = [live.astype(F32) for live in live_sides()]
    for chunk in range(CHUNKS):
        at = slice(chunk * LANES, (chunk + 1) * LANES)
        ids = ids_ref[0, 0, :, at]
        scale = jnp.where(ids < 1536, 1.0, jnp.where(ids < 1792, below, above))
        row_maxima(blocks_ref, [scale] * 3, at, peaks)
    row_out[...] = 1.0 / jnp.sqrt(peaks[...])
    column_maxima(blocks_ref, None, term, 0)
    column_maxima(blocks_ref, row_out, term, 3)
    make_order(keys, *plan[:3], keys_ref)
    scatter_maxima(term, 6, plan, items, totals, part_out)


def pack_kernel(part_ref, lists_ref, send_out, part_out, *packets):
    for half in range(8):
        start = (half % 2) * LANES
        send_out[half : half + 1, :] = lists_ref[0, 0, half // 2 : half // 2 + 1, start : start + LANES]
    to_lists(part_ref, 6, send_out, part_out)
    pack(part_out, 6, packets)


def sweep_kernel(
    blocks_ref, conn_ref, row_ref, part_ref, loads_ref, send_ref, *rest
):
    plan, rest = rest[:5], rest[5:]
    arrived, rest = by_side(rest[:4]), rest[4:]
    row_out, scale_out, part_out, loads_out, rest = rest[0], rest[1], rest[2], rest[3], rest[4:]
    packets, (term, items, totals, peaks, merged) = rest[:4], rest[4:]
    unpack(part_ref, 6, arrived, jnp.maximum, merged)
    row = lax.broadcasted_iota(I32, (NODE_ROWS, LANES), 0)
    below, above = [live.astype(F32) for live in live_sides()]
    start = jnp.where(row < 12, 1.0, jnp.where(row < 14, below, above))
    for c in range(3):
        first = rescale(start, merged[NODE_ROWS * c : NODE_ROWS * (c + 1), :])
        later = NODE_ROWS * (c + 3)
        second = rescale(first, merged[later : later + NODE_ROWS, :])
        merged[NODE_ROWS * c : NODE_ROWS * (c + 1), :] = first
        scale_out[NODE_ROWS * c : NODE_ROWS * (c + 1), :] = second
    for chunk in range(CHUNKS):
        at = slice(chunk * LANES, (chunk + 1) * LANES)
        row_maxima(blocks_ref, node_picks(merged, 3, conn_ref, chunk), at, peaks)
    row_out[...] = row_ref[...] / jnp.sqrt(row_ref[...] * peaks[...])
    column_maxima(blocks_ref, row_out, term, 0)
    scatter_maxima(term, 3, plan, items, totals, merged)
    to_lists(merged, 3, send_ref, part_out)
    pack(part_out, 3, packets)
    tables = [rows_of(loads_ref, 8 * c) for c in range(3)]
    for c, values in enumerate(table_picks(tables, 8, send_ref[...])):
        loads_out[8 * c : 8 * c + 8, :] = values
    even_sector, even_band = even_places()
    for slot, (even, low, high) in enumerate(
        ((even_sector, 1, 0), (even_band, 3, 2), (even_sector, 0, 1), (even_band, 2, 3))
    ):
        for c in range(3):
            packets[slot][12 + 2 * c : 14 + 2 * c, :] = jnp.where(
                even,
                loads_out[8 * c + 2 * high : 8 * c + 2 * high + 2, :],
                loads_out[8 * c + 2 * low : 8 * c + 2 * low + 2, :],
            )


def row_kernel(blocks_ref, conn_ref, row_ref, scale_ref, row_out, peaks):
    for chunk in range(CHUNKS):
        at = slice(chunk * LANES, (chunk + 1) * LANES)
        row_maxima(blocks_ref, node_picks(scale_ref, 3, conn_ref, chunk), at, peaks)
    row_out[...] = row_ref[...] / jnp.sqrt(row_ref[...] * peaks[...])


def target_kernel(blocks_ref, conn_ref, row_ref, scale_ref, part_ref, loads_ref, *rest):
    arrived, rest = by_side(rest[:4]), rest[4:]
    scale_out, image_out, part_out, rest = rest[0], rest[1], rest[2], rest[3:]
    packets, (term, table, strain) = rest[:4], rest[4:]
    unpack(part_ref, 3, arrived, jnp.maximum, table)
    scale = rescale(scale_ref[...], table[...])
    scale_out[...] = scale
    for c in range(3):
        table[NODE_ROWS * c : NODE_ROWS * c + 8, :] = loads_ref[8 * c : 8 * c + 8, :]
        for side in range(SIDES):
            base = NODE_ROWS * c + 8 + 2 * side
            table[base : base + 2, :] = arrived[side][12 + 2 * c : 14 + 2 * c]
    table[...] = scale * (scale * table[...])
    apply_blocks(blocks_ref, table, conn_ref, strain)
    row = row_ref[...]
    image = row * strain[...]
    image_out[...] = image
    strain[...] = row * image
    apply_transpose(blocks_ref, strain, 1, term)
    scatter_sums(term, 3, conn_ref, part_out)
    part_out[...] = part_out[...] * scale
    pack(part_out, 3, packets)


def cone_kernel(blocks_ref, conn_ref, row_ref, scale_ref, image_ref, base_out, part_out, term, strain):
    strain[...] = image_ref[...]
    project_rows(strain)
    base_out[...] = 3.0 * image_ref[...] + 2.0 * strain[...]
    strain[...] = row_ref[...] * strain[...]
    apply_transpose(blocks_ref, strain, 1, term)
    scatter_sums(term, 3, conn_ref, part_out)
    part_out[...] = part_out[...] * scale_ref[...]


def second_kernel(blocks_ref, conn_ref, row_ref, scale_ref, part_ref, joint_ref, *rest):
    arrived, rest = by_side(rest[:4]), rest[4:]
    part_out, packets, (term, table, strain) = rest[0], rest[1:5], rest[5:]
    unpack(part_ref, 3, arrived, jnp.add, table)
    scale = scale_ref[...]
    table[...] = scale * table[...]
    apply_blocks(blocks_ref, table, conn_ref, strain)
    row = row_ref[...]
    strain[...] = row * (row * strain[...])
    apply_transpose(blocks_ref, strain, 1, term)
    scatter_sums(term, 3, conn_ref, part_out)
    part_out[0:48, :] = part_out[0:48, :] * scale
    part_out[48:96, :] = joint_ref[...]
    pack(part_out, 6, packets)


def joint_kernel(blocks_ref, conn_ref, row_ref, scale_ref, joint_ref, line_ref, image_out, table, strain):
    table[...] = scale_ref[...] * joint_ref[...]
    apply_blocks(blocks_ref, table, conn_ref, strain)
    image_out[...] = row_ref[...] * strain[...]


def own_square(ref):
    total = jnp.zeros((8, LANES), F32)
    for c in range(3):
        mine = ref[NODE_ROWS * c : NODE_ROWS * c + 8, :]
        total = total + mine * mine
    return jnp.sum(total, axis=0, keepdims=True)


def third_kernel(
    blocks_ref, conn_ref, row_ref, scale_ref, part_ref, *rest
):
    arrived, rest = by_side(rest[:4]), rest[4:]
    norm_out, joint_out, part_out, right_out, above_out, term, table, strain = rest
    unpack(part_ref, 6, arrived, jnp.add, table)
    norm_out[...] = own_square(table)
    joint_out[...] = table[48:96, :]
    scale = scale_ref[...]
    table[0:48, :] = scale * table[0:48, :]
    apply_blocks(blocks_ref, table, conn_ref, strain)
    row = row_ref[...]
    strain[...] = row * (row * strain[...])
    apply_transpose(blocks_ref, strain, 1, term)
    scatter_sums(term, 3, conn_ref, part_out)
    part_out[...] = part_out[...] * scale
    for packet, side in ((right_out, 1), (above_out, 3)):
        for channel in range(3):
            packet[4 * channel : 4 * channel + 2, :] = side_rows(part_out, side, channel)
            packet[4 * channel + 2 : 4 * channel + 4, :] = side_rows(part_out, side + 4, channel)


def norm_kernel(part_ref, norm_ref, left_ref, below_ref, sums_out, line_out):
    below, above = live_sides()
    squares = jnp.zeros((2, LANES), F32)
    for channel in range(3):
        for side, arrived, live in ((0, left_ref, True), (2, below_ref, below)):
            theirs = arrived[4 * channel : 4 * channel + 4, :]
            theirs = jnp.where(live, theirs, 0.0)
            own = side_rows(part_ref, side, channel) + theirs[2:4]
            copy = side_rows(part_ref, side + 4, channel) + theirs[0:2]
            squares = squares + own * own + copy * copy
        alone = jnp.where(above, 0.0, side_rows(part_ref, 3, channel))
        squares = squares + alone * alone
    last = jnp.sum(squares, axis=0, keepdims=True)
    first = norm_ref[...]
    lane = lax.broadcasted_iota(I32, (1, LANES), 1)
    line = jnp.where(lane < 64, first + pltpu.roll(first, 64, 1), last + pltpu.roll(last, 64, 1))
    sums_out[...] = jnp.broadcast_to(line, sums_out.shape)
    line_out[...] = line


def lines_kernel(scale_ref, loads_ref, joint_ref, inverse_ref, line_ref, velocity_out, lines):
    for c in range(3):
        base = NODE_ROWS * c
        scale = scale_ref[base : base + 8, :]
        lines[8 * c : 8 * c + 8, :] = scale * (scale * loads_ref[8 * c : 8 * c + 8, :])
        lines[24 + 8 * c : 32 + 8 * c, :] = scale * joint_ref[base : base + 8, :]
    tables = [rows_of(lines, 8 * channel) for channel in range(6)]
    for channel, values in enumerate(table_picks(tables, 8, inverse_ref[...])):
        velocity_out[8 * channel : 8 * channel + 8, :] = values


def final_kernel(
    sums_ref, step_ref, velocity_ref, base_ref, joint_ref, row_ref, velocity_out, multiplier_out, *rest
):
    velocity, cones, flat, semaphores = rest
    sums = jnp.sum(sums_ref[...], axis=0, keepdims=True)
    lane = lax.broadcasted_iota(I32, (1, LANES), 1)
    before = jnp.sum(jnp.where(lane < 64, sums, 0.0), axis=1, keepdims=True)
    after = jnp.sum(jnp.where(lane < 64, 0.0, sums), axis=1, keepdims=True)
    largest = jnp.sqrt(after + epsilon) / jnp.sqrt(before + epsilon)
    step = step_ref[0] / jnp.sqrt(largest)
    square = step * step
    velocity[...] = (2.0 * step) * (square * velocity_ref[24:48, :] - velocity_ref[0:24, :])
    first = pltpu.make_async_copy(velocity, velocity_out, semaphores.at[0])
    first.start()
    cones[...] = square * (base_ref[...] - (4.0 * square) * joint_ref[...])
    project_rows(cones)
    cones[...] = row_ref[...] * cones[...]
    for r in range(STRAINS):
        for chunk in range(CHUNKS):
            flat[8 * r + chunk : 8 * r + chunk + 1, :] = cones[
                r : r + 1, chunk * LANES : (chunk + 1) * LANES
            ]
    second = pltpu.make_async_copy(flat, multiplier_out, semaphores.at[1])
    second.start()
    first.wait()
    second.wait()


def call(body, out_shapes, scratch, *arrays, smem=(), outside=(), outside_results=False, work=0, limit=24 * 1024):
    def space(i):
        return pltpu.SMEM if i in smem else pltpu.HBM if i in outside else pltpu.VMEM

    result = pltpu.HBM if outside_results else pltpu.VMEM
    return pl.pallas_call(
        body,
        out_shape=[jax.ShapeDtypeStruct(shape, kind) for shape, kind in out_shapes],
        in_specs=[pl.BlockSpec(memory_space=space(i)) for i in range(len(arrays))],
        out_specs=[pl.BlockSpec(memory_space=result) for _ in out_shapes],
        scratch_shapes=[
            entry if not isinstance(entry, tuple) else pltpu.VMEM(*entry) for entry in scratch
        ],
        cost_estimate=pl.CostEstimate(flops=work, bytes_accessed=work // 256, transcendentals=0),
        compiler_params=pltpu.CompilerParams(vmem_limit_bytes=limit * 1024),
    )(*arrays)


def swap_pairs(axis, odd):
    count = lax.axis_size(axis)
    return [(i, (((i - odd) ^ 1) + odd) % count) for i in range(count)]


PAIRS = (("sector", 1), ("band", 1), ("sector", 0), ("band", 0))


def exchange(packets):
    return [
        lax.ppermute(packet, axis, swap_pairs(axis, odd)) for packet, (axis, odd) in zip(packets, PAIRS)
    ]


def shift_up(packet, axis):
    count = lax.axis_size(axis)
    return lax.ppermute(packet, axis, [(i, (i + 1) % count) for i in range(count)])


def per_device(blocks, connectivity, send_lists, nodal_loads, step_scale):
    packet = [((12, LANES), F32)] * 4
    nodes = ((48, LANES), F32)
    rows = ((STRAINS, 1024), F32)
    items = ((3 * ITEM_ROWS, LANES), F32)
    twice = ((6 * ITEM_ROWS, LANES), F32)
    ids = ((64, LANES), I32)
    few = ((8, LANES), I32)
    *plan, row, part = call(
        start_kernel,
        [((SORTED_ROWS, LANES), I32), few, ((16, LANES), I32), few, ((16, LANES), I32)]
        + [rows, ((96, LANES), F32)],
        [
            ((1, 1, STRAINS, 24, 1024), F32),
            ids,
            twice,
            ((6 * SORTED_ROWS, LANES), F32),
            nodes,
            rows,
            pltpu.SemaphoreType.DMA,
        ],
        blocks,
        connectivity,
        outside=(0,),
        limit=LIMIT,
        work=12_000_000_000,
    )
    send, part, *packets = call(
        pack_kernel,
        [few, ((96, LANES), F32)] + [((24, LANES), F32)] * 4,
        [],
        part,
        send_lists,
    )
    conn, inverse = call(relabel_kernel, [ids, few], [], connectivity, send, work=BESIDE)
    row, scale, part, loads, *packets = call(
        sweep_kernel,
        [rows, nodes, nodes, ((24, LANES), F32)] + [((18, LANES), F32)] * 4,
        [items, ((3 * SORTED_ROWS, LANES), F32), ((24, LANES), F32), rows, ((96, LANES), F32)],
        blocks,
        conn,
        row,
        part,
        nodal_loads.reshape(24, LANES),
        send,
        *plan,
        *exchange(packets),
    )
    (row,) = call(row_kernel, [rows], [rows], blocks, conn, row, scale, work=BESIDE)
    scale, image, part, *packets = call(
        target_kernel,
        [nodes, rows, nodes] + packet,
        [items, nodes, rows],
        blocks,
        conn,
        row,
        scale,
        part,
        loads,
        *exchange(packets),
    )
    base, joint = call(
        cone_kernel, [rows, nodes], [items, rows], blocks, conn, row, scale, image, work=BESIDE
    )
    part, *packets = call(
        second_kernel,
        [((96, LANES), F32)] + [((24, LANES), F32)] * 4,
        [items, nodes, rows],
        blocks,
        conn,
        row,
        scale,
        part,
        joint,
        *exchange(packets),
    )
    norm, joint, part, right, above = call(
        third_kernel,
        [((1, LANES), F32), nodes, nodes] + packet[:2],
        [items, ((96, LANES), F32), rows],
        blocks,
        conn,
        row,
        scale,
        part,
        *exchange(packets),
    )
    count = lax.axis_size("band") * lax.axis_size("sector")
    sums, line = call(
        norm_kernel,
        [((count, LANES), F32), ((1, LANES), F32)],
        [],
        part,
        norm,
        shift_up(right, "sector"),
        shift_up(above, "band"),
    )
    (image,) = call(
        joint_kernel, [rows], [nodes, rows], blocks, conn, row, scale, joint, line, work=BESIDE
    )
    (lines,) = call(
        lines_kernel,
        [((48, LANES), F32)],
        [nodes],
        scale,
        loads,
        joint,
        inverse,
        line,
        work=BESIDE,
    )
    sums = lax.all_to_all(sums, AXES, 0, 0, tiled=True)
    velocities, multipliers = call(
        final_kernel,
        [((24, LANES), F32), ((96, LANES), F32)],
        [((24, LANES), F32), rows, ((96, LANES), F32), pltpu.SemaphoreType.DMA((2,))],
        sums,
        step_scale,
        lines,
        base,
        image,
        row,
        smem=(1,),
        outside_results=True,
    )
    return velocities.reshape(1, 1, 3, 1024), multipliers.reshape(1, 1, STRAINS, 1024)


def solution(mesh):
    in_specs = (
        P("band", "sector", None, None, None),
        P("band", "sector", None, None),
        P("band", "sector", None, None),
        P("band", "sector", None, None),
        P(),
    )
    out_specs = (P("band", "sector", None, None), P("band", "sector", None, None))
    return jax.shard_map(
        per_device, mesh=mesh, in_specs=in_specs, out_specs=out_specs, check_vma=False
    )
```
